32 devices in a mesh: blk: 4 (over z), rows: 8 (over y, x, core).
Axes of the slice: x: 2, y: 2, z: 4, core: 2. Of those that a mesh axis runs over, the one named last changes fastest.
Arguments:
- embeddings: bfloat16 [16384, 768], P(('blk', 'rows')), as said below
- centroids: bfloat16 [8192, 768], P('blk'), as said below
- log_mix: float32 [8192], P('blk'), may hold values from -1.5 to 3.7
Outputs:
- new_centroids: float32 [8192, 768], P('blk')
- new_weights: float32 [8192], P('blk')
The draws below stay inside these ranges and needn't reach their ends.
Inputs may be any that keep to these rules, and one draw needn't show every extreme that they name: `embeddings`: real vectors of no fixed length. `centroids`: real vectors of no fixed length.
All inputs are finite; a program needn't handle non-finite values.
Results may differ from the reference program's by a relative error of at most 0.0024.
Values may be sent and summed in bfloat16 or wider, within the bound.
No kernel may reach another device: no remote copies, remote signals or barrier semaphores. Data moves between devices by JAX's collectives and lax.ppermute only.
A program may use at most 64 MiB of HBM per device.

```python
import math
import jax
import jax.numpy as jnp
from jax import lax

D = 768
K = 8192
NROWS = 16384


def anchor_table(key):
    return jax.random.normal(jax.random.fold_in(key, 101), (K, D), jnp.float32)


def draw_centroids(key, part):
    anchors = anchor_table(key)
    noise_key = jax.random.fold_in(key, 102)
    noise = 0.5 * jax.random.normal(noise_key, (K, D), jnp.float32)
    return (anchors + noise).astype(jnp.bfloat16)


def draw_embeddings(key, part):
    anchors = anchor_table(key)
    assigned = jax.random.randint(jax.random.fold_in(key, 103), (NROWS,), 0, K)
    chosen = anchors[assigned]
    noise_key = jax.random.fold_in(key, 104)
    spread = jnp.exp(jax.random.uniform(jax.random.fold_in(key, 108), (NROWS, 1), jnp.float32, math.log(1.2), math.log(4.0)))
    noise = spread * jax.random.normal(noise_key, (NROWS, D), jnp.float32)
    scales = jnp.exp(jax.random.uniform(jax.random.fold_in(key, 105), (NROWS, 1), jnp.float32, 0.0, math.log(10.0)))
    return ((chosen + noise) * scales).astype(jnp.bfloat16)


def draw_log_mix(key, part):
    position = jnp.arange(K, dtype=jnp.float32) / K
    jitter = jax.random.uniform(jax.random.fold_in(key, 106), (K,), jnp.float32, -1.0, 1.0)
    rising = math.log(9.0) * position
    return jitter + rising


def setup_inputs(seed: int = 0) -> dict:
    key_of = jax.random.split(jax.random.key(seed), 4)
    return {
        "embeddings": draw_embeddings(jax.random.fold_in(key_of[3], 71), 0),
        "centroids": draw_centroids(jax.random.fold_in(key_of[3], 71), 0),
        "log_mix": draw_log_mix(jax.random.fold_in(key_of[3], 71), 0),
    }


concentration = 32.0

def to_unit(values):
    values = values.astype(jnp.float32)
    return (values * lax.rsqrt(lax.optimization_barrier(jnp.sum(values * values, axis=-1, keepdims=True)) + 1e-06)).astype(jnp.bfloat16)

def reference(embeddings, centroids, log_mix):
    centroid_units = to_unit(centroids)
    block_rows = math.gcd(NROWS, 1024)
    grouped = embeddings.reshape(NROWS // block_rows, block_rows, D)

    def accumulate(carried, row_block):
        row_units = to_unit(row_block)
        cosines = jnp.dot(row_units, centroid_units.T, preferred_element_type=jnp.float32)
        scores = jnp.exp(log_mix[None, :] + concentration * (cosines - 1.0))
        totals = lax.optimization_barrier(jnp.sum(scores, axis=1, keepdims=True))
        resp = (scores / totals).astype(jnp.bfloat16)
        weighted = carried[0] + jnp.dot(resp.T, row_units, preferred_element_type=jnp.float32)
        masses = carried[1] + lax.optimization_barrier(jnp.sum(resp.astype(jnp.float32), axis=0))
        return ((weighted, masses), None)
    start_state = (jnp.zeros((K, D), jnp.float32), jnp.zeros((K,), jnp.float32))
    (weighted, masses), _ = lax.scan(accumulate, start_state, grouped)
    new_centroids = weighted * lax.rsqrt(lax.optimization_barrier(jnp.sum(weighted * weighted, axis=1, keepdims=True)) + 1e-06)
    new_weights = masses * (K / NROWS)
    return (new_centroids, new_weights)
```

```python
import functools
import math

import jax
import jax.numpy as jnp
from jax import lax
from jax.experimental import pallas as pl
from jax.experimental.pallas import tpu as pltpu
from jax.sharding import PartitionSpec as P

concentration = 32.0
LOG2E = math.log2(math.e)
LANES = 128
VMEM_LIMIT = 48 * 1024 * 1024


def to_unit(values):
    values = values.astype(jnp.float32)
    return (values * lax.rsqrt(jnp.sum(values * values, axis=-1, keepdims=True) + 1e-06)).astype(
        jnp.bfloat16
    )


def arrival_plan(n):
    plan = []
    for place in range(n):
        order = [("own", 0, place)]
        for step in range(1, n):
            if place - step >= 0:
                order.append(("up", step, place - step))
            if place + step < n:
                order.append(("down", step, place + step))
        plan.append(order)
    return plan


def score_kernel(n_sources, picks, *refs):
    sources = refs[:n_sources]
    units_in, log_mix = refs[n_sources], refs[n_sources + 1]
    scores, rows_out, totals, raw, units, sem = refs[-6:]

    @pl.when(pl.program_id(0) == 0)
    def _():
        for number, source in enumerate(sources):

            @pl.when(picks[0] == number)
            def _():
                pltpu.make_async_copy(source, raw, sem).start()

        pltpu.make_async_copy(sources[0], raw, sem).wait()
        values = raw[...].astype(jnp.float32)
        square = jnp.sum(values * values, axis=-1, keepdims=True)
        unit = (values * lax.rsqrt(square + 1e-06)).astype(jnp.bfloat16)
        units[...] = unit
        rows_out[...] = unit
        totals[...] = jnp.zeros_like(totals)

    cosines = lax.dot_general(
        units_in[...], units[...], (((1,), (1,)), ((), ())), preferred_element_type=jnp.float32
    )
    offset = log_mix[...]
    repeats = cosines.shape[1] // offset.shape[1]
    if repeats > 1:
        offset = jnp.concatenate([offset] * repeats, axis=1)
    value = jnp.exp2(cosines * (concentration * LOG2E) + offset)
    scores[...] = value
    totals[0] += jnp.sum(value, axis=0, keepdims=True)


def score_block(picks, sources, centroid_units, offsets, carried, slot, n_slots):
    part, depth = sources[0].shape
    count = centroid_units.shape[0]
    tile = math.gcd(count, 512)
    shapes = (
        jax.ShapeDtypeStruct((count, n_slots * part), jnp.float32),
        jax.ShapeDtypeStruct((n_slots * part, depth), jnp.bfloat16),
        jax.ShapeDtypeStruct((n_slots, 1, part), jnp.float32),
    )
    n_sources = len(sources)
    aliases = {}
    extra = ()
    if carried is not None:
        extra = carried
        aliases = {1 + n_sources + 2 + i: i for i in range(3)}
    anywhere = pl.BlockSpec(memory_space=pl.ANY)
    return pl.pallas_call(
        functools.partial(score_kernel, n_sources),
        grid_spec=pltpu.PrefetchScalarGridSpec(
            num_scalar_prefetch=1,
            grid=(count // tile,),
            in_specs=[anywhere] * n_sources
            + [
                pl.BlockSpec((tile, depth), lambda t, s: (t, 0)),
                pl.BlockSpec((tile, offsets.shape[1]), lambda t, s: (t, 0)),
            ]
            + [anywhere] * len(extra),
            out_specs=[
                pl.BlockSpec((tile, part), lambda t, s: (t, slot)),
                pl.BlockSpec((part, depth), lambda t, s: (slot, 0)),
                pl.BlockSpec((1, 1, part), lambda t, s: (s[1], 0, 0)),
            ],
            scratch_shapes=[
                pltpu.VMEM((part, depth), jnp.bfloat16),
                pltpu.VMEM((part, depth), jnp.bfloat16),
                pltpu.SemaphoreType.DMA,
            ],
        ),
        out_shape=shapes,
        input_output_aliases=aliases,
        compiler_params=pltpu.CompilerParams(vmem_limit_bytes=VMEM_LIMIT),
        cost_estimate=pl.CostEstimate(
            flops=2 * count * part * depth,
            bytes_accessed=count * part * 4 + count * depth * 2,
            transcendentals=count * part,
        ),
        name="scores",
    )(picks, *sources, centroid_units, offsets, *extra)


def sum_kernel(n_totals, n_slots, has_other, order, *refs):
    totals = refs[:n_totals]
    scores, rows = refs[n_totals], refs[n_totals + 1]
    other = refs[n_totals + 2] if has_other else None
    out, masses, inverse = refs[-3:]
    steps = pl.num_programs(0)
    part = scores.shape[1] // n_slots

    @pl.when(pl.program_id(0) == 0)
    def _():
        for slot in range(n_slots):
            place = order[steps + slot]
            total = totals[0][place]
            for more in totals[1:]:
                total = total + more[place]
            inverse[:, slot * part : (slot + 1) * part] = 1.0 / total

    resp = (scores[...] * inverse[...]).astype(jnp.bfloat16)
    weighted = lax.dot_general(
        resp, rows[...], (((1,), (0,)), ((), ())), preferred_element_type=jnp.float32
    )
    wide = resp.astype(jnp.float32)
    mass = wide[:, :LANES]
    for start in range(LANES, wide.shape[1], LANES):
        mass = mass + wide[:, start : start + LANES]
    masses[0] = jnp.sum(mass.T, axis=0, keepdims=True)
    if has_other:
        weighted = weighted + other[0].astype(jnp.float32)
    out[0] = weighted.astype(out.dtype)


def sum_blocks(blocks, slots_of, totals, scores, rows, masses, other, dtype, n_blocks):
    steps = blocks.shape[0]
    count, width = scores.shape
    depth = rows.shape[1]
    size = count // n_blocks
    n_slots = totals[0].shape[0]
    whole = lambda array: pl.BlockSpec(array.shape, lambda t, s: (0,) * array.ndim)
    inputs = [*totals, scores, rows]
    specs = [whole(array) for array in totals] + [
        pl.BlockSpec((size, width), lambda t, s: (s[t], 0)),
        whole(rows),
    ]
    if other is not None:
        inputs.append(other)
        specs.append(pl.BlockSpec((1, size, depth), lambda t, s: (t, 0, 0)))
    aliases = {}
    if masses is not None:
        aliases = {1 + len(inputs): 1}
        inputs.append(masses)
        specs.append(pl.BlockSpec(memory_space=pl.ANY))
    return pl.pallas_call(
        functools.partial(sum_kernel, len(totals), n_slots, other is not None),
        grid_spec=pltpu.PrefetchScalarGridSpec(
            num_scalar_prefetch=1,
            grid=(steps,),
            in_specs=specs,
            out_specs=[
                pl.BlockSpec((1, size, depth), lambda t, s: (t, 0, 0)),
                pl.BlockSpec((1, 1, size), lambda t, s: (s[t], 0, 0)),
            ],
            scratch_shapes=[pltpu.VMEM((1, width), jnp.float32)],
        ),
        out_shape=(
            jax.ShapeDtypeStruct((steps, size, depth), dtype),
            jax.ShapeDtypeStruct((n_blocks, 1, size), jnp.float32),
        ),
        input_output_aliases=aliases,
        compiler_params=pltpu.CompilerParams(vmem_limit_bytes=VMEM_LIMIT),
        cost_estimate=pl.CostEstimate(
            flops=2 * steps * size * width * depth,
            bytes_accessed=steps * size * (width * 4 + depth * 4) + width * depth * 2,
            transcendentals=0,
        ),
        name="sums",
    )(jnp.concatenate([blocks, slots_of]), *inputs)


def local(embeddings, centroids, log_mix):
    n_places = lax.axis_size("blk")
    n_rows = lax.axis_size("rows")
    place = lax.axis_index("blk")
    me = lax.axis_index("rows")
    held, depth = embeddings.shape
    n_parts = 2 if held % (2 * LANES) == 0 else 1
    part = held // n_parts

    moving = {}
    for number in range(n_parts):
        own = embeddings[number * part : (number + 1) * part]
        moving["own", 0, number] = own
        moving["up", 0, number] = own
        moving["down", 0, number] = own
    for step in range(1, n_places):
        for number in range(n_parts):
            moving["up", step, number] = lax.ppermute(
                moving["up", step - 1, number],
                "blk",
                [(i, i + 1) for i in range(step - 1, n_places - 1)],
            )
            moving["down", step, number] = lax.ppermute(
                moving["down", step - 1, number],
                "blk",
                [(i + 1, i) for i in range(0, n_places - step)],
            )

    centroid_units = to_unit(centroids)
    offsets = jnp.broadcast_to(
        ((log_mix - concentration) * LOG2E)[:, None], (log_mix.shape[0], LANES)
    )

    plan = arrival_plan(n_places)
    n_slots = n_places * n_parts
    carried = None
    blocks_of = []
    for turn in range(n_places):
        kinds = sorted({plan[i][turn][:2] for i in range(n_places)})
        source = jnp.array([kinds.index(plan[i][turn][:2]) for i in range(n_places)], jnp.int32)[place]
        block = jnp.array([plan[i][turn][2] for i in range(n_places)], jnp.int32)[place]
        for number in range(n_parts):
            total_slot = block * n_parts + number
            blocks_of.append(total_slot)
            carried = score_block(
                jnp.stack([source, total_slot]),
                [moving[kind + (number,)] for kind in kinds],
                centroid_units,
                offsets,
                carried,
                turn * n_parts + number,
                n_slots,
            )
    scores, rows, totals = carried
    all_totals = [totals] + [
        lax.ppermute(totals, "blk", [(i, (i + turn) % n_places) for i in range(n_places)])
        for turn in range(1, n_places)
    ]
    slots_of = jnp.stack(blocks_of).astype(jnp.int32)

    def exchange(array, distance):
        return lax.ppermute(array, "rows", [(i, i ^ distance) for i in range(n_rows)])

    def blocks(distances):
        return jnp.stack([me ^ distance for distance in distances]).astype(jnp.int32)

    far = list(range(2, n_rows, 2))
    args = (slots_of, all_totals, scores, rows)
    given, masses = sum_blocks(
        blocks([d ^ 1 for d in far]), *args, None, None, jnp.bfloat16, n_rows
    )
    taken = exchange(given, 1)
    near, masses = sum_blocks(blocks([1]), *args, masses, None, jnp.bfloat16, n_rows)
    near = exchange(near, 1)
    mine, masses = sum_blocks(blocks([0]), *args, masses, None, jnp.float32, n_rows)
    sent, masses = sum_blocks(blocks(far), *args, masses, taken, jnp.bfloat16, n_rows)
    summed = mine[0] + near[0].astype(jnp.float32)
    arrived = [exchange(sent[number], distance) for number, distance in enumerate(far)]
    for array in arrived:
        summed = summed + array.astype(jnp.float32)

    distance = 1
    while distance < n_rows:
        masses = masses + exchange(masses, distance)
        distance *= 2

    unit = summed * lax.rsqrt(jnp.sum(summed * summed, axis=1, keepdims=True) + 1e-06)
    unit = unit.astype(jnp.float16)
    size = unit.shape[0]
    pieces = {0: unit}
    for distance in far:
        pieces[distance] = exchange(unit, distance)
    for distance in [0] + far:
        pieces[distance ^ 1] = exchange(pieces[distance], 1)
    result = jnp.zeros((size * n_rows, depth), jnp.float32)
    for distance, piece in pieces.items():
        result = lax.dynamic_update_slice(
            result, piece.astype(jnp.float32), ((me ^ distance) * size, 0)
        )
    count = size * n_rows * n_places
    factor = count / (held * n_rows * n_places)
    return (result, masses.reshape(-1) * factor)


def solution(mesh):
    return jax.shard_map(
        local,
        mesh=mesh,
        in_specs=(P(("blk", "rows"), None), P("blk", None), P("blk")),
        out_specs=(P("blk", None), P("blk")),
        check_vma=False,
    )
```

```python
import functools
import math

import jax
import jax.numpy as jnp
from jax import lax
from jax.experimental import pallas as pl
from jax.experimental.pallas import tpu as pltpu
from jax.sharding import PartitionSpec as P

concentration = 32.0
LOG2E = math.log2(math.e)
LANES = 128
CORES = 2
VMEM_LIMIT = 48 * 1024 * 1024


def to_unit(values):
    values = values.astype(jnp.float32)
    return (values * lax.rsqrt(jnp.sum(values * values, axis=-1, keepdims=True) + 1e-06)).astype(
        jnp.bfloat16
    )


def arrival_plan(n):
    orders = []
    for place in range(n):
        first = 1 if place < n // 2 else -1
        if 0 < place < n - 1:
            first = -first
        order = [place]
        for step in range(1, n):
            for way in (first, -first):
                if 0 <= place + way * step < n:
                    order.append(place + way * step)
        orders.append(order)
    moves = []
    for place in range(n):
        for slot in range(1, n):
            block = orders[place][slot]
            source = place + (1 if block > place else -1)
            moves.append((source, place, orders[source].index(block), slot))
    return orders, moves


def pick(index, values):
    result = jnp.int32(values[0])
    for number in range(1, len(values)):
        if values[number] != values[0]:
            result = jnp.where(index == number, jnp.int32(values[number]), result)
    return result


def score_kernel(n_sources, choice, ids, *refs):
    sources = refs[:n_sources]
    units_in, log_mix = refs[n_sources], refs[n_sources + 1]
    scores, rows_out, totals, raw, units, sem = refs[-6:]

    @pl.when(pl.program_id(0) == 0)
    def _():
        chosen = pick(ids[0], choice)
        for number, source in enumerate(sources):

            @pl.when(chosen == number)
            def _():
                pltpu.make_async_copy(source, raw, sem).start()

        pltpu.make_async_copy(sources[0], raw, sem).wait()
        values = raw[...].astype(jnp.float32)
        square = jnp.sum(values * values, axis=-1, keepdims=True)
        unit = (values * lax.rsqrt(square + 1e-06)).astype(jnp.bfloat16)
        units[...] = unit
        rows_out[...] = unit
        totals[...] = jnp.zeros_like(totals)

    cosines = lax.dot_general(
        units_in[...], units[...], (((1,), (1,)), ((), ())), preferred_element_type=jnp.float32
    )
    offset = log_mix[...]
    repeats = cosines.shape[1] // offset.shape[1]
    if repeats > 1:
        offset = jnp.concatenate([offset] * repeats, axis=1)
    value = jnp.exp2(cosines * (concentration * LOG2E) + offset)
    scores[...] = value
    totals[0] += jnp.sum(value, axis=0, keepdims=True)


def score_block(ids, sources, choice, blocks, who, units, offsets, carried, column, n_columns):
    part, depth = sources[0].shape
    count = units.shape[0]
    tile = math.gcd(count, 512)
    shapes = (
        jax.ShapeDtypeStruct((count, n_columns * part), jnp.float32),
        jax.ShapeDtypeStruct((n_columns * part, depth), jnp.bfloat16),
        jax.ShapeDtypeStruct((n_columns, 1, part), jnp.float32),
    )
    n_sources = len(sources)
    aliases = {}
    extra = ()
    if carried is not None:
        extra = carried
        aliases = {1 + n_sources + 2 + i: i for i in range(3)}
    anywhere = pl.BlockSpec(memory_space=pl.ANY)
    return pl.pallas_call(
        functools.partial(score_kernel, n_sources, choice),
        grid_spec=pltpu.PrefetchScalarGridSpec(
            num_scalar_prefetch=1,
            grid=(count // tile,),
            in_specs=[anywhere] * n_sources
            + [
                pl.BlockSpec((tile, depth), lambda t, s: (t, 0)),
                pl.BlockSpec((tile, offsets.shape[1]), lambda t, s: (t, 0)),
            ]
            + [anywhere] * len(extra),
            out_specs=[
                pl.BlockSpec((tile, part), lambda t, s: (t, column)),
                pl.BlockSpec((part, depth), lambda t, s: (column, 0)),
                pl.BlockSpec(
                    (1, 1, part),
                    lambda t, s: (pick(s[0], blocks) * CORES + ((s[1] % CORES) ^ who), 0, 0),
                ),
            ],
            scratch_shapes=[
                pltpu.VMEM((part, depth), jnp.bfloat16),
                pltpu.VMEM((part, depth), jnp.bfloat16),
                pltpu.SemaphoreType.DMA,
            ],
        ),
        out_shape=shapes,
        input_output_aliases=aliases,
        compiler_params=pltpu.CompilerParams(vmem_limit_bytes=VMEM_LIMIT),
        cost_estimate=pl.CostEstimate(
            flops=2 * count * part * depth,
            bytes_accessed=2 * (count * part * 4 + count * depth * 2),
            transcendentals=count * part,
        ),
        name="scores",
    )(ids, *sources, units, offsets, *extra)


def sum_kernel(orders, n_totals, ids, *refs):
    totals = refs[:n_totals]
    scores, rows, sent, mine, masses, inverse, total, mass = refs[n_totals:]
    step = pl.program_id(0)
    n_columns = inverse.shape[0]

    @pl.when(step == 0)
    def _():
        for column in range(n_columns):
            slot, who = divmod(column, CORES)
            place = pick(ids[0], [order[slot] for order in orders]) * CORES + (
                (ids[1] % CORES) ^ who
            )
            value = totals[0][place]
            for more in totals[1:]:
                value = value + more[place]
            inverse[column] = 1.0 / value
        total[...] = jnp.zeros_like(total)
        mass[...] = jnp.zeros_like(mass)

    resp = (scores[...] * inverse[step]).astype(jnp.bfloat16)
    total[...] += lax.dot_general(
        resp, rows[...], (((1,), (0,)), ((), ())), preferred_element_type=jnp.float32
    )
    wide = resp.astype(jnp.float32)
    partial = wide[:, :LANES]
    for start in range(LANES, wide.shape[1], LANES):
        partial = partial + wide[:, start : start + LANES]
    mass[...] += partial

    @pl.when(step == pl.num_programs(0) - 1)
    def _():
        size = mine.shape[0]
        quarter = ids[1] // CORES
        for number in range(total.shape[0] // size):
            block = total[number * size : (number + 1) * size, :]
            away = quarter ^ number

            @pl.when(away == 0)
            def _():
                mine[...] = block

            @pl.when(away != 0)
            def _():
                sent[away - 1] = block.astype(sent.dtype)

        masses[...] = jnp.sum(mass[...].T, axis=0, keepdims=True)


def sum_rows(ids, orders, totals, scores, rows, n_owners):
    count, width = scores.shape
    depth = rows.shape[1]
    size = count // n_owners
    n_columns, _, part = totals[0].shape
    return pl.pallas_call(
        functools.partial(sum_kernel, orders, len(totals)),
        grid_spec=pltpu.PrefetchScalarGridSpec(
            num_scalar_prefetch=1,
            grid=(n_columns,),
            in_specs=[pl.BlockSpec(totals[0].shape, lambda t, s: (0, 0, 0)) for _ in totals]
            + [
                pl.BlockSpec((count, part), lambda t, s: (0, t)),
                pl.BlockSpec((part, depth), lambda t, s: (t, 0)),
            ],
            out_specs=[
                pl.BlockSpec((n_owners - 1, size, depth), lambda t, s: (0, 0, 0)),
                pl.BlockSpec((size, depth), lambda t, s: (0, 0)),
                pl.BlockSpec((1, count), lambda t, s: (0, 0)),
            ],
            scratch_shapes=[
                pltpu.VMEM((n_columns, 1, part), jnp.float32),
                pltpu.VMEM((count, depth), jnp.float32),
                pltpu.VMEM((count, LANES), jnp.float32),
            ],
        ),
        out_shape=(
            jax.ShapeDtypeStruct((n_owners - 1, size, depth), jnp.bfloat16),
            jax.ShapeDtypeStruct((size, depth), jnp.float32),
            jax.ShapeDtypeStruct((1, count), jnp.float32),
        ),
        compiler_params=pltpu.CompilerParams(vmem_limit_bytes=VMEM_LIMIT),
        cost_estimate=pl.CostEstimate(
            flops=2 * count * width * depth,
            bytes_accessed=count * (width * 4 + depth * 4) + width * depth * 2,
            transcendentals=0,
        ),
        name="sums",
    )(ids, *totals, scores, rows)


def local(embeddings, centroids, log_mix):
    n_places = lax.axis_size("blk")
    n_rows = lax.axis_size("rows")
    n_owners = n_rows // CORES
    place = lax.axis_index("blk")
    me = lax.axis_index("rows")
    core = lax.rem(me, CORES)
    held, depth = embeddings.shape
    local_centroids = centroids.shape[0]
    half = local_centroids // CORES
    ids = jnp.stack([place, me]).astype(jnp.int32)
    orders, moves = arrival_plan(n_places)

    def exchange(array, distance):
        return lax.ppermute(array, "rows", [(i, i ^ distance) for i in range(n_rows)])

    def swap_cores(array, places):
        pairs = [
            (spot * n_rows + i, spot * n_rows + (i ^ 1)) for spot in places for i in range(n_rows)
        ]
        return lax.ppermute(array, ("blk", "rows"), pairs)

    slots = [[(embeddings, list(range(n_places)))]] + [[] for _ in range(n_places - 1)]

    def start_ready(moves):
        groups = {}
        left = []
        for move in moves:
            source, target, source_slot, slot = move
            holds = [n for n, (_, places) in enumerate(slots[source_slot]) if source in places]
            if not holds:
                left.append(move)
                continue
            turn = 0
            while any(source == s for s, _ in groups.get((slot, source_slot, holds[0], turn), [])):
                turn += 1
            groups.setdefault((slot, source_slot, holds[0], turn), []).append((source, target))
        moved = [
            (slot, lax.ppermute(slots[source_slot][hold][0], "blk", pairs), [p[1] for p in pairs])
            for (slot, source_slot, hold, _), pairs in sorted(groups.items())
        ]
        return moved, left

    def merged(candidates):
        if len(candidates) <= 2:
            return candidates
        array, held_at = candidates[0][0], list(candidates[0][1])
        for other, places in candidates[1:]:
            here = functools.reduce(jnp.logical_or, [place == spot for spot in places])
            array = jnp.where(here, other, array)
            held_at += places
        return [(array, held_at)]

    own_centroids = lax.dynamic_slice_in_dim(centroids, core * half, half, 0)
    own_mix = lax.dynamic_slice_in_dim(log_mix, core * half, half, 0)
    units = to_unit(own_centroids)
    offsets = jnp.broadcast_to(((own_mix - concentration) * LOG2E)[:, None], (half, LANES))

    n_columns = n_places * CORES
    carried = None

    def scores_of(slot, carried):
        blocks = [order[slot] for order in orders]
        swapped = [(swap_cores(array, places), places) for array, places in slots[slot]]
        for who, candidates in enumerate((slots[slot], swapped)):
            choice = [
                next(n for n, (_, places) in enumerate(candidates) if spot in places)
                for spot in range(n_places)
            ]
            carried = score_block(
                ids,
                [array for array, _ in candidates],
                choice,
                blocks,
                who,
                units,
                offsets,
                carried,
                slot * CORES + who,
                n_columns,
            )
        return carried

    for turn in range(n_places):
        while sum(len(places) for _, places in slots[turn]) < n_places:
            moved, moves = start_ready(moves)
            for slot, array, places in moved:
                slots[slot].append((array, places))
        slots[turn] = merged(slots[turn])
        moved, moves = start_ready(moves)
        carried = scores_of(turn, carried)
        if moved:
            arrays, carried = lax.optimization_barrier(([array for _, array, _ in moved], carried))
            for (slot, _, places), array in zip(moved, arrays):
                slots[slot].append((array, places))
    scores, rows, totals = carried
    totals = totals + exchange(totals, 1)
    all_totals = [totals] + [
        lax.ppermute(totals, "blk", [(i, (i + turn) % n_places) for i in range(n_places)])
        for turn in range(1, n_places)
    ]

    sent, summed, masses = sum_rows(ids, orders, all_totals, scores, rows, n_owners)
    far = [CORES * away for away in range(1, n_owners)]
    arrived = [exchange(sent[number], distance) for number, distance in enumerate(far)]
    for array in arrived:
        summed = summed + array.astype(jnp.float32)

    distance = CORES
    while distance < n_rows:
        masses = masses + exchange(masses, distance)
        distance *= 2
    masses = masses.reshape(half)
    other_masses = exchange(masses, 1)
    both = jnp.where(
        core == 0,
        jnp.concatenate([masses, other_masses]),
        jnp.concatenate([other_masses, masses]),
    )

    unit = summed * lax.rsqrt(jnp.sum(summed * summed, axis=1, keepdims=True) + 1e-06)
    unit = unit.astype(jnp.float16)
    size = unit.shape[0]
    result = jnp.zeros((local_centroids, depth), jnp.float32)
    pieces = [(0, unit)] + [(distance, exchange(unit, distance)) for distance in far]
    for distance, piece in pieces:
        for flip, array in ((0, piece), (1, exchange(piece, 1))):
            start = (core ^ flip) * half + lax.div(me ^ distance, CORES) * size
            result = lax.dynamic_update_slice(result, array.astype(jnp.float32), (start, 0))
    count = local_centroids * n_places
    factor = count / (held * n_rows * n_places)
    return (result, both * factor)


def solution(mesh):
    return jax.shard_map(
        local,
        mesh=mesh,
        in_specs=(P(("blk", "rows"), None), P("blk", None), P("blk")),
        out_specs=(P("blk", None), P("blk")),
        check_vma=False,
    )
```

```python
import functools
import math

import jax
import jax.numpy as jnp
from jax import lax
from jax.experimental import pallas as pl
from jax.experimental.pallas import tpu as pltpu
from jax.sharding import PartitionSpec as P

concentration = 32.0
LOG2E = math.log2(math.e)
LANES = 128
CORES = 2
VMEM_LIMIT = 48 * 1024 * 1024


def to_unit(values):
    values = values.astype(jnp.float32)
    return (values * lax.rsqrt(jnp.sum(values * values, axis=-1, keepdims=True) + 1e-06)).astype(
        jnp.bfloat16
    )


def arrival_plan(n):
    orders = []
    for place in range(n):
        first = 1 if place < n // 2 else -1
        if 0 < place < n - 1:
            first = -first
        order = [place]
        for step in range(1, n):
            for way in (first, -first):
                if 0 <= place + way * step < n:
                    order.append(place + way * step)
        orders.append(order)
    moves = []
    for place in range(n):
        for slot in range(1, n):
            block = orders[place][slot]
            source = place + (1 if block > place else -1)
            moves.append((source, place, orders[source].index(block), slot))
    return orders, moves


def pick(index, values):
    result = jnp.int32(values[0])
    for number in range(1, len(values)):
        if values[number] != values[0]:
            result = jnp.where(index == number, jnp.int32(values[number]), result)
    return result


def score_kernel(n_sources, choice, ids, *refs):
    sources = refs[:n_sources]
    units_in, log_mix = refs[n_sources], refs[n_sources + 1]
    scores, rows_out, totals, raw, units, sem = refs[-6:]

    @pl.when(pl.program_id(0) == 0)
    def _():
        chosen = pick(ids[0], choice)
        for number, source in enumerate(sources):

            @pl.when(chosen == number)
            def _():
                pltpu.make_async_copy(source, raw, sem).start()

        pltpu.make_async_copy(sources[0], raw, sem).wait()
        values = raw[...].astype(jnp.float32)
        square = jnp.sum(values * values, axis=-1, keepdims=True)
        unit = (values * lax.rsqrt(square + 1e-06)).astype(jnp.bfloat16)
        units[...] = unit
        rows_out[...] = unit
        totals[...] = jnp.zeros_like(totals)

    cosines = lax.dot_general(
        units_in[...], units[...], (((1,), (1,)), ((), ())), preferred_element_type=jnp.float32
    )
    offset = log_mix[...]
    repeats = cosines.shape[1] // offset.shape[1]
    if repeats > 1:
        offset = jnp.concatenate([offset] * repeats, axis=1)
    value = jnp.exp2(cosines * (concentration * LOG2E) + offset)
    scores[...] = value
    totals[0] += jnp.sum(value, axis=0, keepdims=True)


def score_block(
    ids, sources, choice, blocks, who, units, offsets, carried, column, n_columns, number, n_parts
):
    part, depth = sources[0].shape
    count = units.shape[0]
    tile = math.gcd(count, 512)
    held = part * n_parts
    column = column * n_parts + number
    shapes = (
        jax.ShapeDtypeStruct((count, n_columns * held), jnp.float32),
        jax.ShapeDtypeStruct((n_columns * held, depth), jnp.bfloat16),
        jax.ShapeDtypeStruct((n_columns, 1, held), jnp.float32),
    )
    n_sources = len(sources)
    aliases = {}
    extra = ()
    if carried is not None:
        extra = carried
        aliases = {1 + n_sources + 2 + i: i for i in range(3)}
    anywhere = pl.BlockSpec(memory_space=pl.ANY)
    return pl.pallas_call(
        functools.partial(score_kernel, n_sources, choice),
        grid_spec=pltpu.PrefetchScalarGridSpec(
            num_scalar_prefetch=1,
            grid=(count // tile,),
            in_specs=[anywhere] * n_sources
            + [
                pl.BlockSpec((tile, depth), lambda t, s: (t, 0)),
                pl.BlockSpec((tile, offsets.shape[1]), lambda t, s: (t, 0)),
            ]
            + [anywhere] * len(extra),
            out_specs=[
                pl.BlockSpec((tile, part), lambda t, s: (t, column)),
                pl.BlockSpec((part, depth), lambda t, s: (column, 0)),
                pl.BlockSpec(
                    (1, 1, part),
                    lambda t, s: (pick(s[0], blocks) * CORES + ((s[1] % CORES) ^ who), 0, number),
                ),
            ],
            scratch_shapes=[
                pltpu.VMEM((part, depth), jnp.bfloat16),
                pltpu.VMEM((part, depth), jnp.bfloat16),
                pltpu.SemaphoreType.DMA,
            ],
        ),
        out_shape=shapes,
        input_output_aliases=aliases,
        compiler_params=pltpu.CompilerParams(vmem_limit_bytes=VMEM_LIMIT),
        cost_estimate=pl.CostEstimate(
            flops=2 * count * part * depth,
            bytes_accessed=2 * (count * part * 4 + count * depth * 2),
            transcendentals=count * part,
        ),
        name="scores",
    )(ids, *sources, units, offsets, *extra)


def sum_kernel(orders, n_totals, ids, *refs):
    totals = refs[:n_totals]
    scores, rows, sent, mine, masses, inverse, total, mass = refs[n_totals:]
    step = pl.program_id(0)
    n_columns = inverse.shape[0]

    @pl.when(step == 0)
    def _():
        for column in range(n_columns):
            slot, who = divmod(column, CORES)
            place = pick(ids[0], [order[slot] for order in orders]) * CORES + (
                (ids[1] % CORES) ^ who
            )
            value = totals[0][place]
            for more in totals[1:]:
                value = value + more[place]
            inverse[column] = 1.0 / value
        total[...] = jnp.zeros_like(total)
        mass[...] = jnp.zeros_like(mass)

    resp = (scores[...] * inverse[step]).astype(jnp.bfloat16)
    total[...] += lax.dot_general(
        resp, rows[...], (((1,), (0,)), ((), ())), preferred_element_type=jnp.float32
    )
    wide = resp.astype(jnp.float32)
    partial = wide[:, :LANES]
    for start in range(LANES, wide.shape[1], LANES):
        partial = partial + wide[:, start : start + LANES]
    mass[...] += partial

    @pl.when(step == pl.num_programs(0) - 1)
    def _():
        size = mine.shape[0]
        quarter = ids[1] // CORES
        for number in range(total.shape[0] // size):
            block = total[number * size : (number + 1) * size, :]
            away = quarter ^ number

            @pl.when(away == 0)
            def _():
                mine[...] = block

            @pl.when(away != 0)
            def _():
                sent[away - 1] = block.astype(sent.dtype)

        masses[...] = jnp.sum(mass[...].T, axis=0, keepdims=True)


def sum_rows(ids, orders, totals, scores, rows, n_owners):
    count, width = scores.shape
    depth = rows.shape[1]
    size = count // n_owners
    n_columns, _, part = totals[0].shape
    return pl.pallas_call(
        functools.partial(sum_kernel, orders, len(totals)),
        grid_spec=pltpu.PrefetchScalarGridSpec(
            num_scalar_prefetch=1,
            grid=(n_columns,),
            in_specs=[pl.BlockSpec(totals[0].shape, lambda t, s: (0, 0, 0)) for _ in totals]
            + [
                pl.BlockSpec((count, part), lambda t, s: (0, t)),
                pl.BlockSpec((part, depth), lambda t, s: (t, 0)),
            ],
            out_specs=[
                pl.BlockSpec((n_owners - 1, size, depth), lambda t, s: (0, 0, 0)),
                pl.BlockSpec((size, depth), lambda t, s: (0, 0)),
                pl.BlockSpec((1, count), lambda t, s: (0, 0)),
            ],
            scratch_shapes=[
                pltpu.VMEM((n_columns, 1, part), jnp.float32),
                pltpu.VMEM((count, depth), jnp.float32),
                pltpu.VMEM((count, LANES), jnp.float32),
            ],
        ),
        out_shape=(
            jax.ShapeDtypeStruct((n_owners - 1, size, depth), jnp.bfloat16),
            jax.ShapeDtypeStruct((size, depth), jnp.float32),
            jax.ShapeDtypeStruct((1, count), jnp.float32),
        ),
        compiler_params=pltpu.CompilerParams(vmem_limit_bytes=VMEM_LIMIT),
        cost_estimate=pl.CostEstimate(
            flops=2 * count * width * depth,
            bytes_accessed=count * (width * 4 + depth * 4) + width * depth * 2,
            transcendentals=0,
        ),
        name="sums",
    )(ids, *totals, scores, rows)


def local(embeddings, centroids, log_mix):
    n_places = lax.axis_size("blk")
    n_rows = lax.axis_size("rows")
    n_owners = n_rows // CORES
    place = lax.axis_index("blk")
    me = lax.axis_index("rows")
    core = lax.rem(me, CORES)
    held, depth = embeddings.shape
    local_centroids = centroids.shape[0]
    half = local_centroids // CORES
    ids = jnp.stack([place, me]).astype(jnp.int32)
    orders, moves = arrival_plan(n_places)

    def exchange(array, distance):
        return lax.ppermute(array, "rows", [(i, i ^ distance) for i in range(n_rows)])

    def swap_cores(array, places):
        pairs = [
            (spot * n_rows + i, spot * n_rows + (i ^ 1)) for spot in places for i in range(n_rows)
        ]
        return lax.ppermute(array, ("blk", "rows"), pairs)

    last_parts = 2 if held % (2 * LANES) == 0 and n_places > 2 else 1

    def parts_of(slot):
        return last_parts if slot == n_places - 1 else 1

    slots = [[[] for _ in range(parts_of(slot))] for slot in range(n_places)]
    slots[0][0].append((embeddings, list(range(n_places))))
    moves = [move + (part,) for part in range(last_parts) for move in moves if part < parts_of(move[3])]

    def start_ready(moves):
        groups = {}
        left = []
        for move in moves:
            source, target, source_slot, slot, part = move
            whole = parts_of(source_slot) < parts_of(slot)
            holders = slots[source_slot][0 if whole else part]
            holds = [n for n, (_, places) in enumerate(holders) if source in places]
            if not holds:
                left.append(move)
                continue
            turn = 0
            key = lambda turn: (part, slot, source_slot, holds[0], turn)
            while any(source == s for s, _ in groups.get(key(turn), [])):
                turn += 1
            groups.setdefault(key(turn), []).append((source, target))
        moved = []
        for (part, slot, source_slot, hold, _), pairs in sorted(groups.items()):
            whole = parts_of(source_slot) < parts_of(slot)
            array = slots[source_slot][0 if whole else part][hold][0]
            if whole:
                size = held // parts_of(slot)
                array = array[part * size : (part + 1) * size]
            moved.append((slot, part, lax.ppermute(array, "blk", pairs), [p[1] for p in pairs]))
        return moved, left

    def merged(candidates):
        if len(candidates) <= 2:
            return candidates
        array, held_at = candidates[0][0], list(candidates[0][1])
        for other, places in candidates[1:]:
            here = functools.reduce(jnp.logical_or, [place == spot for spot in places])
            array = jnp.where(here, other, array)
            held_at += places
        return [(array, held_at)]

    own_centroids = lax.dynamic_slice_in_dim(centroids, core * half, half, 0)
    own_mix = lax.dynamic_slice_in_dim(log_mix, core * half, half, 0)
    units = to_unit(own_centroids)
    offsets = jnp.broadcast_to(((own_mix - concentration) * LOG2E)[:, None], (half, LANES))

    n_columns = n_places * CORES
    carried = None

    def scores_of(slot, part, carried):
        blocks = [order[slot] for order in orders]
        arrived = slots[slot][part]
        swapped = [(swap_cores(array, places), places) for array, places in arrived]
        for who, candidates in enumerate((arrived, swapped)):
            choice = [
                next(n for n, (_, places) in enumerate(candidates) if spot in places)
                for spot in range(n_places)
            ]
            carried = score_block(
                ids,
                [array for array, _ in candidates],
                choice,
                blocks,
                who,
                units,
                offsets,
                carried,
                slot * CORES + who,
                n_columns,
                part,
                parts_of(slot),
            )
        return carried

    def arrive(moved):
        for slot, part, array, places in moved:
            slots[slot][part].append((array, places))

    for turn in range(n_places):
        for part in range(parts_of(turn)):
            while sum(len(places) for _, places in slots[turn][part]) < n_places:
                moved, moves = start_ready(moves)
                arrive(moved)
            slots[turn][part] = merged(slots[turn][part])
            moved, moves = start_ready(moves)
            carried = scores_of(turn, part, carried)
            arrive([m for m in moved if m[1] + 1 < parts_of(m[0])])
            moved = [m for m in moved if m[1] + 1 == parts_of(m[0])]
            if moved:
                arrays, carried = lax.optimization_barrier(([m[2] for m in moved], carried))
                arrive([(slot, p, array, places) for (slot, p, _, places), array in zip(moved, arrays)])
    scores, rows, totals = carried
    totals = totals + exchange(totals, 1)
    all_totals = [totals] + [
        lax.ppermute(totals, "blk", [(i, (i + turn) % n_places) for i in range(n_places)])
        for turn in range(1, n_places)
    ]

    sent, summed, masses = sum_rows(ids, orders, all_totals, scores, rows, n_owners)
    far = [CORES * away for away in range(1, n_owners)]
    arrived = [exchange(sent[number], distance) for number, distance in enumerate(far)]
    arrived_masses = [exchange(masses, distance) for distance in far]
    arrived, arrived_masses = lax.optimization_barrier((arrived, arrived_masses))
    for array in arrived:
        summed = summed + array.astype(jnp.float32)

    unit = summed * lax.rsqrt(jnp.sum(summed * summed, axis=1, keepdims=True) + 1e-06)
    unit = unit.astype(jnp.float16)
    size = unit.shape[0]
    pieces = [exchange(unit, distance) for distance in far]
    masses = functools.reduce(jnp.add, arrived_masses, masses)
    masses = masses.reshape(half)
    other_masses = exchange(masses, 1)
    both = jnp.where(
        core == 0,
        jnp.concatenate([masses, other_masses]),
        jnp.concatenate([other_masses, masses]),
    )
    def place_piece(result, distance, flip, array):
        start = (core ^ flip) * half + lax.div(me ^ distance, CORES) * size
        return lax.dynamic_update_slice(result, array.astype(jnp.float32), (start, 0))

    result = jnp.zeros((local_centroids, depth), jnp.float32)
    result = place_piece(result, 0, 0, unit)
    result = place_piece(result, 0, 1, exchange(unit, 1))
    pieces, result = lax.optimization_barrier((pieces, result))
    swapped = [exchange(piece, 1) for piece in pieces]
    for flip, arrays in ((0, pieces), (1, swapped)):
        for distance, array in zip(far, arrays):
            result = place_piece(result, distance, flip, array)
    count = local_centroids * n_places
    factor = count / (held * n_rows * n_places)
    return (result, both * factor)


def solution(mesh):
    return jax.shard_map(
        local,
        mesh=mesh,
        in_specs=(P(("blk", "rows"), None), P("blk", None), P("blk")),
        out_specs=(P("blk", None), P("blk")),
        check_vma=False,
    )
```

```python
import functools
import math

import jax
import jax.numpy as jnp
from jax import lax
from jax.experimental import pallas as pl
from jax.experimental.pallas import tpu as pltpu
from jax.sharding import PartitionSpec as P

concentration = 32.0
LOG2E = math.log2(math.e)
LANES = 128
CORES = 2
EXTRA = 16
VMEM_LIMIT = 48 * 1024 * 1024


def to_unit(values):
    values = values.astype(jnp.float32)
    return (values * lax.rsqrt(jnp.sum(values * values, axis=-1, keepdims=True) + 1e-06)).astype(
        jnp.bfloat16
    )


def arrival_plan(n):
    orders = []
    for place in range(n):
        first = 1 if place < n // 2 else -1
        if 0 < place < n - 1:
            first = -first
        order = [place]
        for step in range(1, n):
            for way in (first, -first):
                if 0 <= place + way * step < n:
                    order.append(place + way * step)
        orders.append(order)
    moves = []
    for place in range(n):
        for slot in range(1, n):
            block = orders[place][slot]
            source = place + (1 if block > place else -1)
            moves.append((source, place, orders[source].index(block), slot))
    return orders, moves


def pick(index, values):
    result = jnp.int32(values[0])
    for number in range(1, len(values)):
        if values[number] != values[0]:
            result = jnp.where(index == number, jnp.int32(values[number]), result)
    return result


def score_kernel(n_sources, choice, ids, *refs):
    sources = refs[:n_sources]
    units_in, log_mix = refs[n_sources], refs[n_sources + 1]
    scores, rows_out, totals, raw, units, sem = refs[-6:]

    @pl.when(pl.program_id(0) == 0)
    def _():
        chosen = pick(ids[0], choice)
        for number, source in enumerate(sources):

            @pl.when(chosen == number)
            def _():
                pltpu.make_async_copy(source, raw, sem).start()

        pltpu.make_async_copy(sources[0], raw, sem).wait()
        values = raw[...].astype(jnp.float32)
        square = jnp.sum(values * values, axis=-1, keepdims=True)
        unit = (values * lax.rsqrt(square + 1e-06)).astype(jnp.bfloat16)
        units[...] = unit
        rows_out[...] = unit
        totals[...] = jnp.zeros_like(totals)

    cosines = lax.dot_general(
        units_in[...], units[...], (((1,), (1,)), ((), ())), preferred_element_type=jnp.float32
    )
    offset = log_mix[...]
    repeats = cosines.shape[1] // offset.shape[1]
    if repeats > 1:
        offset = jnp.concatenate([offset] * repeats, axis=1)
    value = jnp.exp2(cosines * (concentration * LOG2E) + offset)
    scores[...] = value
    totals[0] += jnp.sum(value, axis=0, keepdims=True)


def score_block(
    ids, sources, choice, blocks, who, units, offsets, carried, column, n_columns, number, n_parts
):
    part, depth = sources[0].shape
    count = units.shape[0]
    tile = math.gcd(count, 512)
    held = part * n_parts
    column = column * n_parts + number
    shapes = (
        jax.ShapeDtypeStruct((count, n_columns * held), jnp.float32),
        jax.ShapeDtypeStruct((n_columns * held, depth), jnp.bfloat16),
        jax.ShapeDtypeStruct((n_columns, 1, held), jnp.float32),
    )
    n_sources = len(sources)
    aliases = {}
    extra = ()
    if carried is not None:
        extra = carried
        aliases = {1 + n_sources + 2 + i: i for i in range(3)}
    anywhere = pl.BlockSpec(memory_space=pl.ANY)
    return pl.pallas_call(
        functools.partial(score_kernel, n_sources, choice),
        grid_spec=pltpu.PrefetchScalarGridSpec(
            num_scalar_prefetch=1,
            grid=(count // tile,),
            in_specs=[anywhere] * n_sources
            + [
                pl.BlockSpec((tile, depth), lambda t, s: (t, 0)),
                pl.BlockSpec((tile, offsets.shape[1]), lambda t, s: (t, 0)),
            ]
            + [anywhere] * len(extra),
            out_specs=[
                pl.BlockSpec((tile, part), lambda t, s: (t, column)),
                pl.BlockSpec((part, depth), lambda t, s: (column, 0)),
                pl.BlockSpec(
                    (1, 1, part),
                    lambda t, s: (pick(s[0], blocks) * CORES + ((s[1] % CORES) ^ who), 0, number),
                ),
            ],
            scratch_shapes=[
                pltpu.VMEM((part, depth), jnp.bfloat16),
                pltpu.VMEM((part, depth), jnp.bfloat16),
                pltpu.SemaphoreType.DMA,
            ],
        ),
        out_shape=shapes,
        input_output_aliases=aliases,
        compiler_params=pltpu.CompilerParams(vmem_limit_bytes=VMEM_LIMIT),
        cost_estimate=pl.CostEstimate(
            flops=part * depth, bytes_accessed=part * depth, transcendentals=0
        ),
        name="scores",
    )(ids, *sources, units, offsets, *extra)


def sum_kernel(orders, n_totals, ids, *refs):
    totals = refs[:n_totals]
    scores, rows, sent, mine, masses, inverse, total, mass = refs[n_totals:]
    step = pl.program_id(0)
    n_columns = inverse.shape[0]

    @pl.when(step == 0)
    def _():
        for column in range(n_columns):
            slot, who = divmod(column, CORES)
            place = pick(ids[0], [order[slot] for order in orders]) * CORES + (
                (ids[1] % CORES) ^ who
            )
            value = totals[0][place]
            for more in totals[1:]:
                value = value + more[place]
            inverse[column] = 1.0 / value
        total[...] = jnp.zeros_like(total)
        mass[...] = jnp.zeros_like(mass)

    resp = (scores[...] * inverse[step]).astype(jnp.bfloat16)
    total[...] += lax.dot_general(
        resp, rows[...], (((1,), (0,)), ((), ())), preferred_element_type=jnp.float32
    )
    wide = resp.astype(jnp.float32)
    partial = wide[:, :LANES]
    for start in range(LANES, wide.shape[1], LANES):
        partial = partial + wide[:, start : start + LANES]
    mass[...] += partial

    @pl.when(step == pl.num_programs(0) - 1)
    def _():
        size, depth = mine.shape
        quarter = ids[1] // CORES
        sums = jnp.sum(mass[...].T, axis=0, keepdims=True)
        line = lax.broadcasted_iota(jnp.int32, (EXTRA, size), 0)
        for number in range(total.shape[0] // size):
            block = total[number * size : (number + 1) * size, :]
            own = sums[:, number * size : (number + 1) * size]
            away = quarter ^ number

            @pl.when(away == 0)
            def _():
                mine[...] = block
                masses[...] = own

            @pl.when(away != 0)
            def _():
                sent[away - 1, :size, :] = block.astype(sent.dtype)
                high = own.astype(sent.dtype).astype(jnp.float32)
                rest = own - high
                middle = rest.astype(sent.dtype).astype(jnp.float32)
                low = rest - middle
                three = jnp.where(
                    line == 0, high, jnp.where(line == 1, middle, jnp.where(line == 2, low, 0.0))
                )
                sent[away - 1, size:, :size] = three.astype(sent.dtype)
                if size < depth:
                    sent[away - 1, size:, size:] = jnp.zeros((EXTRA, depth - size), sent.dtype)


def sum_rows(ids, orders, totals, scores, rows, n_owners):
    count, width = scores.shape
    depth = rows.shape[1]
    size = count // n_owners
    n_columns, _, part = totals[0].shape
    return pl.pallas_call(
        functools.partial(sum_kernel, orders, len(totals)),
        grid_spec=pltpu.PrefetchScalarGridSpec(
            num_scalar_prefetch=1,
            grid=(n_columns,),
            in_specs=[pl.BlockSpec(totals[0].shape, lambda t, s: (0, 0, 0)) for _ in totals]
            + [
                pl.BlockSpec((count, part), lambda t, s: (0, t)),
                pl.BlockSpec((part, depth), lambda t, s: (t, 0)),
            ],
            out_specs=[
                pl.BlockSpec((n_owners - 1, size + EXTRA, depth), lambda t, s: (0, 0, 0)),
                pl.BlockSpec((size, depth), lambda t, s: (0, 0)),
                pl.BlockSpec((1, size), lambda t, s: (0, 0)),
            ],
            scratch_shapes=[
                pltpu.VMEM((n_columns, 1, part), jnp.float32),
                pltpu.VMEM((count, depth), jnp.float32),
                pltpu.VMEM((count, LANES), jnp.float32),
            ],
        ),
        out_shape=(
            jax.ShapeDtypeStruct((n_owners - 1, size + EXTRA, depth), jnp.bfloat16),
            jax.ShapeDtypeStruct((size, depth), jnp.float32),
            jax.ShapeDtypeStruct((1, size), jnp.float32),
        ),
        compiler_params=pltpu.CompilerParams(vmem_limit_bytes=VMEM_LIMIT),
        cost_estimate=pl.CostEstimate(
            flops=2 * count * width * depth,
            bytes_accessed=count * (width * 4 + depth * 4) + width * depth * 2,
            transcendentals=0,
        ),
        name="sums",
    )(ids, *totals, scores, rows)


def local(embeddings, centroids, log_mix):
    n_places = lax.axis_size("blk")
    n_rows = lax.axis_size("rows")
    n_owners = n_rows // CORES
    place = lax.axis_index("blk")
    me = lax.axis_index("rows")
    core = lax.rem(me, CORES)
    held, depth = embeddings.shape
    local_centroids = centroids.shape[0]
    half = local_centroids // CORES
    ids = jnp.stack([place, me]).astype(jnp.int32)
    orders, moves = arrival_plan(n_places)

    def exchange(array, distance):
        return lax.ppermute(array, "rows", [(i, i ^ distance) for i in range(n_rows)])

    def swap_cores(array, places):
        pairs = [
            (spot * n_rows + i, spot * n_rows + (i ^ 1)) for spot in places for i in range(n_rows)
        ]
        return lax.ppermute(array, ("blk", "rows"), pairs)

    last_parts = 1

    def parts_of(slot):
        return last_parts if slot == n_places - 1 else 1

    slots = [[[] for _ in range(parts_of(slot))] for slot in range(n_places)]
    slots[0][0].append((embeddings, list(range(n_places))))
    moves = [move + (part,) for part in range(last_parts) for move in moves if part < parts_of(move[3])]

    def start_ready(moves, last_source):
        groups = {}
        left = []
        for move in moves:
            source, target, source_slot, slot, part = move
            if source_slot > last_source:
                left.append(move)
                continue
            whole = parts_of(source_slot) < parts_of(slot)
            holders = slots[source_slot][0 if whole else part]
            holds = [n for n, (_, places) in enumerate(holders) if source in places]
            if not holds:
                left.append(move)
                continue
            turn = 0
            key = lambda turn: (part, slot, source_slot, holds[0], turn)
            while any(source == s for s, _ in groups.get(key(turn), [])):
                turn += 1
            groups.setdefault(key(turn), []).append((source, target))
        moved = []
        for (part, slot, source_slot, hold, _), pairs in sorted(
            groups.items(), reverse=True
        ):
            whole = parts_of(source_slot) < parts_of(slot)
            array = slots[source_slot][0 if whole else part][hold][0]
            if whole:
                size = held // parts_of(slot)
                array = array[part * size : (part + 1) * size]
            moved.append((slot, part, lax.ppermute(array, "blk", pairs), [p[1] for p in pairs]))
        return moved, left

    def merged(candidates):
        if len(candidates) <= 2:
            return candidates
        array, held_at = candidates[0][0], list(candidates[0][1])
        for other, places in candidates[1:]:
            here = functools.reduce(jnp.logical_or, [place == spot for spot in places])
            array = jnp.where(here, other, array)
            held_at += places
        return [(array, held_at)]

    own_centroids = lax.dynamic_slice_in_dim(centroids, core * half, half, 0)
    own_mix = lax.dynamic_slice_in_dim(log_mix, core * half, half, 0)
    units = to_unit(own_centroids)
    offsets = jnp.broadcast_to(((own_mix - concentration) * LOG2E)[:, None], (half, LANES))

    n_columns = n_places * CORES
    carried = None

    def scores_of(slot, part, carried, between):
        blocks = [order[slot] for order in orders]
        arrived = slots[slot][part]
        swapped = [(swap_cores(array, places), places) for array, places in arrived]
        for who, candidates in enumerate((arrived, swapped)):
            choice = [
                next(n for n, (_, places) in enumerate(candidates) if spot in places)
                for spot in range(n_places)
            ]
            carried = score_block(
                ids,
                [array for array, _ in candidates],
                choice,
                blocks,
                who,
                units,
                offsets,
                carried,
                slot * CORES + who,
                n_columns,
                part,
                parts_of(slot),
            )
            if who == 0:
                carried = between(carried)
        return carried

    def arrive(moved):
        for slot, part, array, places in moved:
            slots[slot][part].append((array, places))

    early = []
    for turn in range(n_places):
        for part in range(parts_of(turn)):
            while sum(len(places) for _, places in slots[turn][part]) < n_places:
                moved, moves = start_ready(moves, n_places)
                arrive(moved)
            slots[turn][part] = merged(slots[turn][part])
            moved, moves = start_ready(moves, turn)

            def between(carried):
                nonlocal moves, moved, early
                if early:
                    arrays, carried = lax.optimization_barrier(([m[2] for m in early], carried))
                    for (slot, p, _, places), array in zip(early, arrays):
                        held_arrays = slots[slot][p]
                        old = [n for n, (_, spots) in enumerate(held_arrays) if spots == places]
                        held_arrays[old[0]] = (array, places)
                more, moves = start_ready(moves, n_places)
                moved = moved + more
                return carried

            carried = scores_of(turn, part, carried, between)
            early = [m for m in moved if m[0] != turn + 1]
            arrive(early)
            now = [m for m in moved if m[0] == turn + 1]
            if now and turn == 0:
                arrays, carried = lax.optimization_barrier(([m[2] for m in now], carried))
                now = [(slot, p, array, places) for (slot, p, _, places), array in zip(now, arrays)]
            arrive(now)
    scores, rows, totals = carried
    totals = totals + exchange(totals, 1)
    all_totals = [totals] + [
        lax.ppermute(totals, "blk", [(i, (i + turn) % n_places) for i in range(n_places)])
        for turn in range(1, n_places)
    ]

    sent, summed, masses = sum_rows(ids, orders, all_totals, scores, rows, n_owners)
    far = [CORES * away for away in range(1, n_owners)]
    arrived = [exchange(sent[number], distance) for number, distance in enumerate(far)]
    size = summed.shape[0]
    masses = masses.reshape(size)
    for array in arrived:
        wide = array.astype(jnp.float32)
        summed = summed + wide[:size]
        masses = masses + (wide[size, :size] + wide[size + 1, :size] + wide[size + 2, :size])

    unit = summed * lax.rsqrt(jnp.sum(summed * summed, axis=1, keepdims=True) + 1e-06)
    unit = unit.astype(jnp.float16)
    pieces = [exchange(unit, distance) for distance in far]
    both = lax.all_gather(masses, "rows").reshape(n_owners, CORES, size)
    both = both.transpose(1, 0, 2).reshape(local_centroids)

    def place_piece(result, distance, flip, array):
        start = (core ^ flip) * half + lax.div(me ^ distance, CORES) * size
        return lax.dynamic_update_slice(result, array.astype(jnp.float32), (start, 0))

    result = jnp.zeros((local_centroids, depth), jnp.float32)
    result = place_piece(result, 0, 0, unit)
    result = place_piece(result, 0, 1, exchange(unit, 1))
    pieces, result = lax.optimization_barrier((pieces, result))
    swapped = [exchange(piece, 1) for piece in pieces]
    for flip, arrays in ((0, pieces), (1, swapped)):
        for distance, array in zip(far, arrays):
            result = place_piece(result, distance, flip, array)
    count = local_centroids * n_places
    factor = count / (held * n_rows * n_places)
    return (result, both * factor)


def solution(mesh):
    return jax.shard_map(
        local,
        mesh=mesh,
        in_specs=(P(("blk", "rows"), None), P("blk", None), P("blk")),
        out_specs=(P("blk", None), P("blk")),
        check_vma=False,
    )
```

```python
import functools
import math

import jax
import jax.numpy as jnp
from jax import lax
from jax.experimental import pallas as pl
from jax.experimental.pallas import tpu as pltpu
from jax.sharding import PartitionSpec as P

concentration = 32.0
LOG2E = math.log2(math.e)
LANES = 128
CORES = 2
EXTRA = 16
VMEM_LIMIT = 48 * 1024 * 1024


def to_unit(values):
    values = values.astype(jnp.float32)
    return (values * lax.rsqrt(jnp.sum(values * values, axis=-1, keepdims=True) + 1e-06)).astype(
        jnp.bfloat16
    )


def arrival_plan(n):
    orders = []
    for place in range(n):
        first = 1 if place < n // 2 else -1
        if 0 < place < n - 1:
            first = -first
        order = [place]
        for step in range(1, n):
            for way in (first, -first):
                if 0 <= place + way * step < n:
                    order.append(place + way * step)
        orders.append(order)
    moves = []
    for place in range(n):
        for slot in range(1, n):
            block = orders[place][slot]
            source = place + (1 if block > place else -1)
            moves.append((source, place, orders[source].index(block), slot))
    return orders, moves


def pick(index, values):
    result = jnp.int32(values[0])
    for number in range(1, len(values)):
        if values[number] != values[0]:
            result = jnp.where(index == number, jnp.int32(values[number]), result)
    return result


def score_kernel(n_sources, choice, ids, *refs):
    sources = refs[:n_sources]
    units_in, log_mix = refs[n_sources], refs[n_sources + 1]
    scores, rows_out, totals, raw, units, sem = refs[-6:]

    @pl.when(pl.program_id(0) == 0)
    def _():
        chosen = pick(ids[0], choice)
        for number, source in enumerate(sources):

            @pl.when(chosen == number)
            def _():
                pltpu.make_async_copy(source, raw, sem).start()

        pltpu.make_async_copy(sources[0], raw, sem).wait()
        values = raw[...].astype(jnp.float32)
        square = jnp.sum(values * values, axis=-1, keepdims=True)
        unit = (values * lax.rsqrt(square + 1e-06)).astype(jnp.bfloat16)
        units[...] = unit
        rows_out[...] = unit
        totals[...] = jnp.zeros_like(totals)

    cosines = lax.dot_general(
        units_in[...], units[...], (((1,), (1,)), ((), ())), preferred_element_type=jnp.float32
    )
    offset = log_mix[...]
    repeats = cosines.shape[1] // offset.shape[1]
    if repeats > 1:
        offset = jnp.concatenate([offset] * repeats, axis=1)
    value = jnp.exp2(cosines * (concentration * LOG2E) + offset)
    scores[...] = value
    totals[0] += jnp.sum(value, axis=0, keepdims=True)


def score_block(ids, sources, choice, blocks, who, units, offsets, carried, column, n_columns):
    part, depth = sources[0].shape
    count = units.shape[0]
    tile = math.gcd(count, 512)
    shapes = (
        jax.ShapeDtypeStruct((count, n_columns * part), jnp.float32),
        jax.ShapeDtypeStruct((n_columns * part, depth), jnp.bfloat16),
        jax.ShapeDtypeStruct((n_columns, 1, part), jnp.float32),
    )
    n_sources = len(sources)
    aliases = {}
    extra = ()
    if carried is not None:
        extra = carried
        aliases = {1 + n_sources + 2 + i: i for i in range(3)}
    anywhere = pl.BlockSpec(memory_space=pl.ANY)
    return pl.pallas_call(
        functools.partial(score_kernel, n_sources, choice),
        grid_spec=pltpu.PrefetchScalarGridSpec(
            num_scalar_prefetch=1,
            grid=(count // tile,),
            in_specs=[anywhere] * n_sources
            + [
                pl.BlockSpec((tile, depth), lambda t, s: (t, 0)),
                pl.BlockSpec((tile, offsets.shape[1]), lambda t, s: (t, 0)),
            ]
            + [anywhere] * len(extra),
            out_specs=[
                pl.BlockSpec((tile, part), lambda t, s: (t, column)),
                pl.BlockSpec((part, depth), lambda t, s: (column, 0)),
                pl.BlockSpec(
                    (1, 1, part),
                    lambda t, s: (pick(s[0], blocks) * CORES + ((s[1] % CORES) ^ who), 0, 0),
                ),
            ],
            scratch_shapes=[
                pltpu.VMEM((part, depth), jnp.bfloat16),
                pltpu.VMEM((part, depth), jnp.bfloat16),
                pltpu.SemaphoreType.DMA,
            ],
        ),
        out_shape=shapes,
        input_output_aliases=aliases,
        compiler_params=pltpu.CompilerParams(vmem_limit_bytes=VMEM_LIMIT),
        cost_estimate=pl.CostEstimate(
            flops=2 * count * part * depth,
            bytes_accessed=2 * (count * part * 4 + count * depth * 2),
            transcendentals=count * part,
        ),
        name="scores",
    )(ids, *sources, units, offsets, *extra)


def sum_plan(orders):
    n = len(orders)
    last = {order[-1] for order in orders}
    sorted_slots = []
    for order in orders:
        slots = list(range(n))
        sorted_slots.append(sorted(slots, key=lambda slot: (order[slot] in last, slot)))
    steps = []
    for turn in range(n):
        slots = [sorted_slots[place][turn] for place in range(n)]
        blocks = [orders[place][slot] for place, slot in enumerate(slots)]
        for who in range(CORES):
            steps.append(([slot * CORES + who for slot in slots], blocks, who))
    return steps


def three_rows(values, dtype, depth):
    size = values.shape[1]
    line = lax.broadcasted_iota(jnp.int32, (EXTRA, size), 0)
    high = values.astype(dtype).astype(jnp.float32)
    rest = values - high
    middle = rest.astype(dtype).astype(jnp.float32)
    low = rest - middle
    rows = jnp.where(
        line == 0, high, jnp.where(line == 1, middle, jnp.where(line == 2, low, 0.0))
    )
    if size < depth:
        rows = jnp.concatenate([rows, jnp.zeros((EXTRA, depth - size), jnp.float32)], axis=1)
    return rows.astype(dtype)


def one_row(rows, size):
    return jnp.sum(rows[:, :size].astype(jnp.float32), axis=0, keepdims=True)


def sum_kernel(plan, n_totals, n_owners, first, last, ids, *refs):
    totals = refs[:n_totals]
    scores, rows = refs[n_totals], refs[n_totals + 1]
    state = refs[n_totals + 2 : n_totals + 4]
    total, mass, inverse = refs[-3:]
    outs = refs[n_totals + (2 if first else 4) : -3]
    step = pl.program_id(0)

    @pl.when(step == 0)
    def _():
        for number, (_, blocks, who) in enumerate(plan):
            place = pick(ids[0], blocks) * CORES + ((ids[1] % CORES) ^ who)
            value = totals[0][place]
            for more in totals[1:]:
                value = value + more[place]
            inverse[number] = 1.0 / value
        if first:
            total[...] = jnp.zeros_like(total)
            mass[...] = jnp.zeros_like(mass)
        else:
            total[...] = state[0][...]
            mass[...] = state[1][...]

    resp = (scores[...] * inverse[step]).astype(jnp.bfloat16)
    total[...] += lax.dot_general(
        resp, rows[...], (((1,), (0,)), ((), ())), preferred_element_type=jnp.float32
    )
    wide = resp.astype(jnp.float32)
    partial = wide[:, :LANES]
    for start in range(LANES, wide.shape[1], LANES):
        partial = partial + wide[:, start : start + LANES]
    mass[...] += partial

    @pl.when(step == pl.num_programs(0) - 1)
    def _():
        if not last:
            outs[0][...] = total[...]
            outs[1][...] = mass[...]
            return
        sent = outs[:-2]
        mine, masses = outs[-2:]
        size, depth = mine.shape
        quarter = ids[1] // CORES
        sums = jnp.sum(mass[...].T, axis=0, keepdims=True)
        for number in range(n_owners):
            block = total[number * size : (number + 1) * size, :]
            own = sums[:, number * size : (number + 1) * size]

            @pl.when(quarter == number)
            def _():
                mine[...] = block
                masses[...] = own

            for away in range(1, n_owners):

                @pl.when(quarter ^ number == away)
                def _():
                    target = sent[away - 1]
                    target[:size, :] = block.astype(target.dtype)
                    target[size:, :] = three_rows(own, target.dtype, depth)


def sum_rows(ids, plan, totals, scores, rows, n_owners, carried, last):
    count = scores.shape[0]
    depth = rows.shape[1]
    size = count // n_owners
    part = totals[0].shape[2]
    first = carried is None
    column = lambda t, s: sum(
        jnp.where(t == n, pick(s[0], columns), 0) for n, (columns, _, _) in enumerate(plan)
    )
    fixed = lambda shape: pl.BlockSpec(shape, lambda t, s: (0,) * len(shape))
    in_specs = [fixed(totals[0].shape) for _ in totals] + [
        pl.BlockSpec((count, part), lambda t, s: (0, column(t, s))),
        pl.BlockSpec((part, depth), lambda t, s: (column(t, s), 0)),
    ]
    state = [(count, depth), (count, LANES)]
    if not first:
        in_specs += [fixed(shape) for shape in state]
    if last:
        shapes = [((size + EXTRA, depth), jnp.bfloat16)] * (n_owners - 1) + [
            ((size, depth), jnp.float32),
            ((1, size), jnp.float32),
        ]
    else:
        shapes = [(shape, jnp.float32) for shape in state]
    return pl.pallas_call(
        functools.partial(sum_kernel, plan, len(totals), n_owners, first, last),
        grid_spec=pltpu.PrefetchScalarGridSpec(
            num_scalar_prefetch=1,
            grid=(len(plan),),
            in_specs=in_specs,
            out_specs=[fixed(shape) for shape, _ in shapes],
            scratch_shapes=[
                pltpu.VMEM((count, depth), jnp.float32),
                pltpu.VMEM((count, LANES), jnp.float32),
                pltpu.VMEM((len(plan), 1, part), jnp.float32),
            ],
        ),
        out_shape=[jax.ShapeDtypeStruct(shape, dtype) for shape, dtype in shapes],
        compiler_params=pltpu.CompilerParams(vmem_limit_bytes=VMEM_LIMIT),
        cost_estimate=pl.CostEstimate(
            flops=2 * count * len(plan) * part * depth,
            bytes_accessed=len(plan) * part * (count * 4 + depth * 2) + count * depth * 4,
            transcendentals=0,
        ),
        name="sums",
    )(ids, *totals, scores, rows, *(carried or ()))


def combine_kernel(mine, masses, *refs):
    arrived, out = refs[:-1], refs[-1]
    size, depth = mine.shape
    total = mine[...]
    mass = masses[...]
    for ref in arrived:
        total = total + ref[:size, :].astype(jnp.float32)
        mass = mass + one_row(ref[size:, :], size)
    square = jnp.sum(total * total, axis=1, keepdims=True)
    out[:size, :] = (total * lax.rsqrt(square + 1e-06)).astype(out.dtype)
    out[size:, :] = three_rows(mass, out.dtype, depth)


def combine(mine, masses, arrived):
    size, depth = mine.shape
    return pl.pallas_call(
        combine_kernel,
        out_shape=jax.ShapeDtypeStruct((size + EXTRA, depth), jnp.bfloat16),
        compiler_params=pltpu.CompilerParams(vmem_limit_bytes=VMEM_LIMIT),
        name="combine",
    )(mine, masses, *arrived)


def assemble_kernel(factor, n_pieces, ids, *refs):
    pieces = refs[:n_pieces]
    units, weights = refs[-2:]
    size = units.shape[0]
    for number, piece in enumerate(pieces):

        @pl.when(pl.program_id(0) == number)
        def _():
            units[...] = piece[:size, :].astype(jnp.float32)
            weights[0] = one_row(piece[size:, :], size) * factor


def assemble(ids, pieces, carried, n_blocks, factor):
    size, depth = pieces[0][2].shape
    size -= EXTRA
    half = n_blocks // CORES
    flips = [flip for flip, _, _ in pieces]
    aways = [away for _, away, _ in pieces]

    def block(t, s):
        return ((s[1] % CORES) ^ pick(t, flips)) * half + ((s[1] // CORES) ^ pick(t, aways))

    extra = carried or ()
    aliases = {1 + len(pieces) + n: n for n in range(len(extra))}
    return pl.pallas_call(
        functools.partial(assemble_kernel, factor, len(pieces)),
        grid_spec=pltpu.PrefetchScalarGridSpec(
            num_scalar_prefetch=1,
            grid=(len(pieces),),
            in_specs=[pl.BlockSpec((size + EXTRA, depth), lambda t, s: (0, 0)) for _ in pieces]
            + [pl.BlockSpec(memory_space=pl.ANY) for _ in extra],
            out_specs=[
                pl.BlockSpec((size, depth), lambda t, s: (block(t, s), 0)),
                pl.BlockSpec((1, 1, size), lambda t, s: (block(t, s), 0, 0)),
            ],
        ),
        out_shape=[
            jax.ShapeDtypeStruct((n_blocks * size, depth), jnp.float32),
            jax.ShapeDtypeStruct((n_blocks, 1, size), jnp.float32),
        ],
        input_output_aliases=aliases,
        compiler_params=pltpu.CompilerParams(vmem_limit_bytes=VMEM_LIMIT),
        name="assemble",
    )(ids, *[payload for _, _, payload in pieces], *extra)


def local(embeddings, centroids, log_mix):
    n_places = lax.axis_size("blk")
    n_rows = lax.axis_size("rows")
    n_owners = n_rows // CORES
    place = lax.axis_index("blk")
    me = lax.axis_index("rows")
    core = lax.rem(me, CORES)
    held, depth = embeddings.shape
    local_centroids = centroids.shape[0]
    half = local_centroids // CORES
    ids = jnp.stack([place, me]).astype(jnp.int32)
    orders, moves = arrival_plan(n_places)

    def exchange(array, distance):
        return lax.ppermute(array, "rows", [(i, i ^ distance) for i in range(n_rows)])

    def swap_cores(array, places):
        pairs = [
            (spot * n_rows + i, spot * n_rows + (i ^ 1)) for spot in places for i in range(n_rows)
        ]
        return lax.ppermute(array, ("blk", "rows"), pairs)

    slots = [[(embeddings, list(range(n_places)))]] + [[] for _ in range(n_places - 1)]

    def start_ready(moves):
        groups = {}
        left = []
        for move in moves:
            source, target, source_slot, slot = move
            holds = [n for n, (_, places) in enumerate(slots[source_slot]) if source in places]
            if not holds:
                left.append(move)
                continue
            turn = 0
            while any(source == s for s, _ in groups.get((slot, source_slot, holds[0], turn), [])):
                turn += 1
            groups.setdefault((slot, source_slot, holds[0], turn), []).append((source, target))
        moved = [
            (slot, lax.ppermute(slots[source_slot][hold][0], "blk", pairs), [p[1] for p in pairs])
            for (slot, source_slot, hold, _), pairs in sorted(groups.items())
        ]
        return moved, left

    def merged(candidates):
        if len(candidates) <= 2:
            return candidates
        array, held_at = candidates[0][0], list(candidates[0][1])
        for other, places in candidates[1:]:
            here = functools.reduce(jnp.logical_or, [place == spot for spot in places])
            array = jnp.where(here, other, array)
            held_at += places
        return [(array, held_at)]

    own_centroids = lax.dynamic_slice_in_dim(centroids, core * half, half, 0)
    own_mix = lax.dynamic_slice_in_dim(log_mix, core * half, half, 0)
    units = to_unit(own_centroids)
    offsets = jnp.broadcast_to(((own_mix - concentration) * LOG2E)[:, None], (half, LANES))

    n_columns = n_places * CORES
    carried = None

    def scores_of(slot, carried):
        blocks = [order[slot] for order in orders]
        swapped = [(swap_cores(array, places), places) for array, places in slots[slot]]
        for who, candidates in enumerate((slots[slot], swapped)):
            choice = [
                next(n for n, (_, places) in enumerate(candidates) if spot in places)
                for spot in range(n_places)
            ]
            carried = score_block(
                ids,
                [array for array, _ in candidates],
                choice,
                blocks,
                who,
                units,
                offsets,
                carried,
                slot * CORES + who,
                n_columns,
            )
        return carried

    def totals_of(own):
        both = own + exchange(own, 1)
        return [both] + [
            lax.ppermute(both, "blk", [(i, (i + turn) % n_places) for i in range(n_places)])
            for turn in range(1, n_places)
        ]

    settled = {
        block for block in range(n_places) if all(order[-1] != block for order in orders)
    }
    early_totals = None
    for turn in range(n_places):
        while sum(len(places) for _, places in slots[turn]) < n_places:
            moved, moves = start_ready(moves)
            for slot, array, places in moved:
                slots[slot].append((array, places))
        slots[turn] = merged(slots[turn])
        moved, moves = start_ready(moves)
        carried = scores_of(turn, carried)
        if turn == n_places - 2 and settled:
            early_totals = totals_of(carried[2])
            early_totals, carried = lax.optimization_barrier((early_totals, carried))
        if moved:
            arrays, carried = lax.optimization_barrier(([array for _, array, _ in moved], carried))
            for (slot, _, places), array in zip(moved, arrays):
                slots[slot].append((array, places))
    scores, rows, totals = carried
    steps = sum_plan(orders)
    late = totals_of(totals)
    if early_totals is not None:
        ready = [step for step in steps if all(block in settled for block in step[1])]
        rest = [step for step in steps if step not in ready]
        state = sum_rows(ids, ready, early_totals, scores, rows, n_owners, None, False)
        late, state = lax.optimization_barrier((late, state))
    else:
        rest, state = steps, None
    *sent, mine, masses = sum_rows(ids, rest, late, scores, rows, n_owners, state, True)
    far = [CORES * away for away in range(1, n_owners)]
    arrived = [exchange(array, distance) for array, distance in zip(sent, far)]
    payload = combine(mine, masses, arrived)

    count = local_centroids * n_places
    factor = count / (held * n_rows * n_places)
    pieces = [exchange(payload, distance) for distance in far]
    done = assemble(
        ids, [(0, 0, payload), (1, 0, exchange(payload, 1))], None, n_rows, factor
    )
    pieces, done = lax.optimization_barrier((pieces, done))
    placed = [(0, away + 1, piece) for away, piece in enumerate(pieces)]
    placed += [(1, away + 1, exchange(piece, 1)) for away, piece in enumerate(pieces)]
    result, weights = assemble(ids, placed, done, n_rows, factor)
    return (result, weights.reshape(local_centroids))


def solution(mesh):
    return jax.shard_map(
        local,
        mesh=mesh,
        in_specs=(P(("blk", "rows"), None), P("blk", None), P("blk")),
        out_specs=(P("blk", None), P("blk")),
        check_vma=False,
    )
```

```python
import functools
import math

import jax
import jax.numpy as jnp
from jax import lax
from jax.experimental import pallas as pl
from jax.experimental.pallas import tpu as pltpu
from jax.sharding import PartitionSpec as P

concentration = 32.0
LOG2E = math.log2(math.e)
LANES = 128
CORES = 2
EXTRA = 16
VMEM_LIMIT = 48 * 1024 * 1024


def to_unit(values):
    values = values.astype(jnp.float32)
    return (values * lax.rsqrt(jnp.sum(values * values, axis=-1, keepdims=True) + 1e-06)).astype(
        jnp.bfloat16
    )


def arrival_plan(n):
    orders = []
    for place in range(n):
        first = 1 if place < n // 2 else -1
        if 0 < place < n - 1:
            first = -first
        order = [place]
        for step in range(1, n):
            for way in (first, -first):
                if 0 <= place + way * step < n:
                    order.append(place + way * step)
        orders.append(order)
    moves = []
    for place in range(n):
        for slot in range(1, n):
            block = orders[place][slot]
            source = place + (1 if block > place else -1)
            moves.append((source, place, orders[source].index(block), slot))
    return orders, moves


def pick(index, values):
    result = jnp.int32(values[0])
    for number in range(1, len(values)):
        if values[number] != values[0]:
            result = jnp.where(index == number, jnp.int32(values[number]), result)
    return result


def score_kernel(n_sources, choice, ids, *refs):
    sources = refs[:n_sources]
    units_in, log_mix = refs[n_sources], refs[n_sources + 1]
    scores, rows_out, totals, raw, units, sem = refs[-6:]

    @pl.when(pl.program_id(0) == 0)
    def _():
        chosen = pick(ids[0], choice)
        for number, source in enumerate(sources):

            @pl.when(chosen == number)
            def _():
                pltpu.make_async_copy(source, raw, sem).start()

        pltpu.make_async_copy(sources[0], raw, sem).wait()
        values = raw[...].astype(jnp.float32)
        square = jnp.sum(values * values, axis=-1, keepdims=True)
        unit = (values * lax.rsqrt(square + 1e-06)).astype(jnp.bfloat16)
        units[...] = unit
        rows_out[...] = unit
        totals[...] = jnp.zeros_like(totals)

    cosines = lax.dot_general(
        units_in[...], units[...], (((1,), (1,)), ((), ())), preferred_element_type=jnp.float32
    )
    offset = log_mix[...]
    repeats = cosines.shape[1] // offset.shape[1]
    if repeats > 1:
        offset = jnp.concatenate([offset] * repeats, axis=1)
    value = jnp.exp2(cosines * (concentration * LOG2E) + offset)
    scores[...] = value
    totals[0] += jnp.sum(value, axis=0, keepdims=True)


def score_block(ids, sources, choice, blocks, who, units, offsets, carried, column, n_columns):
    part, depth = sources[0].shape
    count = units.shape[0]
    tile = math.gcd(count, 512)
    shapes = (
        jax.ShapeDtypeStruct((count, n_columns * part), jnp.float32),
        jax.ShapeDtypeStruct((n_columns * part, depth), jnp.bfloat16),
        jax.ShapeDtypeStruct((n_columns, 1, part), jnp.float32),
    )
    n_sources = len(sources)
    aliases = {}
    extra = ()
    if carried is not None:
        extra = carried
        aliases = {1 + n_sources + 2 + i: i for i in range(3)}
    anywhere = pl.BlockSpec(memory_space=pl.ANY)
    return pl.pallas_call(
        functools.partial(score_kernel, n_sources, choice),
        grid_spec=pltpu.PrefetchScalarGridSpec(
            num_scalar_prefetch=1,
            grid=(count // tile,),
            in_specs=[anywhere] * n_sources
            + [
                pl.BlockSpec((tile, depth), lambda t, s: (t, 0)),
                pl.BlockSpec((tile, offsets.shape[1]), lambda t, s: (t, 0)),
            ]
            + [anywhere] * len(extra),
            out_specs=[
                pl.BlockSpec((tile, part), lambda t, s: (t, column)),
                pl.BlockSpec((part, depth), lambda t, s: (column, 0)),
                pl.BlockSpec(
                    (1, 1, part),
                    lambda t, s: (pick(s[0], blocks) * CORES + ((s[1] % CORES) ^ who), 0, 0),
                ),
            ],
            scratch_shapes=[
                pltpu.VMEM((part, depth), jnp.bfloat16),
                pltpu.VMEM((part, depth), jnp.bfloat16),
                pltpu.SemaphoreType.DMA,
            ],
        ),
        out_shape=shapes,
        input_output_aliases=aliases,
        compiler_params=pltpu.CompilerParams(vmem_limit_bytes=VMEM_LIMIT),
        cost_estimate=pl.CostEstimate(
            flops=2 * count * part * depth,
            bytes_accessed=2 * (count * part * 4 + count * depth * 2),
            transcendentals=count * part,
        ),
        name="scores",
    )(ids, *sources, units, offsets, *extra)


def sum_plan(orders):
    n = len(orders)
    last = {order[-1] for order in orders}
    sorted_slots = []
    for order in orders:
        slots = list(range(n))
        sorted_slots.append(sorted(slots, key=lambda slot: (order[slot] in last, slot)))
    steps = []
    for turn in range(n):
        slots = [sorted_slots[place][turn] for place in range(n)]
        blocks = [orders[place][slot] for place, slot in enumerate(slots)]
        for who in range(CORES):
            steps.append(([slot * CORES + who for slot in slots], blocks, who))
    return steps


def three_rows(values, dtype, depth):
    size = values.shape[1]
    line = lax.broadcasted_iota(jnp.int32, (EXTRA, size), 0)
    high = values.astype(dtype).astype(jnp.float32)
    rest = values - high
    middle = rest.astype(dtype).astype(jnp.float32)
    low = rest - middle
    rows = jnp.where(
        line == 0, high, jnp.where(line == 1, middle, jnp.where(line == 2, low, 0.0))
    )
    if size < depth:
        rows = jnp.concatenate([rows, jnp.zeros((EXTRA, depth - size), jnp.float32)], axis=1)
    return rows.astype(dtype)


def one_row(rows, size):
    return jnp.sum(rows[:, :size].astype(jnp.float32), axis=0, keepdims=True)


def sum_kernel(plan, n_totals, n_owners, first, last, ids, *refs):
    totals = refs[:n_totals]
    scores, rows = refs[n_totals], refs[n_totals + 1]
    state = refs[n_totals + 2 : n_totals + 4]
    total, mass, inverse = refs[-3:]
    outs = refs[n_totals + (2 if first else 4) : -3]
    step = pl.program_id(0)

    @pl.when(step == 0)
    def _():
        for number, (_, blocks, who) in enumerate(plan):
            place = pick(ids[0], blocks) * CORES + ((ids[1] % CORES) ^ who)
            value = totals[0][place]
            for more in totals[1:]:
                value = value + more[place]
            inverse[number] = 1.0 / value
        if first:
            total[...] = jnp.zeros_like(total)
            mass[...] = jnp.zeros_like(mass)
        else:
            total[...] = state[0][...]
            mass[...] = state[1][...]

    resp = (scores[...] * inverse[step]).astype(jnp.bfloat16)
    total[...] += lax.dot_general(
        resp, rows[...], (((1,), (0,)), ((), ())), preferred_element_type=jnp.float32
    )
    wide = resp.astype(jnp.float32)
    partial = wide[:, :LANES]
    for start in range(LANES, wide.shape[1], LANES):
        partial = partial + wide[:, start : start + LANES]
    mass[...] += partial

    @pl.when(step == pl.num_programs(0) - 1)
    def _():
        if not last:
            outs[0][...] = total[...]
            outs[1][...] = mass[...]
            return
        sent = outs[:-2]
        mine, masses = outs[-2:]
        size, depth = mine.shape
        upper = size // 2
        quarter = ids[1] // CORES
        sums = jnp.sum(mass[...].T, axis=0, keepdims=True)
        for number in range(n_owners):
            block = total[number * size : (number + 1) * size, :]
            own = sums[:, number * size : (number + 1) * size]

            @pl.when(quarter == number)
            def _():
                mine[...] = block
                masses[...] = own

            for away in range(1, n_owners):

                @pl.when(quarter ^ number == away)
                def _():
                    first_half, second_half = sent[2 * away - 2 : 2 * away]
                    first_half[...] = block[:upper].astype(first_half.dtype)
                    second_half[: size - upper, :] = block[upper:].astype(second_half.dtype)
                    second_half[size - upper :, :] = three_rows(own, second_half.dtype, depth)


def sum_rows(ids, plan, totals, scores, rows, n_owners, carried, last):
    count = scores.shape[0]
    depth = rows.shape[1]
    size = count // n_owners
    part = totals[0].shape[2]
    first = carried is None
    column = lambda t, s: sum(
        jnp.where(t == n, pick(s[0], columns), 0) for n, (columns, _, _) in enumerate(plan)
    )
    fixed = lambda shape: pl.BlockSpec(shape, lambda t, s: (0,) * len(shape))
    in_specs = [fixed(totals[0].shape) for _ in totals] + [
        pl.BlockSpec((count, part), lambda t, s: (0, column(t, s))),
        pl.BlockSpec((part, depth), lambda t, s: (column(t, s), 0)),
    ]
    state = [(count, depth), (count, LANES)]
    if not first:
        in_specs += [fixed(shape) for shape in state]
    if last:
        shapes = []
        for away in range(1, n_owners):
            kept = [n_owners == 4 and keep == away for keep in (2, 1)]
            for keep, height in zip(kept, (size // 2, size - size // 2 + EXTRA)):
                shapes.append(((height, depth), jnp.float32 if keep else jnp.bfloat16))
        shapes += [((size, depth), jnp.float32), ((1, size), jnp.float32)]
    else:
        shapes = [(shape, jnp.float32) for shape in state]
    return pl.pallas_call(
        functools.partial(sum_kernel, plan, len(totals), n_owners, first, last),
        grid_spec=pltpu.PrefetchScalarGridSpec(
            num_scalar_prefetch=1,
            grid=(len(plan),),
            in_specs=in_specs,
            out_specs=[fixed(shape) for shape, _ in shapes],
            scratch_shapes=[
                pltpu.VMEM((count, depth), jnp.float32),
                pltpu.VMEM((count, LANES), jnp.float32),
                pltpu.VMEM((len(plan), 1, part), jnp.float32),
            ],
        ),
        out_shape=[jax.ShapeDtypeStruct(shape, dtype) for shape, dtype in shapes],
        compiler_params=pltpu.CompilerParams(vmem_limit_bytes=VMEM_LIMIT),
        cost_estimate=pl.CostEstimate(
            flops=2 * count * len(plan) * part * depth,
            bytes_accessed=len(plan) * part * (count * 4 + depth * 2) + count * depth * 4,
            transcendentals=0,
        ),
        name="sums",
    )(ids, *totals, scores, rows, *(carried or ()))


def pass_on_kernel(has_masses, size, mine, arrived, out):
    depth = mine.shape[1]
    height = mine.shape[0] - (EXTRA if has_masses else 0)
    total = mine[:height, :] + arrived[:height, :].astype(jnp.float32)
    out[:height, :] = total.astype(out.dtype)
    if has_masses:
        mass = one_row(mine[height:, :], size) + one_row(arrived[height:, :], size)
        out[height:, :] = three_rows(mass, out.dtype, depth)


def pass_on(mine, arrived, has_masses, size):
    return pl.pallas_call(
        functools.partial(pass_on_kernel, has_masses, size),
        out_shape=jax.ShapeDtypeStruct(arrived.shape, arrived.dtype),
        compiler_params=pltpu.CompilerParams(vmem_limit_bytes=VMEM_LIMIT),
        name="pass_on",
    )(mine, arrived)


def combine_kernel(mine, masses, *refs):
    first_out, second_out = refs[-2:]
    size, depth = mine.shape
    upper = size // 2
    first = mine[:upper, :]
    second = mine[upper:, :]
    mass = masses[...]
    for ref in refs[:-2]:
        if ref.shape[0] == upper:
            first = first + ref[...].astype(jnp.float32)
        else:
            second = second + ref[: size - upper, :].astype(jnp.float32)
            mass = mass + one_row(ref[size - upper :, :], size)
    for total, out in ((first, first_out), (second, second_out)):
        square = jnp.sum(total * total, axis=1, keepdims=True)
        out[: total.shape[0], :] = (total * lax.rsqrt(square + 1e-06)).astype(out.dtype)
    second_out[size - upper :, :] = three_rows(mass, second_out.dtype, depth)


def combine(mine, masses, arrived):
    size, depth = mine.shape
    upper = size // 2
    return pl.pallas_call(
        combine_kernel,
        out_shape=[
            jax.ShapeDtypeStruct((upper, depth), jnp.bfloat16),
            jax.ShapeDtypeStruct((size - upper + EXTRA, depth), jnp.bfloat16),
        ],
        compiler_params=pltpu.CompilerParams(vmem_limit_bytes=VMEM_LIMIT),
        name="combine",
    )(mine, masses, *arrived)


def assemble_kernel(factor, n_pieces, ids, *refs):
    units, weights = refs[-2:]
    size = units.shape[0]
    upper = size // 2
    for number in range(n_pieces):

        @pl.when(pl.program_id(0) == number)
        def _():
            first, second = refs[2 * number : 2 * number + 2]
            units[:upper, :] = first[...].astype(jnp.float32)
            units[upper:, :] = second[: size - upper, :].astype(jnp.float32)
            weights[0] = one_row(second[size - upper :, :], size) * factor


def assemble(ids, pieces, carried, n_blocks, factor):
    arrays = [array for _, _, halves in pieces for array in halves]
    depth = arrays[0].shape[1]
    size = arrays[0].shape[0] + arrays[1].shape[0] - EXTRA
    half = n_blocks // CORES
    flips = [flip for flip, _, _ in pieces]
    aways = [away for _, away, _ in pieces]

    def block(t, s):
        return ((s[1] % CORES) ^ pick(t, flips)) * half + ((s[1] // CORES) ^ pick(t, aways))

    extra = carried or ()
    aliases = {1 + len(arrays) + n: n for n in range(len(extra))}
    return pl.pallas_call(
        functools.partial(assemble_kernel, factor, len(pieces)),
        grid_spec=pltpu.PrefetchScalarGridSpec(
            num_scalar_prefetch=1,
            grid=(len(pieces),),
            in_specs=[pl.BlockSpec(array.shape, lambda t, s: (0, 0)) for array in arrays]
            + [pl.BlockSpec(memory_space=pl.ANY) for _ in extra],
            out_specs=[
                pl.BlockSpec((size, depth), lambda t, s: (block(t, s), 0)),
                pl.BlockSpec((1, 1, size), lambda t, s: (block(t, s), 0, 0)),
            ],
        ),
        out_shape=[
            jax.ShapeDtypeStruct((n_blocks * size, depth), jnp.float32),
            jax.ShapeDtypeStruct((n_blocks, 1, size), jnp.float32),
        ],
        input_output_aliases=aliases,
        compiler_params=pltpu.CompilerParams(vmem_limit_bytes=VMEM_LIMIT),
        name="assemble",
    )(ids, *arrays, *extra)


def local(embeddings, centroids, log_mix):
    n_places = lax.axis_size("blk")
    n_rows = lax.axis_size("rows")
    n_owners = n_rows // CORES
    place = lax.axis_index("blk")
    me = lax.axis_index("rows")
    core = lax.rem(me, CORES)
    held, depth = embeddings.shape
    local_centroids = centroids.shape[0]
    half = local_centroids // CORES
    ids = jnp.stack([place, me]).astype(jnp.int32)
    orders, moves = arrival_plan(n_places)

    def exchange(array, distance):
        return lax.ppermute(array, "rows", [(i, i ^ distance) for i in range(n_rows)])

    def swap_cores(array, places):
        pairs = [
            (spot * n_rows + i, spot * n_rows + (i ^ 1)) for spot in places for i in range(n_rows)
        ]
        return lax.ppermute(array, ("blk", "rows"), pairs)

    slots = [[(embeddings, list(range(n_places)))]] + [[] for _ in range(n_places - 1)]

    def start_ready(moves):
        groups = {}
        left = []
        for move in moves:
            source, target, source_slot, slot = move
            holds = [n for n, (_, places) in enumerate(slots[source_slot]) if source in places]
            if not holds:
                left.append(move)
                continue
            turn = 0
            while any(source == s for s, _ in groups.get((slot, source_slot, holds[0], turn), [])):
                turn += 1
            groups.setdefault((slot, source_slot, holds[0], turn), []).append((source, target))
        moved = [
            (slot, lax.ppermute(slots[source_slot][hold][0], "blk", pairs), [p[1] for p in pairs])
            for (slot, source_slot, hold, _), pairs in sorted(groups.items())
        ]
        return moved, left

    def merged(candidates):
        if len(candidates) <= 2:
            return candidates
        array, held_at = candidates[0][0], list(candidates[0][1])
        for other, places in candidates[1:]:
            here = functools.reduce(jnp.logical_or, [place == spot for spot in places])
            array = jnp.where(here, other, array)
            held_at += places
        return [(array, held_at)]

    own_centroids = lax.dynamic_slice_in_dim(centroids, core * half, half, 0)
    own_mix = lax.dynamic_slice_in_dim(log_mix, core * half, half, 0)
    units = to_unit(own_centroids)
    offsets = jnp.broadcast_to(((own_mix - concentration) * LOG2E)[:, None], (half, LANES))

    n_columns = n_places * CORES
    carried = None

    def scores_of(slot, carried):
        blocks = [order[slot] for order in orders]
        swapped = [(swap_cores(array, places), places) for array, places in slots[slot]]
        for who, candidates in enumerate((slots[slot], swapped)):
            choice = [
                next(n for n, (_, places) in enumerate(candidates) if spot in places)
                for spot in range(n_places)
            ]
            carried = score_block(
                ids,
                [array for array, _ in candidates],
                choice,
                blocks,
                who,
                units,
                offsets,
                carried,
                slot * CORES + who,
                n_columns,
            )
        return carried

    def totals_of(own):
        both = own + exchange(own, 1)
        return [both] + [
            lax.ppermute(both, "blk", [(i, (i + turn) % n_places) for i in range(n_places)])
            for turn in range(1, n_places)
        ]

    settled = {
        block for block in range(n_places) if all(order[-1] != block for order in orders)
    }
    early_totals = None
    for turn in range(n_places):
        while sum(len(places) for _, places in slots[turn]) < n_places:
            moved, moves = start_ready(moves)
            for slot, array, places in moved:
                slots[slot].append((array, places))
        slots[turn] = merged(slots[turn])
        moved, moves = start_ready(moves)
        carried = scores_of(turn, carried)
        if turn == n_places - 2 and settled:
            early_totals = totals_of(carried[2])
            early_totals, carried = lax.optimization_barrier((early_totals, carried))
        if moved:
            arrays, carried = lax.optimization_barrier(([array for _, array, _ in moved], carried))
            for (slot, _, places), array in zip(moved, arrays):
                slots[slot].append((array, places))
    scores, rows, totals = carried
    steps = sum_plan(orders)
    late = totals_of(totals)
    if early_totals is not None:
        ready = [step for step in steps if all(block in settled for block in step[1])]
        rest = [step for step in steps if step not in ready]
        state = sum_rows(ids, ready, early_totals, scores, rows, n_owners, None, False)
        late, state = lax.optimization_barrier((late, state))
    else:
        rest, state = steps, None
    *sent, mine, masses = sum_rows(ids, rest, late, scores, rows, n_owners, state, True)
    size = mine.shape[0]
    one, two = CORES, 2 * CORES
    if n_owners == 4:
        across, along, corner = sent[0:2], sent[2:4], sent[4:6]
        passing = exchange(corner[0], one), exchange(corner[1], two)
        arrived = [exchange(across[0], one), exchange(along[1], two)]
        arrived.append(exchange(pass_on(along[0], passing[0], False, size), two))
        arrived.append(exchange(pass_on(across[1], passing[1], True, size), one))
    else:
        arrived = [
            exchange(array, CORES * (1 + number // 2)) for number, array in enumerate(sent)
        ]
    payload = combine(mine, masses, arrived)

    count = local_centroids * n_places
    factor = count / (held * n_rows * n_places)
    if n_owners == 4:
        first = exchange(payload[0], one), exchange(payload[1], two)
        second = exchange(payload[1], one), exchange(payload[0], two)
        third = exchange(first[0], two), exchange(first[1], one)
        far = [(1, (first[0], second[0])), (2, (second[1], first[1])), (3, third)]
    else:
        far = [
            (away, tuple(exchange(array, CORES * away) for array in payload))
            for away in range(1, n_owners)
        ]
    swap = lambda halves: tuple(exchange(array, 1) for array in halves)
    done = assemble(ids, [(0, 0, payload), (1, 0, swap(payload))], None, n_rows, factor)
    swapped = [swap(halves) for _, halves in far[:-1]]
    arrays, swapped, done = lax.optimization_barrier(
        ([halves for _, halves in far], swapped, done)
    )
    swapped.append(swap(arrays[-1]))
    placed = [(0, away, halves) for (away, _), halves in zip(far, arrays)]
    placed += [(1, away, halves) for (away, _), halves in zip(far, swapped)]
    last = [piece for piece in placed if piece[1] == n_owners - 1]
    early = [piece for piece in placed if piece[1] != n_owners - 1]
    done = assemble(ids, early, done, n_rows, factor)
    done = assemble(ids, last, done, n_rows, factor)
    result, weights = done
    return (result, weights.reshape(local_centroids))


def solution(mesh):
    return jax.shard_map(
        local,
        mesh=mesh,
        in_specs=(P(("blk", "rows"), None), P("blk", None), P("blk")),
        out_specs=(P("blk", None), P("blk")),
        check_vma=False,
    )
```

```python
import functools
import math

import jax
import jax.numpy as jnp
from jax import lax
from jax.experimental import pallas as pl
from jax.experimental.pallas import tpu as pltpu
from jax.sharding import PartitionSpec as P

concentration = 32.0
LOG2E = math.log2(math.e)
LANES = 128
CORES = 2
EXTRA = 16
VMEM_LIMIT = 48 * 1024 * 1024


def to_unit(values):
    values = values.astype(jnp.float32)
    return (values * lax.rsqrt(jnp.sum(values * values, axis=-1, keepdims=True) + 1e-06)).astype(
        jnp.bfloat16
    )


def arrival_plan(n):
    orders = []
    for place in range(n):
        first = 1 if place < n // 2 else -1
        if 0 < place < n - 1:
            first = -first
        order = [place]
        for step in range(1, n):
            for way in (first, -first):
                if 0 <= place + way * step < n:
                    order.append(place + way * step)
        orders.append(order)
    moves = []
    for place in range(n):
        for slot in range(1, n):
            block = orders[place][slot]
            source = place + (1 if block > place else -1)
            moves.append((source, place, orders[source].index(block), slot))
    return orders, moves


def pick(index, values):
    result = jnp.int32(values[0])
    for number in range(1, len(values)):
        if values[number] != values[0]:
            result = jnp.where(index == number, jnp.int32(values[number]), result)
    return result


def score_kernel(n_sources, choice, ids, *refs):
    sources = refs[:n_sources]
    units_in, log_mix = refs[n_sources], refs[n_sources + 1]
    scores, rows_out, totals, raw, units, sem = refs[-6:]

    @pl.when(pl.program_id(0) == 0)
    def _():
        chosen = pick(ids[0], choice)
        for number, source in enumerate(sources):

            @pl.when(chosen == number)
            def _():
                pltpu.make_async_copy(source, raw, sem).start()

        pltpu.make_async_copy(sources[0], raw, sem).wait()
        values = raw[...].astype(jnp.float32)
        square = jnp.sum(values * values, axis=-1, keepdims=True)
        unit = (values * lax.rsqrt(square + 1e-06)).astype(jnp.bfloat16)
        units[...] = unit
        rows_out[...] = unit
        totals[...] = jnp.zeros_like(totals)

    cosines = lax.dot_general(
        units_in[...], units[...], (((1,), (1,)), ((), ())), preferred_element_type=jnp.float32
    )
    offset = log_mix[...]
    repeats = cosines.shape[1] // offset.shape[1]
    if repeats > 1:
        offset = jnp.concatenate([offset] * repeats, axis=1)
    value = jnp.exp2(cosines * (concentration * LOG2E) + offset)
    scores[...] = value
    totals[0] += jnp.sum(value, axis=0, keepdims=True)


def score_block(ids, sources, choice, blocks, who, units, offsets, carried, column, n_columns):
    part, depth = sources[0].shape
    count = units.shape[0]
    tile = math.gcd(count, 512)
    shapes = (
        jax.ShapeDtypeStruct((count, n_columns * part), jnp.float32),
        jax.ShapeDtypeStruct((n_columns * part, depth), jnp.bfloat16),
        jax.ShapeDtypeStruct((n_columns, 1, part), jnp.float32),
    )
    n_sources = len(sources)
    aliases = {}
    extra = ()
    if carried is not None:
        extra = carried
        aliases = {1 + n_sources + 2 + i: i for i in range(3)}
    anywhere = pl.BlockSpec(memory_space=pl.ANY)
    return pl.pallas_call(
        functools.partial(score_kernel, n_sources, choice),
        grid_spec=pltpu.PrefetchScalarGridSpec(
            num_scalar_prefetch=1,
            grid=(count // tile,),
            in_specs=[anywhere] * n_sources
            + [
                pl.BlockSpec((tile, depth), lambda t, s: (t, 0)),
                pl.BlockSpec((tile, offsets.shape[1]), lambda t, s: (t, 0)),
            ]
            + [anywhere] * len(extra),
            out_specs=[
                pl.BlockSpec((tile, part), lambda t, s: (t, column)),
                pl.BlockSpec((part, depth), lambda t, s: (column, 0)),
                pl.BlockSpec(
                    (1, 1, part),
                    lambda t, s: (pick(s[0], blocks) * CORES + ((s[1] % CORES) ^ who), 0, 0),
                ),
            ],
            scratch_shapes=[
                pltpu.VMEM((part, depth), jnp.bfloat16),
                pltpu.VMEM((part, depth), jnp.bfloat16),
                pltpu.SemaphoreType.DMA,
            ],
        ),
        out_shape=shapes,
        input_output_aliases=aliases,
        compiler_params=pltpu.CompilerParams(vmem_limit_bytes=VMEM_LIMIT),
        cost_estimate=pl.CostEstimate(
            flops=2 * count * part * depth,
            bytes_accessed=2 * (count * part * 4 + count * depth * 2),
            transcendentals=count * part,
        ),
        name="scores",
    )(ids, *sources, units, offsets, *extra)


def sum_plan(orders):
    n = len(orders)
    last = {order[-1] for order in orders}
    sorted_slots = []
    for order in orders:
        slots = list(range(n))
        sorted_slots.append(sorted(slots, key=lambda slot: (order[slot] in last, slot)))
    steps = []
    for turn in range(n):
        slots = [sorted_slots[place][turn] for place in range(n)]
        blocks = [orders[place][slot] for place, slot in enumerate(slots)]
        for who in range(CORES):
            steps.append(([slot * CORES + who for slot in slots], blocks, who))
    return steps


def three_rows(values, dtype, depth):
    size = values.shape[1]
    line = lax.broadcasted_iota(jnp.int32, (EXTRA, size), 0)
    high = values.astype(dtype).astype(jnp.float32)
    rest = values - high
    middle = rest.astype(dtype).astype(jnp.float32)
    low = rest - middle
    rows = jnp.where(
        line == 0, high, jnp.where(line == 1, middle, jnp.where(line == 2, low, 0.0))
    )
    if size < depth:
        rows = jnp.concatenate([rows, jnp.zeros((EXTRA, depth - size), jnp.float32)], axis=1)
    return rows.astype(dtype)


def one_row(rows, size):
    return jnp.sum(rows[:, :size].astype(jnp.float32), axis=0, keepdims=True)


def sum_kernel(plan, n_totals, n_owners, first, last, ids, *refs):
    totals = refs[:n_totals]
    scores, rows = refs[n_totals], refs[n_totals + 1]
    state = refs[n_totals + 2 : n_totals + 4]
    total, mass, inverse = refs[-3:]
    outs = refs[n_totals + (2 if first else 4) : -3]
    step = pl.program_id(0)

    @pl.when(step == 0)
    def _():
        for number, (_, blocks, who) in enumerate(plan):
            place = pick(ids[0], blocks) * CORES + ((ids[1] % CORES) ^ who)
            value = totals[0][place]
            for more in totals[1:]:
                value = value + more[place]
            inverse[number] = 1.0 / value
        if first:
            total[...] = jnp.zeros_like(total)
            mass[...] = jnp.zeros_like(mass)
        else:
            total[...] = state[0][...]
            mass[...] = state[1][...]

    resp = (scores[...] * inverse[step]).astype(jnp.bfloat16)
    total[...] += lax.dot_general(
        resp, rows[...], (((1,), (0,)), ((), ())), preferred_element_type=jnp.float32
    )
    wide = resp.astype(jnp.float32)
    partial = wide[:, :LANES]
    for start in range(LANES, wide.shape[1], LANES):
        partial = partial + wide[:, start : start + LANES]
    mass[...] += partial

    @pl.when(step == pl.num_programs(0) - 1)
    def _():
        if not last:
            outs[0][...] = total[...]
            outs[1][...] = mass[...]
            return
        sent = outs[:-2]
        mine, masses = outs[-2:]
        size, depth = mine.shape
        upper = size // 2
        quarter = ids[1] // CORES
        sums = jnp.sum(mass[...].T, axis=0, keepdims=True)
        for number in range(n_owners):
            block = total[number * size : (number + 1) * size, :]
            own = sums[:, number * size : (number + 1) * size]

            @pl.when(quarter == number)
            def _():
                mine[...] = block
                masses[...] = own

            for away in range(1, n_owners):

                @pl.when(quarter ^ number == away)
                def _():
                    first_half, second_half = sent[2 * away - 2 : 2 * away]
                    first_half[...] = block[:upper].astype(first_half.dtype)
                    second_half[: size - upper, :] = block[upper:].astype(second_half.dtype)
                    second_half[size - upper :, :] = three_rows(own, second_half.dtype, depth)


def sum_rows(ids, plan, totals, scores, rows, n_owners, carried, last):
    count = scores.shape[0]
    depth = rows.shape[1]
    size = count // n_owners
    part = totals[0].shape[2]
    first = carried is None
    column = lambda t, s: sum(
        jnp.where(t == n, pick(s[0], columns), 0) for n, (columns, _, _) in enumerate(plan)
    )
    fixed = lambda shape: pl.BlockSpec(shape, lambda t, s: (0,) * len(shape))
    in_specs = [fixed(totals[0].shape) for _ in totals] + [
        pl.BlockSpec((count, part), lambda t, s: (0, column(t, s))),
        pl.BlockSpec((part, depth), lambda t, s: (column(t, s), 0)),
    ]
    state = [(count, depth), (count, LANES)]
    if not first:
        in_specs += [fixed(shape) for shape in state]
    if last:
        shapes = []
        for away in range(1, n_owners):
            kept = [n_owners == 4 and keep == away for keep in (2, 1)]
            for keep, height in zip(kept, (size // 2, size - size // 2 + EXTRA)):
                shapes.append(((height, depth), jnp.float32 if keep else jnp.bfloat16))
        shapes += [((size, depth), jnp.float32), ((1, size), jnp.float32)]
    else:
        shapes = [(shape, jnp.float32) for shape in state]
    return pl.pallas_call(
        functools.partial(sum_kernel, plan, len(totals), n_owners, first, last),
        grid_spec=pltpu.PrefetchScalarGridSpec(
            num_scalar_prefetch=1,
            grid=(len(plan),),
            in_specs=in_specs,
            out_specs=[fixed(shape) for shape, _ in shapes],
            scratch_shapes=[
                pltpu.VMEM((count, depth), jnp.float32),
                pltpu.VMEM((count, LANES), jnp.float32),
                pltpu.VMEM((len(plan), 1, part), jnp.float32),
            ],
        ),
        out_shape=[jax.ShapeDtypeStruct(shape, dtype) for shape, dtype in shapes],
        compiler_params=pltpu.CompilerParams(vmem_limit_bytes=VMEM_LIMIT),
        cost_estimate=pl.CostEstimate(
            flops=2 * count * len(plan) * part * depth,
            bytes_accessed=len(plan) * part * (count * 4 + depth * 2) + count * depth * 4,
            transcendentals=0,
        ),
        name="sums",
    )(ids, *totals, scores, rows, *(carried or ()))


def pass_on_kernel(has_masses, size, mine, arrived, out):
    depth = mine.shape[1]
    height = mine.shape[0] - (EXTRA if has_masses else 0)
    total = mine[:height, :] + arrived[:height, :].astype(jnp.float32)
    out[:height, :] = total.astype(out.dtype)
    if has_masses:
        mass = one_row(mine[height:, :], size) + one_row(arrived[height:, :], size)
        out[height:, :] = three_rows(mass, out.dtype, depth)


def pass_on(mine, arrived, has_masses, size):
    return pl.pallas_call(
        functools.partial(pass_on_kernel, has_masses, size),
        out_shape=jax.ShapeDtypeStruct(arrived.shape, arrived.dtype),
        compiler_params=pltpu.CompilerParams(vmem_limit_bytes=VMEM_LIMIT),
        name="pass_on",
    )(mine, arrived)


def combine_kernel(mine, masses, *refs):
    first_out, second_out = refs[-2:]
    size, depth = mine.shape
    upper = size // 2
    first = mine[:upper, :]
    second = mine[upper:, :]
    mass = masses[...]
    for ref in refs[:-2]:
        if ref.shape[0] == upper:
            first = first + ref[...].astype(jnp.float32)
        else:
            second = second + ref[: size - upper, :].astype(jnp.float32)
            mass = mass + one_row(ref[size - upper :, :], size)
    for total, out in ((first, first_out), (second, second_out)):
        square = jnp.sum(total * total, axis=1, keepdims=True)
        out[: total.shape[0], :] = (total * lax.rsqrt(square + 1e-06)).astype(out.dtype)
    second_out[size - upper :, :] = three_rows(mass, second_out.dtype, depth)


def combine(mine, masses, arrived):
    size, depth = mine.shape
    upper = size // 2
    return pl.pallas_call(
        combine_kernel,
        out_shape=[
            jax.ShapeDtypeStruct((upper, depth), jnp.bfloat16),
            jax.ShapeDtypeStruct((size - upper + EXTRA, depth), jnp.bfloat16),
        ],
        compiler_params=pltpu.CompilerParams(vmem_limit_bytes=VMEM_LIMIT),
        name="combine",
    )(mine, masses, *arrived)


def assemble_kernel(factor, n_pieces, ids, *refs):
    units, weights = refs[-2:]
    size = units.shape[0]
    upper = size // 2
    for number in range(n_pieces):

        @pl.when(pl.program_id(0) == number)
        def _():
            first, second = refs[2 * number : 2 * number + 2]
            units[:upper, :] = first[...].astype(jnp.float32)
            units[upper:, :] = second[: size - upper, :].astype(jnp.float32)
            weights[0] = one_row(second[size - upper :, :], size) * factor


def assemble(ids, pieces, carried, n_blocks, factor):
    arrays = [array for _, _, halves in pieces for array in halves]
    depth = arrays[0].shape[1]
    size = arrays[0].shape[0] + arrays[1].shape[0] - EXTRA
    half = n_blocks // CORES
    flips = [flip for flip, _, _ in pieces]
    aways = [away for _, away, _ in pieces]

    def block(t, s):
        return ((s[1] % CORES) ^ pick(t, flips)) * half + ((s[1] // CORES) ^ pick(t, aways))

    extra = carried or ()
    aliases = {1 + len(arrays) + n: n for n in range(len(extra))}
    return pl.pallas_call(
        functools.partial(assemble_kernel, factor, len(pieces)),
        grid_spec=pltpu.PrefetchScalarGridSpec(
            num_scalar_prefetch=1,
            grid=(len(pieces),),
            in_specs=[pl.BlockSpec(array.shape, lambda t, s: (0, 0)) for array in arrays]
            + [pl.BlockSpec(memory_space=pl.ANY) for _ in extra],
            out_specs=[
                pl.BlockSpec((size, depth), lambda t, s: (block(t, s), 0)),
                pl.BlockSpec((1, 1, size), lambda t, s: (block(t, s), 0, 0)),
            ],
        ),
        out_shape=[
            jax.ShapeDtypeStruct((n_blocks * size, depth), jnp.float32),
            jax.ShapeDtypeStruct((n_blocks, 1, size), jnp.float32),
        ],
        input_output_aliases=aliases,
        compiler_params=pltpu.CompilerParams(vmem_limit_bytes=VMEM_LIMIT),
        name="assemble",
    )(ids, *arrays, *extra)


def local(embeddings, centroids, log_mix):
    n_places = lax.axis_size("blk")
    n_rows = lax.axis_size("rows")
    n_owners = n_rows // CORES
    place = lax.axis_index("blk")
    me = lax.axis_index("rows")
    core = lax.rem(me, CORES)
    held, depth = embeddings.shape
    local_centroids = centroids.shape[0]
    half = local_centroids // CORES
    ids = jnp.stack([place, me]).astype(jnp.int32)
    orders, moves = arrival_plan(n_places)

    def exchange(array, distance):
        return lax.ppermute(array, "rows", [(i, i ^ distance) for i in range(n_rows)])

    def swap_cores(array, places):
        pairs = [
            (spot * n_rows + i, spot * n_rows + (i ^ 1)) for spot in places for i in range(n_rows)
        ]
        return lax.ppermute(array, ("blk", "rows"), pairs)

    slots = [[(embeddings, list(range(n_places)))]] + [[] for _ in range(n_places - 1)]

    def start_ready(moves):
        groups = {}
        left = []
        for move in moves:
            source, target, source_slot, slot = move
            holds = [n for n, (_, places) in enumerate(slots[source_slot]) if source in places]
            if not holds:
                left.append(move)
                continue
            turn = 0
            while any(source == s for s, _ in groups.get((slot, source_slot, holds[0], turn), [])):
                turn += 1
            groups.setdefault((slot, source_slot, holds[0], turn), []).append((source, target))
        moved = [
            (slot, lax.ppermute(slots[source_slot][hold][0], "blk", pairs), [p[1] for p in pairs])
            for (slot, source_slot, hold, _), pairs in sorted(groups.items())
        ]
        return moved, left

    def merged(candidates):
        if len(candidates) <= 2:
            return candidates
        array, held_at = candidates[0][0], list(candidates[0][1])
        for other, places in candidates[1:]:
            here = functools.reduce(jnp.logical_or, [place == spot for spot in places])
            array = jnp.where(here, other, array)
            held_at += places
        return [(array, held_at)]

    own_centroids = lax.dynamic_slice_in_dim(centroids, core * half, half, 0)
    own_mix = lax.dynamic_slice_in_dim(log_mix, core * half, half, 0)
    units = to_unit(own_centroids)
    offsets = jnp.broadcast_to(((own_mix - concentration) * LOG2E)[:, None], (half, LANES))

    n_columns = n_places * CORES
    carried = None

    def scores_of(slot, carried):
        blocks = [order[slot] for order in orders]
        swapped = [(swap_cores(array, places), places) for array, places in slots[slot]]
        for who, candidates in enumerate((slots[slot], swapped)):
            choice = [
                next(n for n, (_, places) in enumerate(candidates) if spot in places)
                for spot in range(n_places)
            ]
            carried = score_block(
                ids,
                [array for array, _ in candidates],
                choice,
                blocks,
                who,
                units,
                offsets,
                carried,
                slot * CORES + who,
                n_columns,
            )
        return carried

    def totals_of(own):
        both = own + exchange(own, 1)
        return [both] + [
            lax.ppermute(both, "blk", [(i, (i + turn) % n_places) for i in range(n_places)])
            for turn in range(1, n_places)
        ]

    settled = {
        block for block in range(n_places) if all(order[-1] != block for order in orders)
    }
    early_totals = None
    def arrive(moved):
        for slot, array, places in moved:
            slots[slot].append((array, places))

    def arrive_behind(moved, carried):
        if moved:
            arrays, carried = lax.optimization_barrier(([array for _, array, _ in moved], carried))
            arrive([(slot, array, places) for (slot, _, places), array in zip(moved, arrays)])
        return carried

    for turn in range(n_places):
        while sum(len(places) for _, places in slots[turn]) < n_places:
            moved, moves = start_ready(moves)
            arrive(moved)
        slots[turn] = merged(slots[turn])
        moved, moves = start_ready(moves)

        carried = scores_of(turn, carried)
        if turn == n_places - 2 and settled:
            early_totals = totals_of(carried[2])
            early_totals, carried = lax.optimization_barrier((early_totals, carried))
        if turn == 0:
            arrive([m for m in moved if m[0] > turn + 1])
            moved = [m for m in moved if m[0] <= turn + 1]
        carried = arrive_behind(moved, carried)
    scores, rows, totals = carried
    steps = sum_plan(orders)
    late = totals_of(totals)
    if early_totals is not None:
        ready = [step for step in steps if all(block in settled for block in step[1])]
        rest = [step for step in steps if step not in ready]
        state = sum_rows(ids, ready, early_totals, scores, rows, n_owners, None, False)
        late, state = lax.optimization_barrier((late, state))
    else:
        rest, state = steps, None
    *sent, mine, masses = sum_rows(ids, rest, late, scores, rows, n_owners, state, True)
    size = mine.shape[0]
    one, two = CORES, 2 * CORES
    if n_owners == 4:
        across, along, corner = sent[0:2], sent[2:4], sent[4:6]
        passing = exchange(corner[0], one), exchange(corner[1], two)
        arrived = [exchange(across[0], one), exchange(along[1], two)]
        arrived.append(exchange(pass_on(along[0], passing[0], False, size), two))
        arrived.append(exchange(pass_on(across[1], passing[1], True, size), one))
    else:
        arrived = [
            exchange(array, CORES * (1 + number // 2)) for number, array in enumerate(sent)
        ]
    payload = combine(mine, masses, arrived)

    count = local_centroids * n_places
    factor = count / (held * n_rows * n_places)
    if n_owners == 4:
        first = exchange(payload[0], one), exchange(payload[1], two)
        second = exchange(payload[1], one), exchange(payload[0], two)
        third = exchange(first[0], two), exchange(first[1], one)
        far = [(1, (first[0], second[0])), (2, (second[1], first[1])), (3, third)]
    else:
        far = [
            (away, tuple(exchange(array, CORES * away) for array in payload))
            for away in range(1, n_owners)
        ]
    swap = lambda halves: tuple(exchange(array, 1) for array in halves)
    done = assemble(ids, [(0, 0, payload), (1, 0, swap(payload))], None, n_rows, factor)
    swapped = [swap(halves) for _, halves in far[:-1]]
    arrays, swapped, done = lax.optimization_barrier(
        ([halves for _, halves in far], swapped, done)
    )
    swapped.append(swap(arrays[-1]))
    placed = [(0, away, halves) for (away, _), halves in zip(far, arrays)]
    placed += [(1, away, halves) for (away, _), halves in zip(far, swapped)]
    last = [piece for piece in placed if piece[1] == n_owners - 1]
    early = [piece for piece in placed if piece[1] != n_owners - 1]
    done = assemble(ids, early, done, n_rows, factor)
    done = assemble(ids, last, done, n_rows, factor)
    result, weights = done
    return (result, weights.reshape(local_centroids))


def solution(mesh):
    return jax.shard_map(
        local,
        mesh=mesh,
        in_specs=(P(("blk", "rows"), None), P("blk", None), P("blk")),
        out_specs=(P("blk", None), P("blk")),
        check_vma=False,
    )
```

```python
import functools
import math

import jax
import jax.numpy as jnp
from jax import lax
from jax.experimental import pallas as pl
from jax.experimental.pallas import tpu as pltpu
from jax.sharding import PartitionSpec as P

concentration = 32.0
LOG2E = math.log2(math.e)
LANES = 128
CORES = 2
EXTRA = 16
VMEM_LIMIT = 20 * 1024 * 1024


def to_unit(values):
    values = values.astype(jnp.float32)
    return (values * lax.rsqrt(jnp.sum(values * values, axis=-1, keepdims=True) + 1e-06)).astype(
        jnp.bfloat16
    )


def arrival_plan(n):
    orders = []
    for place in range(n):
        first = 1 if place < n // 2 else -1
        if 0 < place < n - 1:
            first = -first
        order = [place]
        for step in range(1, n):
            for way in (first, -first):
                if 0 <= place + way * step < n:
                    order.append(place + way * step)
        orders.append(order)
    moves = []
    for place in range(n):
        for slot in range(1, n):
            block = orders[place][slot]
            source = place + (1 if block > place else -1)
            moves.append((source, place, orders[source].index(block), slot))
    return orders, moves


def pick(index, values):
    result = jnp.int32(values[0])
    for number in range(1, len(values)):
        if values[number] != values[0]:
            result = jnp.where(index == number, jnp.int32(values[number]), result)
    return result


def score_kernel(n_sources, choice, ids, *refs):
    sources = refs[:n_sources]
    units_in, log_mix = refs[n_sources], refs[n_sources + 1]
    scores, rows_out, totals, raw, units, sem = refs[-6:]

    @pl.when(pl.program_id(0) == 0)
    def _():
        chosen = pick(ids[0], choice)
        for number, source in enumerate(sources):

            @pl.when(chosen == number)
            def _():
                pltpu.make_async_copy(source, raw, sem).start()

        pltpu.make_async_copy(sources[0], raw, sem).wait()
        values = raw[...].astype(jnp.float32)
        square = jnp.sum(values * values, axis=-1, keepdims=True)
        unit = (values * lax.rsqrt(square + 1e-06)).astype(jnp.bfloat16)
        units[...] = unit
        rows_out[...] = unit
        totals[...] = jnp.zeros_like(totals)

    cosines = lax.dot_general(
        units_in[...], units[...], (((1,), (1,)), ((), ())), preferred_element_type=jnp.float32
    )
    offset = log_mix[...]
    repeats = cosines.shape[1] // offset.shape[1]
    if repeats > 1:
        offset = jnp.concatenate([offset] * repeats, axis=1)
    value = jnp.exp2(cosines * (concentration * LOG2E) + offset)
    scores[0] = value
    totals[0] += jnp.sum(value, axis=0, keepdims=True)


def score_block(ids, sources, choice, blocks, who, units, offsets, carried, column, n_columns):
    part, depth = sources[0].shape
    count = units.shape[0]
    tile = math.gcd(count, 512)
    shapes = (
        jax.ShapeDtypeStruct((n_columns, count, part), jnp.float32),
        jax.ShapeDtypeStruct((n_columns * part, depth), jnp.bfloat16),
        jax.ShapeDtypeStruct((n_columns, 1, part), jnp.float32),
    )
    n_sources = len(sources)
    aliases = {}
    extra = ()
    if carried is not None:
        extra = carried
        aliases = {1 + n_sources + 2 + i: i for i in range(3)}
    anywhere = pl.BlockSpec(memory_space=pl.ANY)
    return pl.pallas_call(
        functools.partial(score_kernel, n_sources, choice),
        grid_spec=pltpu.PrefetchScalarGridSpec(
            num_scalar_prefetch=1,
            grid=(count // tile,),
            in_specs=[anywhere] * n_sources
            + [
                pl.BlockSpec((tile, depth), lambda t, s: (t, 0)),
                pl.BlockSpec((tile, offsets.shape[1]), lambda t, s: (t, 0)),
            ]
            + [anywhere] * len(extra),
            out_specs=[
                pl.BlockSpec((1, tile, part), lambda t, s: (column, t, 0)),
                pl.BlockSpec((part, depth), lambda t, s: (column, 0)),
                pl.BlockSpec(
                    (1, 1, part),
                    lambda t, s: (pick(s[0], blocks) * CORES + ((s[1] % CORES) ^ who), 0, 0),
                ),
            ],
            scratch_shapes=[
                pltpu.VMEM((part, depth), jnp.bfloat16),
                pltpu.VMEM((part, depth), jnp.bfloat16),
                pltpu.SemaphoreType.DMA,
            ],
        ),
        out_shape=shapes,
        input_output_aliases=aliases,
        compiler_params=pltpu.CompilerParams(vmem_limit_bytes=VMEM_LIMIT),
        cost_estimate=pl.CostEstimate(
            flops=2 * count * part * depth,
            bytes_accessed=2 * (count * part * 4 + count * depth * 2),
            transcendentals=count * part,
        ),
        name="scores",
    )(ids, *sources, units, offsets, *extra)


def sum_plan(orders):
    n = len(orders)
    last = {order[-1] for order in orders}
    sorted_slots = []
    for order in orders:
        slots = list(range(n))
        sorted_slots.append(sorted(slots, key=lambda slot: (order[slot] in last, slot)))
    steps = []
    for turn in range(n):
        slots = [sorted_slots[place][turn] for place in range(n)]
        blocks = [orders[place][slot] for place, slot in enumerate(slots)]
        for who in range(CORES):
            steps.append(([slot * CORES + who for slot in slots], blocks, who))
    return steps


def three_rows(values, dtype, depth):
    size = values.shape[1]
    line = lax.broadcasted_iota(jnp.int32, (EXTRA, size), 0)
    high = values.astype(dtype).astype(jnp.float32)
    rest = values - high
    middle = rest.astype(dtype).astype(jnp.float32)
    low = rest - middle
    rows = jnp.where(
        line == 0, high, jnp.where(line == 1, middle, jnp.where(line == 2, low, 0.0))
    )
    if size < depth:
        rows = jnp.concatenate([rows, jnp.zeros((EXTRA, depth - size), jnp.float32)], axis=1)
    return rows.astype(dtype)


def one_row(rows, size):
    return jnp.sum(rows[:, :size].astype(jnp.float32), axis=0, keepdims=True)


def sum_kernel(plan, n_totals, n_owners, first, last, ids, *refs):
    totals = refs[:n_totals]
    scores, rows = refs[n_totals], refs[n_totals + 1]
    state = refs[n_totals + 2 : n_totals + 4]
    total, mass, inverse = refs[-3:]
    outs = refs[n_totals + (2 if first else 4) : -3]
    step = pl.program_id(0)

    @pl.when(step == 0)
    def _():
        for number, (_, blocks, who) in enumerate(plan):
            place = pick(ids[0], blocks) * CORES + ((ids[1] % CORES) ^ who)
            value = totals[0][place]
            for more in totals[1:]:
                value = value + more[place]
            inverse[number] = 1.0 / value
        if first:
            total[...] = jnp.zeros_like(total)
            mass[...] = jnp.zeros_like(mass)
        else:
            total[...] = state[0][...]
            mass[...] = state[1][...]

    resp = (scores[0] * inverse[step]).astype(jnp.bfloat16)
    total[...] += lax.dot_general(
        resp, rows[...], (((1,), (0,)), ((), ())), preferred_element_type=jnp.float32
    )
    wide = resp.astype(jnp.float32)
    partial = wide[:, :LANES]
    for start in range(LANES, wide.shape[1], LANES):
        partial = partial + wide[:, start : start + LANES]
    mass[...] += partial

    @pl.when(step == pl.num_programs(0) - 1)
    def _():
        if not last:
            outs[0][...] = total[...]
            outs[1][...] = mass[...]
            return
        sent = outs[:-2]
        mine, masses = outs[-2:]
        size, depth = mine.shape
        upper = size // 2
        quarter = ids[1] // CORES
        sums = jnp.sum(mass[...].T, axis=0, keepdims=True)
        for number in range(n_owners):
            block = total[number * size : (number + 1) * size, :]
            own = sums[:, number * size : (number + 1) * size]

            @pl.when(quarter == number)
            def _():
                mine[...] = block
                masses[...] = own

            for away in range(1, n_owners):

                @pl.when(quarter ^ number == away)
                def _():
                    first_half, second_half = sent[2 * away - 2 : 2 * away]
                    first_half[...] = block[:upper].astype(first_half.dtype)
                    second_half[: size - upper, :] = block[upper:].astype(second_half.dtype)
                    second_half[size - upper :, :] = three_rows(own, second_half.dtype, depth)


def sum_rows(ids, plan, totals, scores, rows, n_owners, carried, last):
    count = scores.shape[1]
    depth = rows.shape[1]
    size = count // n_owners
    part = totals[0].shape[2]
    first = carried is None
    column = lambda t, s: sum(
        jnp.where(t == n, pick(s[0], columns), 0) for n, (columns, _, _) in enumerate(plan)
    )
    fixed = lambda shape: pl.BlockSpec(shape, lambda t, s: (0,) * len(shape))
    in_specs = [fixed(totals[0].shape) for _ in totals] + [
        pl.BlockSpec((1, count, part), lambda t, s: (column(t, s), 0, 0)),
        pl.BlockSpec((part, depth), lambda t, s: (column(t, s), 0)),
    ]
    state = [(count, depth), (count, LANES)]
    if not first:
        in_specs += [fixed(shape) for shape in state]
    if last:
        shapes = []
        for away in range(1, n_owners):
            kept = [n_owners == 4 and keep == away for keep in (2, 1)]
            for keep, height in zip(kept, (size // 2, size - size // 2 + EXTRA)):
                shapes.append(((height, depth), jnp.float32 if keep else jnp.bfloat16))
        shapes += [((size, depth), jnp.float32), ((1, size), jnp.float32)]
    else:
        shapes = [(shape, jnp.float32) for shape in state]
    return pl.pallas_call(
        functools.partial(sum_kernel, plan, len(totals), n_owners, first, last),
        grid_spec=pltpu.PrefetchScalarGridSpec(
            num_scalar_prefetch=1,
            grid=(len(plan),),
            in_specs=in_specs,
            out_specs=[fixed(shape) for shape, _ in shapes],
            scratch_shapes=[
                pltpu.VMEM((count, depth), jnp.float32),
                pltpu.VMEM((count, LANES), jnp.float32),
                pltpu.VMEM((len(plan), 1, part), jnp.float32),
            ],
        ),
        out_shape=[jax.ShapeDtypeStruct(shape, dtype) for shape, dtype in shapes],
        compiler_params=pltpu.CompilerParams(vmem_limit_bytes=VMEM_LIMIT),
        cost_estimate=pl.CostEstimate(
            flops=2 * count * len(plan) * part * depth,
            bytes_accessed=len(plan) * part * (count * 4 + depth * 2) + count * depth * 4,
            transcendentals=0,
        ),
        name="sums",
    )(ids, *totals, scores, rows, *(carried or ()))


def pass_on_kernel(has_masses, size, mine, arrived, out):
    depth = mine.shape[1]
    height = mine.shape[0] - (EXTRA if has_masses else 0)
    total = mine[:height, :] + arrived[:height, :].astype(jnp.float32)
    out[:height, :] = total.astype(out.dtype)
    if has_masses:
        mass = one_row(mine[height:, :], size) + one_row(arrived[height:, :], size)
        out[height:, :] = three_rows(mass, out.dtype, depth)


def pass_on(mine, arrived, has_masses, size):
    return pl.pallas_call(
        functools.partial(pass_on_kernel, has_masses, size),
        out_shape=jax.ShapeDtypeStruct(arrived.shape, arrived.dtype),
        compiler_params=pltpu.CompilerParams(vmem_limit_bytes=VMEM_LIMIT),
        name="pass_on",
    )(mine, arrived)


def combine_kernel(mine, masses, *refs):
    first_out, second_out = refs[-2:]
    size, depth = mine.shape
    upper = size // 2
    first = mine[:upper, :]
    second = mine[upper:, :]
    mass = masses[...]
    for ref in refs[:-2]:
        if ref.shape[0] == upper:
            first = first + ref[...].astype(jnp.float32)
        else:
            second = second + ref[: size - upper, :].astype(jnp.float32)
            mass = mass + one_row(ref[size - upper :, :], size)
    for total, out in ((first, first_out), (second, second_out)):
        square = jnp.sum(total * total, axis=1, keepdims=True)
        out[: total.shape[0], :] = (total * lax.rsqrt(square + 1e-06)).astype(out.dtype)
    second_out[size - upper :, :] = three_rows(mass, second_out.dtype, depth)


def combine(mine, masses, arrived):
    size, depth = mine.shape
    upper = size // 2
    return pl.pallas_call(
        combine_kernel,
        out_shape=[
            jax.ShapeDtypeStruct((upper, depth), jnp.bfloat16),
            jax.ShapeDtypeStruct((size - upper + EXTRA, depth), jnp.bfloat16),
        ],
        compiler_params=pltpu.CompilerParams(vmem_limit_bytes=VMEM_LIMIT),
        name="combine",
    )(mine, masses, *arrived)


def assemble_kernel(factor, n_pieces, ids, *refs):
    units, weights = refs[-2:]
    size = units.shape[0]
    upper = size // 2
    for number in range(n_pieces):

        @pl.when(pl.program_id(0) == number)
        def _():
            first, second = refs[2 * number : 2 * number + 2]
            units[:upper, :] = first[...].astype(jnp.float32)
            units[upper:, :] = second[: size - upper, :].astype(jnp.float32)
            weights[0] = one_row(second[size - upper :, :], size) * factor


def assemble(ids, pieces, carried, n_blocks, factor):
    arrays = [array for _, _, halves in pieces for array in halves]
    depth = arrays[0].shape[1]
    size = arrays[0].shape[0] + arrays[1].shape[0] - EXTRA
    half = n_blocks // CORES
    flips = [flip for flip, _, _ in pieces]
    aways = [away for _, away, _ in pieces]

    def block(t, s):
        return ((s[1] % CORES) ^ pick(t, flips)) * half + ((s[1] // CORES) ^ pick(t, aways))

    extra = carried or ()
    aliases = {1 + len(arrays) + n: n for n in range(len(extra))}
    return pl.pallas_call(
        functools.partial(assemble_kernel, factor, len(pieces)),
        grid_spec=pltpu.PrefetchScalarGridSpec(
            num_scalar_prefetch=1,
            grid=(len(pieces),),
            in_specs=[pl.BlockSpec(array.shape, lambda t, s: (0, 0)) for array in arrays]
            + [pl.BlockSpec(memory_space=pl.ANY) for _ in extra],
            out_specs=[
                pl.BlockSpec((size, depth), lambda t, s: (block(t, s), 0)),
                pl.BlockSpec((1, 1, size), lambda t, s: (block(t, s), 0, 0)),
            ],
        ),
        out_shape=[
            jax.ShapeDtypeStruct((n_blocks * size, depth), jnp.float32),
            jax.ShapeDtypeStruct((n_blocks, 1, size), jnp.float32),
        ],
        input_output_aliases=aliases,
        compiler_params=pltpu.CompilerParams(vmem_limit_bytes=VMEM_LIMIT),
        name="assemble",
    )(ids, *arrays, *extra)


def local(embeddings, centroids, log_mix):
    n_places = lax.axis_size("blk")
    n_rows = lax.axis_size("rows")
    n_owners = n_rows // CORES
    place = lax.axis_index("blk")
    me = lax.axis_index("rows")
    core = lax.rem(me, CORES)
    held, depth = embeddings.shape
    local_centroids = centroids.shape[0]
    half = local_centroids // CORES
    ids = jnp.stack([place, me]).astype(jnp.int32)
    orders, moves = arrival_plan(n_places)

    def exchange(array, distance):
        return lax.ppermute(array, "rows", [(i, i ^ distance) for i in range(n_rows)])

    def swap_cores(array, places):
        pairs = [
            (spot * n_rows + i, spot * n_rows + (i ^ 1)) for spot in places for i in range(n_rows)
        ]
        return lax.ppermute(array, ("blk", "rows"), pairs)

    slots = [[(embeddings, list(range(n_places)))]] + [[] for _ in range(n_places - 1)]

    def start_ready(moves):
        groups = {}
        left = []
        for move in moves:
            source, target, source_slot, slot = move
            holds = [n for n, (_, places) in enumerate(slots[source_slot]) if source in places]
            if not holds:
                left.append(move)
                continue
            turn = 0
            while any(source == s for s, _ in groups.get((slot, source_slot, holds[0], turn), [])):
                turn += 1
            groups.setdefault((slot, source_slot, holds[0], turn), []).append((source, target))
        moved = [
            (slot, lax.ppermute(slots[source_slot][hold][0], "blk", pairs), [p[1] for p in pairs])
            for (slot, source_slot, hold, _), pairs in sorted(groups.items())
        ]
        return moved, left

    def merged(candidates):
        if len(candidates) <= 2:
            return candidates
        array, held_at = candidates[0][0], list(candidates[0][1])
        for other, places in candidates[1:]:
            here = functools.reduce(jnp.logical_or, [place == spot for spot in places])
            array = jnp.where(here, other, array)
            held_at += places
        return [(array, held_at)]

    own_centroids = lax.dynamic_slice_in_dim(centroids, core * half, half, 0)
    own_mix = lax.dynamic_slice_in_dim(log_mix, core * half, half, 0)
    units = to_unit(own_centroids)
    offsets = jnp.broadcast_to(((own_mix - concentration) * LOG2E)[:, None], (half, LANES))

    n_columns = n_places * CORES
    carried = None

    def scores_of(slot, carried):
        blocks = [order[slot] for order in orders]
        swapped = [(swap_cores(array, places), places) for array, places in slots[slot]]
        for who, candidates in enumerate((slots[slot], swapped)):
            choice = [
                next(n for n, (_, places) in enumerate(candidates) if spot in places)
                for spot in range(n_places)
            ]
            carried = score_block(
                ids,
                [array for array, _ in candidates],
                choice,
                blocks,
                who,
                units,
                offsets,
                carried,
                slot * CORES + who,
                n_columns,
            )
        return carried

    def totals_of(own):
        both = own + exchange(own, 1)
        return [both] + [
            lax.ppermute(both, "blk", [(i, (i + turn) % n_places) for i in range(n_places)])
            for turn in range(1, n_places)
        ]

    settled = {
        block for block in range(n_places) if all(order[-1] != block for order in orders)
    }
    early_totals = None
    def arrive(moved):
        for slot, array, places in moved:
            slots[slot].append((array, places))

    def arrive_behind(moved, carried):
        if moved:
            arrays, carried = lax.optimization_barrier(([array for _, array, _ in moved], carried))
            arrive([(slot, array, places) for (slot, _, places), array in zip(moved, arrays)])
        return carried

    for turn in range(n_places):
        while sum(len(places) for _, places in slots[turn]) < n_places:
            moved, moves = start_ready(moves)
            arrive(moved)
        slots[turn] = merged(slots[turn])
        moved, moves = start_ready(moves)

        carried = scores_of(turn, carried)
        if turn == n_places - 2 and settled:
            early_totals = totals_of(carried[2])
            early_totals, carried = lax.optimization_barrier((early_totals, carried))
        if turn == 0:
            arrive([m for m in moved if m[0] > turn + 1])
            moved = [m for m in moved if m[0] <= turn + 1]
        carried = arrive_behind(moved, carried)
    scores, rows, totals = carried
    steps = sum_plan(orders)
    late = totals_of(totals)
    if early_totals is not None:
        ready = [step for step in steps if all(block in settled for block in step[1])]
        rest = [step for step in steps if step not in ready]
        state = sum_rows(ids, ready, early_totals, scores, rows, n_owners, None, False)
        late, state = lax.optimization_barrier((late, state))
    else:
        rest, state = steps, None
    *sent, mine, masses = sum_rows(ids, rest, late, scores, rows, n_owners, state, True)
    size = mine.shape[0]
    one, two = CORES, 2 * CORES
    if n_owners == 4:
        across, along, corner = sent[0:2], sent[2:4], sent[4:6]
        passing = exchange(corner[0], one), exchange(corner[1], two)
        arrived = [exchange(across[0], one), exchange(along[1], two)]
        arrived.append(exchange(pass_on(along[0], passing[0], False, size), two))
        arrived.append(exchange(pass_on(across[1], passing[1], True, size), one))
    else:
        arrived = [
            exchange(array, CORES * (1 + number // 2)) for number, array in enumerate(sent)
        ]
    payload = combine(mine, masses, arrived)

    count = local_centroids * n_places
    factor = count / (held * n_rows * n_places)
    if n_owners == 4:
        first = exchange(payload[0], one), exchange(payload[1], two)
        second = exchange(payload[1], one), exchange(payload[0], two)
        third = exchange(first[0], two), exchange(first[1], one)
        far = [(1, (first[0], second[0])), (2, (second[1], first[1])), (3, third)]
    else:
        far = [
            (away, tuple(exchange(array, CORES * away) for array in payload))
            for away in range(1, n_owners)
        ]
    swap = lambda halves: tuple(exchange(array, 1) for array in halves)
    done = assemble(ids, [(0, 0, payload), (1, 0, swap(payload))], None, n_rows, factor)
    swapped = [swap(halves) for _, halves in far[:-1]]
    arrays, swapped, done = lax.optimization_barrier(
        ([halves for _, halves in far], swapped, done)
    )
    swapped.append(swap(arrays[-1]))
    placed = [(0, away, halves) for (away, _), halves in zip(far, arrays)]
    placed += [(1, away, halves) for (away, _), halves in zip(far, swapped)]
    last = [piece for piece in placed if piece[1] == n_owners - 1]
    early = [piece for piece in placed if piece[1] != n_owners - 1]
    done = assemble(ids, early, done, n_rows, factor)
    done = assemble(ids, last, done, n_rows, factor)
    result, weights = done
    return (result, weights.reshape(local_centroids))


def solution(mesh):
    return jax.shard_map(
        local,
        mesh=mesh,
        in_specs=(P(("blk", "rows"), None), P("blk", None), P("blk")),
        out_specs=(P("blk", None), P("blk")),
        check_vma=False,
    )
```

```python
import functools
import math

import jax
import jax.numpy as jnp
from jax import lax
from jax.experimental import pallas as pl
from jax.experimental.pallas import tpu as pltpu
from jax.sharding import PartitionSpec as P

concentration = 32.0
LOG2E = math.log2(math.e)
LANES = 128
CORES = 2
EXTRA = 16
VMEM_LIMIT = 20 * 1024 * 1024


def to_unit(values):
    values = values.astype(jnp.float32)
    return (values * lax.rsqrt(jnp.sum(values * values, axis=-1, keepdims=True) + 1e-06)).astype(
        jnp.bfloat16
    )


def arrival_plan(n):
    orders = []
    for place in range(n):
        first = 1 if place < n // 2 else -1
        if 0 < place < n - 1:
            first = -first
        order = [place]
        for step in range(1, n):
            for way in (first, -first):
                if 0 <= place + way * step < n:
                    order.append(place + way * step)
        orders.append(order)
    moves = []
    for place in range(n):
        for slot in range(1, n):
            block = orders[place][slot]
            source = place + (1 if block > place else -1)
            moves.append((source, place, orders[source].index(block), slot))
    return orders, moves


def pick(index, values):
    result = jnp.int32(values[0])
    for number in range(1, len(values)):
        if values[number] != values[0]:
            result = jnp.where(index == number, jnp.int32(values[number]), result)
    return result


def score_kernel(n_sources, choice, ids, *refs):
    sources = refs[:n_sources]
    units_in, log_mix = refs[n_sources], refs[n_sources + 1]
    scores, rows_out, totals, raw, units, sem = refs[-6:]

    @pl.when(pl.program_id(0) == 0)
    def _():
        chosen = pick(ids[0], choice)
        for number, source in enumerate(sources):

            @pl.when(chosen == number)
            def _():
                pltpu.make_async_copy(source, raw, sem).start()

        pltpu.make_async_copy(sources[0], raw, sem).wait()
        values = raw[...].astype(jnp.float32)
        square = jnp.sum(values * values, axis=-1, keepdims=True)
        unit = (values * lax.rsqrt(square + 1e-06)).astype(jnp.bfloat16)
        units[...] = unit
        rows_out[...] = unit
        totals[...] = jnp.zeros_like(totals)

    cosines = lax.dot_general(
        units_in[...], units[...], (((1,), (1,)), ((), ())), preferred_element_type=jnp.float32
    )
    offset = log_mix[...]
    repeats = cosines.shape[1] // offset.shape[1]
    if repeats > 1:
        offset = jnp.concatenate([offset] * repeats, axis=1)
    value = jnp.exp2(cosines * (concentration * LOG2E) + offset)
    scores[0] = value
    totals[0] += jnp.sum(value, axis=0, keepdims=True)


def score_block(ids, sources, choice, blocks, who, units, offsets, carried, column, n_columns):
    part, depth = sources[0].shape
    count = units.shape[0]
    tile = math.gcd(count, 512)
    shapes = (
        jax.ShapeDtypeStruct((n_columns, count, part), jnp.float32),
        jax.ShapeDtypeStruct((n_columns * part, depth), jnp.bfloat16),
        jax.ShapeDtypeStruct((n_columns, 1, part), jnp.float32),
    )
    n_sources = len(sources)
    aliases = {}
    extra = ()
    if carried is not None:
        extra = carried
        aliases = {1 + n_sources + 2 + i: i for i in range(3)}
    anywhere = pl.BlockSpec(memory_space=pl.ANY)
    return pl.pallas_call(
        functools.partial(score_kernel, n_sources, choice),
        grid_spec=pltpu.PrefetchScalarGridSpec(
            num_scalar_prefetch=1,
            grid=(count // tile,),
            in_specs=[anywhere] * n_sources
            + [
                pl.BlockSpec((tile, depth), lambda t, s: (t, 0)),
                pl.BlockSpec((tile, offsets.shape[1]), lambda t, s: (t, 0)),
            ]
            + [anywhere] * len(extra),
            out_specs=[
                pl.BlockSpec((1, tile, part), lambda t, s: (column, t, 0)),
                pl.BlockSpec((part, depth), lambda t, s: (column, 0)),
                pl.BlockSpec(
                    (1, 1, part),
                    lambda t, s: (pick(s[0], blocks) * CORES + ((s[1] % CORES) ^ who), 0, 0),
                ),
            ],
            scratch_shapes=[
                pltpu.VMEM((part, depth), jnp.bfloat16),
                pltpu.VMEM((part, depth), jnp.bfloat16),
                pltpu.SemaphoreType.DMA,
            ],
        ),
        out_shape=shapes,
        input_output_aliases=aliases,
        compiler_params=pltpu.CompilerParams(vmem_limit_bytes=VMEM_LIMIT),
        cost_estimate=pl.CostEstimate(
            flops=2 * count * part * depth,
            bytes_accessed=2 * (count * part * 4 + count * depth * 2),
            transcendentals=count * part,
        ),
        name="scores",
    )(ids, *sources, units, offsets, *extra)


def sum_plan(orders):
    n = len(orders)
    last = {order[-1] for order in orders}
    sorted_slots = []
    for order in orders:
        slots = list(range(n))
        sorted_slots.append(sorted(slots, key=lambda slot: (order[slot] in last, slot)))
    steps = []
    for turn in range(n):
        slots = [sorted_slots[place][turn] for place in range(n)]
        blocks = [orders[place][slot] for place, slot in enumerate(slots)]
        for who in range(CORES):
            steps.append(([slot * CORES + who for slot in slots], blocks, who))
    return steps


def three_rows(values, dtype, depth):
    size = values.shape[1]
    line = lax.broadcasted_iota(jnp.int32, (EXTRA, size), 0)
    high = values.astype(dtype).astype(jnp.float32)
    rest = values - high
    middle = rest.astype(dtype).astype(jnp.float32)
    low = rest - middle
    rows = jnp.where(
        line == 0, high, jnp.where(line == 1, middle, jnp.where(line == 2, low, 0.0))
    )
    if size < depth:
        rows = jnp.concatenate([rows, jnp.zeros((EXTRA, depth - size), jnp.float32)], axis=1)
    return rows.astype(dtype)


def one_row(rows, size):
    return jnp.sum(rows[:, :size].astype(jnp.float32), axis=0, keepdims=True)


def sum_kernel(plan, n_totals, n_owners, first, last, ids, *refs):
    totals = refs[:n_totals]
    scores, rows = refs[n_totals], refs[n_totals + 1]
    state = refs[n_totals + 2 : n_totals + 4]
    total, mass, inverse = refs[-3:]
    outs = refs[n_totals + (2 if first else 4) : -3]
    step = pl.program_id(0)

    @pl.when(step == 0)
    def _():
        for number, (_, blocks, who) in enumerate(plan):
            place = pick(ids[0], blocks) * CORES + ((ids[1] % CORES) ^ who)
            value = totals[0][place]
            for more in totals[1:]:
                value = value + more[place]
            inverse[number] = 1.0 / value
        if first:
            total[...] = jnp.zeros_like(total)
            mass[...] = jnp.zeros_like(mass)
        else:
            total[...] = state[0][...]
            mass[...] = state[1][...]

    resp = (scores[0] * inverse[step]).astype(jnp.bfloat16)
    total[...] += lax.dot_general(
        resp, rows[...], (((1,), (0,)), ((), ())), preferred_element_type=jnp.float32
    )
    wide = resp.astype(jnp.float32)
    partial = wide[:, :LANES]
    for start in range(LANES, wide.shape[1], LANES):
        partial = partial + wide[:, start : start + LANES]
    mass[...] += partial

    @pl.when(step == pl.num_programs(0) - 1)
    def _():
        if not last:
            outs[0][...] = total[...]
            outs[1][...] = mass[...]
            return
        sent = outs[:-2]
        mine, masses = outs[-2:]
        size, depth = mine.shape
        upper = size // 2
        quarter = ids[1] // CORES
        sums = jnp.sum(mass[...].T, axis=0, keepdims=True)
        for number in range(n_owners):
            block = total[number * size : (number + 1) * size, :]
            own = sums[:, number * size : (number + 1) * size]

            @pl.when(quarter == number)
            def _():
                mine[...] = block
                masses[...] = own

            for away in range(1, n_owners):

                @pl.when(quarter ^ number == away)
                def _():
                    first_half, second_half = sent[2 * away - 2 : 2 * away]
                    first_half[...] = block[:upper].astype(first_half.dtype)
                    second_half[: size - upper, :] = block[upper:].astype(second_half.dtype)
                    second_half[size - upper :, :] = three_rows(own, second_half.dtype, depth)


def sum_rows(ids, plan, totals, scores, rows, n_owners, carried, last):
    count = scores.shape[1]
    depth = rows.shape[1]
    size = count // n_owners
    part = totals[0].shape[2]
    first = carried is None
    column = lambda t, s: sum(
        jnp.where(t == n, pick(s[0], columns), 0) for n, (columns, _, _) in enumerate(plan)
    )
    fixed = lambda shape: pl.BlockSpec(shape, lambda t, s: (0,) * len(shape))
    in_specs = [fixed(totals[0].shape) for _ in totals] + [
        pl.BlockSpec((1, count, part), lambda t, s: (column(t, s), 0, 0)),
        pl.BlockSpec((part, depth), lambda t, s: (column(t, s), 0)),
    ]
    state = [(count, depth), (count, LANES)]
    if not first:
        in_specs += [fixed(shape) for shape in state]
    if last:
        shapes = []
        for away in range(1, n_owners):
            kept = [n_owners == 4 and keep == away for keep in (2, 1)]
            for keep, height in zip(kept, (size // 2, size - size // 2 + EXTRA)):
                shapes.append(((height, depth), jnp.float32 if keep else jnp.bfloat16))
        shapes += [((size, depth), jnp.float32), ((1, size), jnp.float32)]
    else:
        shapes = [(shape, jnp.float32) for shape in state]
    return pl.pallas_call(
        functools.partial(sum_kernel, plan, len(totals), n_owners, first, last),
        grid_spec=pltpu.PrefetchScalarGridSpec(
            num_scalar_prefetch=1,
            grid=(len(plan),),
            in_specs=in_specs,
            out_specs=[fixed(shape) for shape, _ in shapes],
            scratch_shapes=[
                pltpu.VMEM((count, depth), jnp.float32),
                pltpu.VMEM((count, LANES), jnp.float32),
                pltpu.VMEM((len(plan), 1, part), jnp.float32),
            ],
        ),
        out_shape=[jax.ShapeDtypeStruct(shape, dtype) for shape, dtype in shapes],
        compiler_params=pltpu.CompilerParams(vmem_limit_bytes=VMEM_LIMIT),
        cost_estimate=pl.CostEstimate(
            flops=2 * count * len(plan) * part * depth,
            bytes_accessed=len(plan) * part * (count * 4 + depth * 2) + count * depth * 4,
            transcendentals=0,
        ),
        name="sums",
    )(ids, *totals, scores, rows, *(carried or ()))


def pass_on_kernel(has_masses, size, mine, arrived, out):
    depth = mine.shape[1]
    height = mine.shape[0] - (EXTRA if has_masses else 0)
    total = mine[:height, :] + arrived[:height, :].astype(jnp.float32)
    out[:height, :] = total.astype(out.dtype)
    if has_masses:
        mass = one_row(mine[height:, :], size) + one_row(arrived[height:, :], size)
        out[height:, :] = three_rows(mass, out.dtype, depth)


def pass_on(mine, arrived, has_masses, size):
    return pl.pallas_call(
        functools.partial(pass_on_kernel, has_masses, size),
        out_shape=jax.ShapeDtypeStruct(arrived.shape, arrived.dtype),
        compiler_params=pltpu.CompilerParams(vmem_limit_bytes=VMEM_LIMIT),
        name="pass_on",
    )(mine, arrived)


def combine_kernel(mine, masses, *refs):
    first_out, second_out = refs[-2:]
    size, depth = mine.shape
    upper = size // 2
    first = mine[:upper, :]
    second = mine[upper:, :]
    mass = masses[...]
    for ref in refs[:-2]:
        if ref.shape[0] == upper:
            first = first + ref[...].astype(jnp.float32)
        else:
            second = second + ref[: size - upper, :].astype(jnp.float32)
            mass = mass + one_row(ref[size - upper :, :], size)
    for total, out in ((first, first_out), (second, second_out)):
        square = jnp.sum(total * total, axis=1, keepdims=True)
        out[: total.shape[0], :] = (total * lax.rsqrt(square + 1e-06)).astype(out.dtype)
    second_out[size - upper :, :] = three_rows(mass, second_out.dtype, depth)


def combine(mine, masses, arrived):
    size, depth = mine.shape
    upper = size // 2
    return pl.pallas_call(
        combine_kernel,
        out_shape=[
            jax.ShapeDtypeStruct((upper, depth), jnp.bfloat16),
            jax.ShapeDtypeStruct((size - upper + EXTRA, depth), jnp.bfloat16),
        ],
        compiler_params=pltpu.CompilerParams(vmem_limit_bytes=VMEM_LIMIT),
        name="combine",
    )(mine, masses, *arrived)


def assemble_kernel(factor, spots, half, ids, *refs):
    units, weights, wide, light, sems = refs[-5:]
    size = wide.shape[1]
    upper = size // 2
    copies = []
    for number, (flip, away) in enumerate(spots):
        first, second = refs[2 * number : 2 * number + 2]
        wide[number, :upper, :] = first[...].astype(jnp.float32)
        wide[number, upper:, :] = second[: size - upper, :].astype(jnp.float32)
        light[number] = one_row(second[size - upper :, :], size) * factor
        block = ((ids[1] % CORES) ^ flip) * half + ((ids[1] // CORES) ^ away)
        place = pl.ds(pl.multiple_of(block * size, size), size)
        copies.append(
            pltpu.make_async_copy(wide.at[number], units.at[place], sems.at[2 * number])
        )
        copies.append(
            pltpu.make_async_copy(light.at[number], weights.at[block], sems.at[2 * number + 1])
        )
        copies[-2].start()
        copies[-1].start()
    for copy in copies:
        copy.wait()


def assemble(ids, pieces, carried, n_blocks, factor):
    arrays = [array for _, _, halves in pieces for array in halves]
    depth = arrays[0].shape[1]
    size = arrays[0].shape[0] + arrays[1].shape[0] - EXTRA
    spots = [(flip, away) for flip, away, _ in pieces]
    extra = carried or ()
    anywhere = pl.BlockSpec(memory_space=pl.ANY)
    return pl.pallas_call(
        functools.partial(assemble_kernel, factor, spots, n_blocks // CORES),
        in_specs=[pl.BlockSpec(memory_space=pltpu.SMEM)]
        + [pl.BlockSpec(memory_space=pltpu.VMEM)] * len(arrays)
        + [anywhere] * len(extra),
        out_specs=[anywhere, anywhere],
        out_shape=[
            jax.ShapeDtypeStruct((n_blocks * size, depth), jnp.float32),
            jax.ShapeDtypeStruct((n_blocks, 1, size), jnp.float32),
        ],
        scratch_shapes=[
            pltpu.VMEM((len(pieces), size, depth), jnp.float32),
            pltpu.VMEM((len(pieces), 1, size), jnp.float32),
            pltpu.SemaphoreType.DMA((2 * len(pieces),)),
        ],
        input_output_aliases={1 + len(arrays) + n: n for n in range(len(extra))},
        compiler_params=pltpu.CompilerParams(vmem_limit_bytes=VMEM_LIMIT),
        name="assemble",
    )(ids, *arrays, *extra)


def local(embeddings, centroids, log_mix):
    n_places = lax.axis_size("blk")
    n_rows = lax.axis_size("rows")
    n_owners = n_rows // CORES
    place = lax.axis_index("blk")
    me = lax.axis_index("rows")
    core = lax.rem(me, CORES)
    held, depth = embeddings.shape
    local_centroids = centroids.shape[0]
    half = local_centroids // CORES
    ids = jnp.stack([place, me]).astype(jnp.int32)
    orders, moves = arrival_plan(n_places)

    def exchange(array, distance):
        return lax.ppermute(array, "rows", [(i, i ^ distance) for i in range(n_rows)])

    def swap_cores(array, places):
        pairs = [
            (spot * n_rows + i, spot * n_rows + (i ^ 1)) for spot in places for i in range(n_rows)
        ]
        return lax.ppermute(array, ("blk", "rows"), pairs)

    slots = [[(embeddings, list(range(n_places)))]] + [[] for _ in range(n_places - 1)]

    def start_ready(moves):
        groups = {}
        left = []
        for move in moves:
            source, target, source_slot, slot = move
            holds = [n for n, (_, places) in enumerate(slots[source_slot]) if source in places]
            if not holds:
                left.append(move)
                continue
            turn = 0
            while any(source == s for s, _ in groups.get((slot, source_slot, holds[0], turn), [])):
                turn += 1
            groups.setdefault((slot, source_slot, holds[0], turn), []).append((source, target))
        moved = [
            (slot, lax.ppermute(slots[source_slot][hold][0], "blk", pairs), [p[1] for p in pairs])
            for (slot, source_slot, hold, _), pairs in sorted(groups.items())
        ]
        return moved, left

    def merged(candidates):
        if len(candidates) <= 2:
            return candidates
        array, held_at = candidates[0][0], list(candidates[0][1])
        for other, places in candidates[1:]:
            here = functools.reduce(jnp.logical_or, [place == spot for spot in places])
            array = jnp.where(here, other, array)
            held_at += places
        return [(array, held_at)]

    own_centroids = lax.dynamic_slice_in_dim(centroids, core * half, half, 0)
    own_mix = lax.dynamic_slice_in_dim(log_mix, core * half, half, 0)
    units = to_unit(own_centroids)
    offsets = jnp.broadcast_to(((own_mix - concentration) * LOG2E)[:, None], (half, LANES))

    n_columns = n_places * CORES
    carried = None

    def scores_of(slot, carried):
        blocks = [order[slot] for order in orders]
        swapped = [(swap_cores(array, places), places) for array, places in slots[slot]]
        for who, candidates in enumerate((slots[slot], swapped)):
            choice = [
                next(n for n, (_, places) in enumerate(candidates) if spot in places)
                for spot in range(n_places)
            ]
            carried = score_block(
                ids,
                [array for array, _ in candidates],
                choice,
                blocks,
                who,
                units,
                offsets,
                carried,
                slot * CORES + who,
                n_columns,
            )
        return carried

    def totals_of(own):
        both = own + exchange(own, 1)
        return [both] + [
            lax.ppermute(both, "blk", [(i, (i + turn) % n_places) for i in range(n_places)])
            for turn in range(1, n_places)
        ]

    settled = {
        block for block in range(n_places) if all(order[-1] != block for order in orders)
    }
    early_totals = None
    def arrive(moved):
        for slot, array, places in moved:
            slots[slot].append((array, places))

    def arrive_behind(moved, carried):
        if moved:
            arrays, carried = lax.optimization_barrier(([array for _, array, _ in moved], carried))
            arrive([(slot, array, places) for (slot, _, places), array in zip(moved, arrays)])
        return carried

    for turn in range(n_places):
        while sum(len(places) for _, places in slots[turn]) < n_places:
            moved, moves = start_ready(moves)
            arrive(moved)
        slots[turn] = merged(slots[turn])
        moved, moves = start_ready(moves)

        carried = scores_of(turn, carried)
        if turn == n_places - 2 and settled:
            early_totals = totals_of(carried[2])
            early_totals, carried = lax.optimization_barrier((early_totals, carried))
        if turn == 0:
            arrive([m for m in moved if m[0] > turn + 1])
            moved = [m for m in moved if m[0] <= turn + 1]
        carried = arrive_behind(moved, carried)
    scores, rows, totals = carried
    steps = sum_plan(orders)
    late = totals_of(totals)
    if early_totals is not None:
        ready = [step for step in steps if all(block in settled for block in step[1])]
        rest = [step for step in steps if step not in ready]
        state = sum_rows(ids, ready, early_totals, scores, rows, n_owners, None, False)
        late, state = lax.optimization_barrier((late, state))
    else:
        rest, state = steps, None
    *sent, mine, masses = sum_rows(ids, rest, late, scores, rows, n_owners, state, True)
    size = mine.shape[0]
    one, two = CORES, 2 * CORES
    if n_owners == 4:
        across, along, corner = sent[0:2], sent[2:4], sent[4:6]
        passing = exchange(corner[0], one), exchange(corner[1], two)
        arrived = [exchange(across[0], one), exchange(along[1], two)]
        arrived.append(exchange(pass_on(along[0], passing[0], False, size), two))
        arrived.append(exchange(pass_on(across[1], passing[1], True, size), one))
    else:
        arrived = [
            exchange(array, CORES * (1 + number // 2)) for number, array in enumerate(sent)
        ]
    payload = combine(mine, masses, arrived)

    count = local_centroids * n_places
    factor = count / (held * n_rows * n_places)
    if n_owners == 4:
        first = exchange(payload[0], one), exchange(payload[1], two)
        second = exchange(payload[1], one), exchange(payload[0], two)
        third = exchange(first[0], two), exchange(first[1], one)
        far = [(1, (first[0], second[0])), (2, (second[1], first[1])), (3, third)]
    else:
        far = [
            (away, tuple(exchange(array, CORES * away) for array in payload))
            for away in range(1, n_owners)
        ]
    swap = lambda halves: tuple(exchange(array, 1) for array in halves)
    done = assemble(ids, [(0, 0, payload), (1, 0, swap(payload))], None, n_rows, factor)
    swapped = [swap(halves) for _, halves in far[:-1]]
    arrays, swapped, done = lax.optimization_barrier(
        ([halves for _, halves in far], swapped, done)
    )
    swapped.append(swap(arrays[-1]))
    placed = [(0, away, halves) for (away, _), halves in zip(far, arrays)]
    placed += [(1, away, halves) for (away, _), halves in zip(far, swapped)]
    last = [piece for piece in placed if piece[1] == n_owners - 1]
    early = [piece for piece in placed if piece[1] != n_owners - 1]
    done = assemble(ids, early, done, n_rows, factor)
    done = assemble(ids, last, done, n_rows, factor)
    result, weights = done
    return (result, weights.reshape(local_centroids))


def solution(mesh):
    return jax.shard_map(
        local,
        mesh=mesh,
        in_specs=(P(("blk", "rows"), None), P("blk", None), P("blk")),
        out_specs=(P("blk", None), P("blk")),
        check_vma=False,
    )
```

```python
import functools
import math

import jax
import jax.numpy as jnp
from jax import lax
from jax.experimental import pallas as pl
from jax.experimental.pallas import tpu as pltpu
from jax.sharding import PartitionSpec as P

concentration = 32.0
LOG2E = math.log2(math.e)
LANES = 128
CORES = 2
EXTRA = 16
VMEM_LIMIT = 16 * 1024 * 1024


def to_unit(values):
    values = values.astype(jnp.float32)
    return (values * lax.rsqrt(jnp.sum(values * values, axis=-1, keepdims=True) + 1e-06)).astype(
        jnp.bfloat16
    )


def arrival_plan(n):
    orders = []
    for place in range(n):
        first = 1 if place < n // 2 else -1
        if 0 < place < n - 1:
            first = -first
        order = [place]
        for step in range(1, n):
            for way in (first, -first):
                if 0 <= place + way * step < n:
                    order.append(place + way * step)
        orders.append(order)
    moves = []
    for place in range(n):
        for slot in range(1, n):
            block = orders[place][slot]
            source = place + (1 if block > place else -1)
            moves.append((source, place, orders[source].index(block), slot))
    return orders, moves


def pick(index, values):
    result = jnp.int32(values[0])
    for number in range(1, len(values)):
        if values[number] != values[0]:
            result = jnp.where(index == number, jnp.int32(values[number]), result)
    return result


def score_kernel(n_sources, choice, ids, *refs):
    sources = refs[:n_sources]
    units_in, log_mix = refs[n_sources], refs[n_sources + 1]
    scores, rows_out, totals, raw, units, sem = refs[-6:]

    @pl.when(pl.program_id(0) == 0)
    def _():
        chosen = pick(ids[0], choice)
        for number, source in enumerate(sources):

            @pl.when(chosen == number)
            def _():
                pltpu.make_async_copy(source, raw, sem).start()

        pltpu.make_async_copy(sources[0], raw, sem).wait()
        values = raw[...].astype(jnp.float32)
        square = jnp.sum(values * values, axis=-1, keepdims=True)
        unit = (values * lax.rsqrt(square + 1e-06)).astype(jnp.bfloat16)
        units[...] = unit
        rows_out[...] = unit
        totals[...] = jnp.zeros_like(totals)

    cosines = lax.dot_general(
        units_in[...], units[...], (((1,), (1,)), ((), ())), preferred_element_type=jnp.float32
    )
    offset = log_mix[...]
    repeats = cosines.shape[1] // offset.shape[1]
    if repeats > 1:
        offset = jnp.concatenate([offset] * repeats, axis=1)
    value = jnp.exp2(cosines * (concentration * LOG2E) + offset)
    scores[0] = value
    totals[0] += jnp.sum(value, axis=0, keepdims=True)


def score_block(ids, sources, choice, blocks, who, units, offsets, carried, column, n_columns):
    part, depth = sources[0].shape
    count = units.shape[0]
    tile = math.gcd(count, 1024)
    shapes = (
        jax.ShapeDtypeStruct((n_columns, count, part), jnp.float32),
        jax.ShapeDtypeStruct((n_columns * part, depth), jnp.bfloat16),
        jax.ShapeDtypeStruct((n_columns, 1, part), jnp.float32),
    )
    n_sources = len(sources)
    aliases = {}
    extra = ()
    if carried is not None:
        extra = carried
        aliases = {1 + n_sources + 2 + i: i for i in range(3)}
    anywhere = pl.BlockSpec(memory_space=pl.ANY)
    return pl.pallas_call(
        functools.partial(score_kernel, n_sources, choice),
        grid_spec=pltpu.PrefetchScalarGridSpec(
            num_scalar_prefetch=1,
            grid=(count // tile,),
            in_specs=[anywhere] * n_sources
            + [
                pl.BlockSpec((tile, depth), lambda t, s: (t, 0)),
                pl.BlockSpec((tile, offsets.shape[1]), lambda t, s: (t, 0)),
            ]
            + [anywhere] * len(extra),
            out_specs=[
                pl.BlockSpec((1, tile, part), lambda t, s: (column, t, 0)),
                pl.BlockSpec((part, depth), lambda t, s: (column, 0)),
                pl.BlockSpec(
                    (1, 1, part),
                    lambda t, s: (pick(s[0], blocks) * CORES + ((s[1] % CORES) ^ who), 0, 0),
                ),
            ],
            scratch_shapes=[
                pltpu.VMEM((part, depth), jnp.bfloat16),
                pltpu.VMEM((part, depth), jnp.bfloat16),
                pltpu.SemaphoreType.DMA,
            ],
        ),
        out_shape=shapes,
        input_output_aliases=aliases,
        compiler_params=pltpu.CompilerParams(vmem_limit_bytes=VMEM_LIMIT),
        cost_estimate=pl.CostEstimate(
            flops=2 * count * part * depth,
            bytes_accessed=2 * (count * part * 4 + count * depth * 2),
            transcendentals=count * part,
        ),
        name="scores",
    )(ids, *sources, units, offsets, *extra)


def sum_plan(orders):
    n = len(orders)
    last = {order[-1] for order in orders}
    sorted_slots = []
    for order in orders:
        slots = list(range(n))
        sorted_slots.append(sorted(slots, key=lambda slot: (order[slot] in last, slot)))
    steps = []
    for turn in range(n):
        slots = [sorted_slots[place][turn] for place in range(n)]
        blocks = [orders[place][slot] for place, slot in enumerate(slots)]
        for who in range(CORES):
            steps.append(([slot * CORES + who for slot in slots], blocks, who))
    return steps


def three_rows(values, dtype, depth):
    size = values.shape[1]
    line = lax.broadcasted_iota(jnp.int32, (EXTRA, size), 0)
    high = values.astype(dtype).astype(jnp.float32)
    rest = values - high
    middle = rest.astype(dtype).astype(jnp.float32)
    low = rest - middle
    rows = jnp.where(
        line == 0, high, jnp.where(line == 1, middle, jnp.where(line == 2, low, 0.0))
    )
    if size < depth:
        rows = jnp.concatenate([rows, jnp.zeros((EXTRA, depth - size), jnp.float32)], axis=1)
    return rows.astype(dtype)


def one_row(rows, size):
    return jnp.sum(rows[:, :size].astype(jnp.float32), axis=0, keepdims=True)


def sum_kernel(plan, n_totals, n_owners, first, last, ids, *refs):
    totals = refs[:n_totals]
    scores, rows = refs[n_totals], refs[n_totals + 1]
    state = refs[n_totals + 2 : n_totals + 4]
    total, mass, inverse = refs[-3:]
    outs = refs[n_totals + (2 if first else 4) : -3]
    step = pl.program_id(0)

    @pl.when(step == 0)
    def _():
        for number, (_, blocks, who) in enumerate(plan):
            place = pick(ids[0], blocks) * CORES + ((ids[1] % CORES) ^ who)
            value = totals[0][place]
            for more in totals[1:]:
                value = value + more[place]
            inverse[number] = 1.0 / value
        if first:
            total[...] = jnp.zeros_like(total)
            mass[...] = jnp.zeros_like(mass)
        else:
            total[...] = state[0][...]
            mass[...] = state[1][...]

    resp = (scores[0] * inverse[step]).astype(jnp.bfloat16)
    total[...] += lax.dot_general(
        resp, rows[...], (((1,), (0,)), ((), ())), preferred_element_type=jnp.float32
    )
    wide = resp.astype(jnp.float32)
    partial = wide[:, :LANES]
    for start in range(LANES, wide.shape[1], LANES):
        partial = partial + wide[:, start : start + LANES]
    mass[...] += partial

    @pl.when(step == pl.num_programs(0) - 1)
    def _():
        if not last:
            outs[0][...] = total[...]
            outs[1][...] = mass[...]
            return
        sent = outs[:-2]
        mine, masses = outs[-2:]
        size, depth = mine.shape
        upper = size // 2
        quarter = ids[1] // CORES
        sums = jnp.sum(mass[...].T, axis=0, keepdims=True)
        for number in range(n_owners):
            block = total[number * size : (number + 1) * size, :]
            own = sums[:, number * size : (number + 1) * size]

            @pl.when(quarter == number)
            def _():
                mine[...] = block
                masses[...] = own

            for away in range(1, n_owners):

                @pl.when(quarter ^ number == away)
                def _():
                    first_half, second_half = sent[2 * away - 2 : 2 * away]
                    first_half[...] = block[:upper].astype(first_half.dtype)
                    second_half[: size - upper, :] = block[upper:].astype(second_half.dtype)
                    second_half[size - upper :, :] = three_rows(own, second_half.dtype, depth)


def sum_rows(ids, plan, totals, scores, rows, n_owners, carried, last):
    count = scores.shape[1]
    depth = rows.shape[1]
    size = count // n_owners
    part = totals[0].shape[2]
    first = carried is None
    column = lambda t, s: sum(
        jnp.where(t == n, pick(s[0], columns), 0) for n, (columns, _, _) in enumerate(plan)
    )
    fixed = lambda shape: pl.BlockSpec(shape, lambda t, s: (0,) * len(shape))
    in_specs = [fixed(totals[0].shape) for _ in totals] + [
        pl.BlockSpec((1, count, part), lambda t, s: (column(t, s), 0, 0)),
        pl.BlockSpec((part, depth), lambda t, s: (column(t, s), 0)),
    ]
    state = [(count, depth), (count, LANES)]
    if not first:
        in_specs += [fixed(shape) for shape in state]
    if last:
        shapes = []
        for away in range(1, n_owners):
            kept = [n_owners == 4 and keep == away for keep in (2, 1)]
            for keep, height in zip(kept, (size // 2, size - size // 2 + EXTRA)):
                shapes.append(((height, depth), jnp.float32 if keep else jnp.bfloat16))
        shapes += [((size, depth), jnp.float32), ((1, size), jnp.float32)]
    else:
        shapes = [(shape, jnp.float32) for shape in state]
    return pl.pallas_call(
        functools.partial(sum_kernel, plan, len(totals), n_owners, first, last),
        grid_spec=pltpu.PrefetchScalarGridSpec(
            num_scalar_prefetch=1,
            grid=(len(plan),),
            in_specs=in_specs,
            out_specs=[fixed(shape) for shape, _ in shapes],
            scratch_shapes=[
                pltpu.VMEM((count, depth), jnp.float32),
                pltpu.VMEM((count, LANES), jnp.float32),
                pltpu.VMEM((len(plan), 1, part), jnp.float32),
            ],
        ),
        out_shape=[jax.ShapeDtypeStruct(shape, dtype) for shape, dtype in shapes],
        compiler_params=pltpu.CompilerParams(vmem_limit_bytes=VMEM_LIMIT),
        cost_estimate=pl.CostEstimate(
            flops=2 * count * len(plan) * part * depth,
            bytes_accessed=len(plan) * part * (count * 4 + depth * 2) + count * depth * 4,
            transcendentals=0,
        ),
        name="sums",
    )(ids, *totals, scores, rows, *(carried or ()))


def pass_on_kernel(has_masses, size, mine, arrived, out):
    depth = mine.shape[1]
    height = mine.shape[0] - (EXTRA if has_masses else 0)
    total = mine[:height, :] + arrived[:height, :].astype(jnp.float32)
    out[:height, :] = total.astype(out.dtype)
    if has_masses:
        mass = one_row(mine[height:, :], size) + one_row(arrived[height:, :], size)
        out[height:, :] = three_rows(mass, out.dtype, depth)


def pass_on(mine, arrived, has_masses, size):
    return pl.pallas_call(
        functools.partial(pass_on_kernel, has_masses, size),
        out_shape=jax.ShapeDtypeStruct(arrived.shape, arrived.dtype),
        compiler_params=pltpu.CompilerParams(vmem_limit_bytes=VMEM_LIMIT),
        name="pass_on",
    )(mine, arrived)


def combine_kernel(mine, masses, *refs):
    first_out, second_out = refs[-2:]
    size, depth = mine.shape
    upper = size // 2
    first = mine[:upper, :]
    second = mine[upper:, :]
    mass = masses[...]
    for ref in refs[:-2]:
        if ref.shape[0] == upper:
            first = first + ref[...].astype(jnp.float32)
        else:
            second = second + ref[: size - upper, :].astype(jnp.float32)
            mass = mass + one_row(ref[size - upper :, :], size)
    for total, out in ((first, first_out), (second, second_out)):
        square = jnp.sum(total * total, axis=1, keepdims=True)
        out[: total.shape[0], :] = (total * lax.rsqrt(square + 1e-06)).astype(out.dtype)
    second_out[size - upper :, :] = three_rows(mass, second_out.dtype, depth)


def combine(mine, masses, arrived):
    size, depth = mine.shape
    upper = size // 2
    return pl.pallas_call(
        combine_kernel,
        out_shape=[
            jax.ShapeDtypeStruct((upper, depth), jnp.bfloat16),
            jax.ShapeDtypeStruct((size - upper + EXTRA, depth), jnp.bfloat16),
        ],
        compiler_params=pltpu.CompilerParams(vmem_limit_bytes=VMEM_LIMIT),
        name="combine",
    )(mine, masses, *arrived)


def assemble_kernel(factor, spots, half, ids, *refs):
    units, weights, wide, light, sems = refs[-5:]
    size = wide.shape[1]
    upper = size // 2
    copies = []
    for number, (flip, away) in enumerate(spots):
        first, second = refs[2 * number : 2 * number + 2]
        wide[number, :upper, :] = first[...].astype(jnp.float32)
        wide[number, upper:, :] = second[: size - upper, :].astype(jnp.float32)
        light[number] = one_row(second[size - upper :, :], size) * factor
        block = ((ids[1] % CORES) ^ flip) * half + ((ids[1] // CORES) ^ away)
        place = pl.ds(pl.multiple_of(block * size, size), size)
        copies.append(
            pltpu.make_async_copy(wide.at[number], units.at[place], sems.at[2 * number])
        )
        copies.append(
            pltpu.make_async_copy(light.at[number], weights.at[block], sems.at[2 * number + 1])
        )
        copies[-2].start()
        copies[-1].start()
    for copy in copies:
        copy.wait()


def assemble(ids, pieces, carried, n_blocks, factor):
    arrays = [array for _, _, halves in pieces for array in halves]
    depth = arrays[0].shape[1]
    size = arrays[0].shape[0] + arrays[1].shape[0] - EXTRA
    spots = [(flip, away) for flip, away, _ in pieces]
    extra = carried or ()
    anywhere = pl.BlockSpec(memory_space=pl.ANY)
    return pl.pallas_call(
        functools.partial(assemble_kernel, factor, spots, n_blocks // CORES),
        in_specs=[pl.BlockSpec(memory_space=pltpu.SMEM)]
        + [pl.BlockSpec(memory_space=pltpu.VMEM)] * len(arrays)
        + [anywhere] * len(extra),
        out_specs=[anywhere, anywhere],
        out_shape=[
            jax.ShapeDtypeStruct((n_blocks * size, depth), jnp.float32),
            jax.ShapeDtypeStruct((n_blocks, 1, size), jnp.float32),
        ],
        scratch_shapes=[
            pltpu.VMEM((len(pieces), size, depth), jnp.float32),
            pltpu.VMEM((len(pieces), 1, size), jnp.float32),
            pltpu.SemaphoreType.DMA((2 * len(pieces),)),
        ],
        input_output_aliases={1 + len(arrays) + n: n for n in range(len(extra))},
        compiler_params=pltpu.CompilerParams(vmem_limit_bytes=VMEM_LIMIT),
        name="assemble",
    )(ids, *arrays, *extra)


def local(embeddings, centroids, log_mix):
    n_places = lax.axis_size("blk")
    n_rows = lax.axis_size("rows")
    n_owners = n_rows // CORES
    place = lax.axis_index("blk")
    me = lax.axis_index("rows")
    core = lax.rem(me, CORES)
    held, depth = embeddings.shape
    local_centroids = centroids.shape[0]
    half = local_centroids // CORES
    ids = jnp.stack([place, me]).astype(jnp.int32)
    orders, moves = arrival_plan(n_places)

    def exchange(array, distance):
        return lax.ppermute(array, "rows", [(i, i ^ distance) for i in range(n_rows)])

    def swap_cores(array, places):
        pairs = [
            (spot * n_rows + i, spot * n_rows + (i ^ 1)) for spot in places for i in range(n_rows)
        ]
        return lax.ppermute(array, ("blk", "rows"), pairs)

    slots = [[(embeddings, list(range(n_places)))]] + [[] for _ in range(n_places - 1)]

    def start_ready(moves):
        groups = {}
        left = []
        for move in moves:
            source, target, source_slot, slot = move
            holds = [n for n, (_, places) in enumerate(slots[source_slot]) if source in places]
            if not holds:
                left.append(move)
                continue
            turn = 0
            while any(source == s for s, _ in groups.get((slot, source_slot, holds[0], turn), [])):
                turn += 1
            groups.setdefault((slot, source_slot, holds[0], turn), []).append((source, target))
        moved = [
            (slot, lax.ppermute(slots[source_slot][hold][0], "blk", pairs), [p[1] for p in pairs])
            for (slot, source_slot, hold, _), pairs in sorted(groups.items())
        ]
        return moved, left

    def merged(candidates):
        if len(candidates) <= 2:
            return candidates
        array, held_at = candidates[0][0], list(candidates[0][1])
        for other, places in candidates[1:]:
            here = functools.reduce(jnp.logical_or, [place == spot for spot in places])
            array = jnp.where(here, other, array)
            held_at += places
        return [(array, held_at)]

    own_centroids = lax.dynamic_slice_in_dim(centroids, core * half, half, 0)
    own_mix = lax.dynamic_slice_in_dim(log_mix, core * half, half, 0)
    units = to_unit(own_centroids)
    offsets = jnp.broadcast_to(((own_mix - concentration) * LOG2E)[:, None], (half, LANES))

    n_columns = n_places * CORES
    carried = None

    def scores_of(slot, carried):
        blocks = [order[slot] for order in orders]
        swapped = [(swap_cores(array, places), places) for array, places in slots[slot]]
        for who, candidates in enumerate((slots[slot], swapped)):
            choice = [
                next(n for n, (_, places) in enumerate(candidates) if spot in places)
                for spot in range(n_places)
            ]
            carried = score_block(
                ids,
                [array for array, _ in candidates],
                choice,
                blocks,
                who,
                units,
                offsets,
                carried,
                slot * CORES + who,
                n_columns,
            )
        return carried

    def totals_of(own):
        both = own + exchange(own, 1)
        return [both] + [
            lax.ppermute(both, "blk", [(i, (i + turn) % n_places) for i in range(n_places)])
            for turn in range(1, n_places)
        ]

    settled = {
        block for block in range(n_places) if all(order[-1] != block for order in orders)
    }
    early_totals = None
    def arrive(moved):
        for slot, array, places in moved:
            slots[slot].append((array, places))

    def arrive_behind(moved, carried):
        if moved:
            arrays, carried = lax.optimization_barrier(([array for _, array, _ in moved], carried))
            arrive([(slot, array, places) for (slot, _, places), array in zip(moved, arrays)])
        return carried

    for turn in range(n_places):
        while sum(len(places) for _, places in slots[turn]) < n_places:
            moved, moves = start_ready(moves)
            arrive(moved)
        slots[turn] = merged(slots[turn])
        moved, moves = start_ready(moves)

        carried = scores_of(turn, carried)
        if turn == n_places - 2 and settled:
            early_totals = totals_of(carried[2])
            early_totals, carried = lax.optimization_barrier((early_totals, carried))
        if turn == 0:
            arrive([m for m in moved if m[0] > turn + 1])
            moved = [m for m in moved if m[0] <= turn + 1]
        carried = arrive_behind(moved, carried)
    scores, rows, totals = carried
    steps = sum_plan(orders)
    late = totals_of(totals)
    if early_totals is not None:
        ready = [step for step in steps if all(block in settled for block in step[1])]
        rest = [step for step in steps if step not in ready]
        state = sum_rows(ids, ready, early_totals, scores, rows, n_owners, None, False)
        late, state = lax.optimization_barrier((late, state))
    else:
        rest, state = steps, None
    *sent, mine, masses = sum_rows(ids, rest, late, scores, rows, n_owners, state, True)
    size = mine.shape[0]
    one, two = CORES, 2 * CORES
    if n_owners == 4:
        across, along, corner = sent[0:2], sent[2:4], sent[4:6]
        passing = exchange(corner[0], one), exchange(corner[1], two)
        arrived = [exchange(across[0], one), exchange(along[1], two)]
        arrived.append(exchange(pass_on(along[0], passing[0], False, size), two))
        arrived.append(exchange(pass_on(across[1], passing[1], True, size), one))
    else:
        arrived = [
            exchange(array, CORES * (1 + number // 2)) for number, array in enumerate(sent)
        ]
    payload = combine(mine, masses, arrived)

    count = local_centroids * n_places
    factor = count / (held * n_rows * n_places)
    if n_owners == 4:
        first = exchange(payload[0], one), exchange(payload[1], two)
        second = exchange(payload[1], one), exchange(payload[0], two)
        third = exchange(first[0], two), exchange(first[1], one)
        far = [(1, (first[0], second[0])), (2, (second[1], first[1])), (3, third)]
    else:
        far = [
            (away, tuple(exchange(array, CORES * away) for array in payload))
            for away in range(1, n_owners)
        ]
    swap = lambda halves: tuple(exchange(array, 1) for array in halves)
    done = assemble(ids, [(0, 0, payload), (1, 0, swap(payload))], None, n_rows, factor)
    if n_owners == 4:
        last_half, done = lax.optimization_barrier((second[1], done))
        far[1] = (2, (last_half, first[1]))
    swapped = [swap(halves) for _, halves in far[:-1]]
    arrays, swapped, done = lax.optimization_barrier(
        ([halves for _, halves in far], swapped, done)
    )
    swapped.append(swap(arrays[-1]))
    placed = [(0, away, halves) for (away, _), halves in zip(far, arrays)]
    placed += [(1, away, halves) for (away, _), halves in zip(far, swapped)]
    last = [piece for piece in placed if piece[1] == n_owners - 1]
    early = [piece for piece in placed if piece[1] != n_owners - 1]
    done = assemble(ids, early, done, n_rows, factor)
    done = assemble(ids, last, done, n_rows, factor)
    result, weights = done
    return (result, weights.reshape(local_centroids))


def solution(mesh):
    return jax.shard_map(
        local,
        mesh=mesh,
        in_specs=(P(("blk", "rows"), None), P("blk", None), P("blk")),
        out_specs=(P("blk", None), P("blk")),
        check_vma=False,
    )
```

```python
import functools
import math

import jax
import jax.numpy as jnp
from jax import lax
from jax.experimental import pallas as pl
from jax.experimental.pallas import tpu as pltpu
from jax.sharding import PartitionSpec as P

concentration = 32.0
LOG2E = math.log2(math.e)
LANES = 128
CORES = 2
EXTRA = 16
VMEM_LIMIT = 16 * 1024 * 1024


def to_unit(values):
    values = values.astype(jnp.float32)
    return (values * lax.rsqrt(jnp.sum(values * values, axis=-1, keepdims=True) + 1e-06)).astype(
        jnp.bfloat16
    )


def arrival_plan(n):
    orders = []
    for place in range(n):
        first = 1 if place < n // 2 else -1
        if 0 < place < n - 1:
            first = -first
        order = [place]
        for step in range(1, n):
            for way in (first, -first):
                if 0 <= place + way * step < n:
                    order.append(place + way * step)
        orders.append(order)
    moves = []
    for place in range(n):
        for slot in range(1, n):
            block = orders[place][slot]
            source = place + (1 if block > place else -1)
            moves.append((source, place, orders[source].index(block), slot))
    return orders, moves


def pick(index, values):
    result = jnp.int32(values[0])
    for number in range(1, len(values)):
        if values[number] != values[0]:
            result = jnp.where(index == number, jnp.int32(values[number]), result)
    return result


def score_kernel(n_sources, choice, ids, *refs):
    sources = refs[:n_sources]
    units_in, log_mix = refs[n_sources], refs[n_sources + 1]
    scores, rows_out, totals, raw, units, sem = refs[-6:]

    @pl.when(pl.program_id(0) == 0)
    def _():
        chosen = pick(ids[0], choice)
        for number, source in enumerate(sources):

            @pl.when(chosen == number)
            def _():
                pltpu.make_async_copy(source, raw, sem).start()

        pltpu.make_async_copy(sources[0], raw, sem).wait()
        values = raw[...].astype(jnp.float32)
        square = jnp.sum(values * values, axis=-1, keepdims=True)
        unit = (values * lax.rsqrt(square + 1e-06)).astype(jnp.bfloat16)
        units[...] = unit
        rows_out[...] = unit
        totals[...] = jnp.zeros_like(totals)

    cosines = lax.dot_general(
        units_in[...], units[...], (((1,), (1,)), ((), ())), preferred_element_type=jnp.float32
    )
    offset = log_mix[...]
    repeats = cosines.shape[1] // offset.shape[1]
    if repeats > 1:
        offset = jnp.concatenate([offset] * repeats, axis=1)
    value = jnp.exp2(cosines * (concentration * LOG2E) + offset)
    scores[0] = value
    totals[0] += jnp.sum(value, axis=0, keepdims=True)


def score_block(ids, sources, choice, blocks, who, units, offsets, carried, column, n_columns):
    part, depth = sources[0].shape
    count = units.shape[0]
    tile = math.gcd(count, 1024)
    shapes = (
        jax.ShapeDtypeStruct((n_columns, count, part), jnp.float32),
        jax.ShapeDtypeStruct((n_columns * part, depth), jnp.bfloat16),
        jax.ShapeDtypeStruct((n_columns, 1, part), jnp.float32),
    )
    n_sources = len(sources)
    aliases = {}
    extra = ()
    if carried is not None:
        extra = carried
        aliases = {1 + n_sources + 2 + i: i for i in range(3)}
    anywhere = pl.BlockSpec(memory_space=pl.ANY)
    return pl.pallas_call(
        functools.partial(score_kernel, n_sources, choice),
        grid_spec=pltpu.PrefetchScalarGridSpec(
            num_scalar_prefetch=1,
            grid=(count // tile,),
            in_specs=[anywhere] * n_sources
            + [
                pl.BlockSpec((tile, depth), lambda t, s: (t, 0)),
                pl.BlockSpec((tile, offsets.shape[1]), lambda t, s: (t, 0)),
            ]
            + [anywhere] * len(extra),
            out_specs=[
                pl.BlockSpec((1, tile, part), lambda t, s: (column, t, 0)),
                pl.BlockSpec((part, depth), lambda t, s: (column, 0)),
                pl.BlockSpec(
                    (1, 1, part),
                    lambda t, s: (pick(s[0], blocks) * CORES + ((s[1] % CORES) ^ who), 0, 0),
                ),
            ],
            scratch_shapes=[
                pltpu.VMEM((part, depth), jnp.bfloat16),
                pltpu.VMEM((part, depth), jnp.bfloat16),
                pltpu.SemaphoreType.DMA,
            ],
        ),
        out_shape=shapes,
        input_output_aliases=aliases,
        compiler_params=pltpu.CompilerParams(vmem_limit_bytes=VMEM_LIMIT),
        cost_estimate=pl.CostEstimate(
            flops=2 * count * part * depth,
            bytes_accessed=2 * (count * part * 4 + count * depth * 2),
            transcendentals=count * part,
        ),
        name="scores",
    )(ids, *sources, units, offsets, *extra)


def sum_plan(orders):
    n = len(orders)
    last = {order[-1] for order in orders}
    sorted_slots = []
    for order in orders:
        slots = list(range(n))
        sorted_slots.append(sorted(slots, key=lambda slot: (order[slot] in last, slot)))
    steps = []
    for turn in range(n):
        slots = [sorted_slots[place][turn] for place in range(n)]
        blocks = [orders[place][slot] for place, slot in enumerate(slots)]
        for who in range(CORES):
            steps.append(([slot * CORES + who for slot in slots], blocks, who))
    return steps


def three_rows(values, dtype, depth):
    size = values.shape[1]
    line = lax.broadcasted_iota(jnp.int32, (EXTRA, size), 0)
    high = values.astype(dtype).astype(jnp.float32)
    rest = values - high
    middle = rest.astype(dtype).astype(jnp.float32)
    low = rest - middle
    rows = jnp.where(
        line == 0, high, jnp.where(line == 1, middle, jnp.where(line == 2, low, 0.0))
    )
    if size < depth:
        rows = jnp.concatenate([rows, jnp.zeros((EXTRA, depth - size), jnp.float32)], axis=1)
    return rows.astype(dtype)


def one_row(rows, size):
    return jnp.sum(rows[:, :size].astype(jnp.float32), axis=0, keepdims=True)


def sum_kernel(plan, n_totals, n_owners, first, last, ids, *refs):
    totals = refs[:n_totals]
    scores, rows = refs[n_totals], refs[n_totals + 1]
    state = refs[n_totals + 2 : n_totals + 4]
    total, mass, inverse = refs[-3:]
    outs = refs[n_totals + (2 if first else 4) : -3]
    step = pl.program_id(0)

    @pl.when(step == 0)
    def _():
        for number, (_, blocks, who) in enumerate(plan):
            place = pick(ids[0], blocks) * CORES + ((ids[1] % CORES) ^ who)
            value = totals[0][place]
            for more in totals[1:]:
                value = value + more[place]
            inverse[number] = 1.0 / value
        if first:
            total[...] = jnp.zeros_like(total)
            mass[...] = jnp.zeros_like(mass)
        else:
            total[...] = state[0][...]
            mass[...] = state[1][...]

    resp = (scores[0] * inverse[step]).astype(jnp.bfloat16)
    total[...] += lax.dot_general(
        resp, rows[...], (((1,), (0,)), ((), ())), preferred_element_type=jnp.float32
    )
    wide = resp.astype(jnp.float32)
    partial = wide[:, :LANES]
    for start in range(LANES, wide.shape[1], LANES):
        partial = partial + wide[:, start : start + LANES]
    mass[...] += partial

    @pl.when(step == pl.num_programs(0) - 1)
    def _():
        if not last:
            outs[0][...] = total[...]
            outs[1][...] = mass[...]
            return
        sent = outs[:-2]
        mine, masses = outs[-2:]
        size, depth = mine.shape
        upper = size // 2
        quarter = ids[1] // CORES
        sums = jnp.sum(mass[...].T, axis=0, keepdims=True)
        for number in range(n_owners):
            block = total[number * size : (number + 1) * size, :]
            own = sums[:, number * size : (number + 1) * size]

            @pl.when(quarter == number)
            def _():
                mine[...] = block
                masses[...] = own

            for away in range(1, n_owners):

                @pl.when(quarter ^ number == away)
                def _():
                    first_half, second_half = sent[2 * away - 2 : 2 * away]
                    first_half[...] = block[:upper].astype(first_half.dtype)
                    second_half[: size - upper, :] = block[upper:].astype(second_half.dtype)
                    second_half[size - upper :, :] = three_rows(own, second_half.dtype, depth)


def sum_rows(ids, plan, totals, scores, rows, n_owners, carried, last):
    count = scores.shape[1]
    depth = rows.shape[1]
    size = count // n_owners
    part = totals[0].shape[2]
    first = carried is None
    column = lambda t, s: sum(
        jnp.where(t == n, pick(s[0], columns), 0) for n, (columns, _, _) in enumerate(plan)
    )
    fixed = lambda shape: pl.BlockSpec(shape, lambda t, s: (0,) * len(shape))
    in_specs = [fixed(totals[0].shape) for _ in totals] + [
        pl.BlockSpec((1, count, part), lambda t, s: (column(t, s), 0, 0)),
        pl.BlockSpec((part, depth), lambda t, s: (column(t, s), 0)),
    ]
    state = [(count, depth), (count, LANES)]
    if not first:
        in_specs += [fixed(shape) for shape in state]
    if last:
        shapes = []
        for away in range(1, n_owners):
            kept = [n_owners == 4 and keep == away for keep in (2, 1)]
            for keep, height in zip(kept, (size // 2, size - size // 2 + EXTRA)):
                shapes.append(((height, depth), jnp.float32 if keep else jnp.bfloat16))
        shapes += [((size, depth), jnp.float32), ((1, size), jnp.float32)]
    else:
        shapes = [(shape, jnp.float32) for shape in state]
    return pl.pallas_call(
        functools.partial(sum_kernel, plan, len(totals), n_owners, first, last),
        grid_spec=pltpu.PrefetchScalarGridSpec(
            num_scalar_prefetch=1,
            grid=(len(plan),),
            in_specs=in_specs,
            out_specs=[fixed(shape) for shape, _ in shapes],
            scratch_shapes=[
                pltpu.VMEM((count, depth), jnp.float32),
                pltpu.VMEM((count, LANES), jnp.float32),
                pltpu.VMEM((len(plan), 1, part), jnp.float32),
            ],
        ),
        out_shape=[jax.ShapeDtypeStruct(shape, dtype) for shape, dtype in shapes],
        compiler_params=pltpu.CompilerParams(vmem_limit_bytes=VMEM_LIMIT),
        cost_estimate=pl.CostEstimate(
            flops=2 * count * len(plan) * part * depth,
            bytes_accessed=len(plan) * part * (count * 4 + depth * 2) + count * depth * 4,
            transcendentals=0,
        ),
        name="sums",
    )(ids, *totals, scores, rows, *(carried or ()))


def pass_on_kernel(has_masses, size, mine, arrived, out):
    depth = mine.shape[1]
    height = mine.shape[0] - (EXTRA if has_masses else 0)
    total = mine[:height, :] + arrived[:height, :].astype(jnp.float32)
    out[:height, :] = total.astype(out.dtype)
    if has_masses:
        mass = one_row(mine[height:, :], size) + one_row(arrived[height:, :], size)
        out[height:, :] = three_rows(mass, out.dtype, depth)


def pass_on(mine, arrived, has_masses, size):
    return pl.pallas_call(
        functools.partial(pass_on_kernel, has_masses, size),
        out_shape=jax.ShapeDtypeStruct(arrived.shape, arrived.dtype),
        compiler_params=pltpu.CompilerParams(vmem_limit_bytes=VMEM_LIMIT),
        name="pass_on",
    )(mine, arrived)


def combine_kernel(mine, masses, *refs):
    first_out, second_out = refs[-2:]
    size, depth = mine.shape
    upper = size // 2
    first = mine[:upper, :]
    second = mine[upper:, :]
    mass = masses[...]
    for ref in refs[:-2]:
        if ref.shape[0] == upper:
            first = first + ref[...].astype(jnp.float32)
        else:
            second = second + ref[: size - upper, :].astype(jnp.float32)
            mass = mass + one_row(ref[size - upper :, :], size)
    for total, out in ((first, first_out), (second, second_out)):
        square = jnp.sum(total * total, axis=1, keepdims=True)
        out[: total.shape[0], :] = (total * lax.rsqrt(square + 1e-06)).astype(out.dtype)
    second_out[size - upper :, :] = three_rows(mass, second_out.dtype, depth)


def combine(mine, masses, arrived):
    size, depth = mine.shape
    upper = size // 2
    return pl.pallas_call(
        combine_kernel,
        out_shape=[
            jax.ShapeDtypeStruct((upper, depth), jnp.bfloat16),
            jax.ShapeDtypeStruct((size - upper + EXTRA, depth), jnp.bfloat16),
        ],
        compiler_params=pltpu.CompilerParams(vmem_limit_bytes=VMEM_LIMIT),
        name="combine",
    )(mine, masses, *arrived)


def assemble_kernel(factor, spots, half, ids, *refs):
    units, weights, wide, light, sems = refs[-5:]
    size = wide.shape[1]
    upper = size // 2
    copies = []
    for number, (flip, away) in enumerate(spots):
        first, second = refs[2 * number : 2 * number + 2]
        wide[number, :upper, :] = first[...].astype(jnp.float32)
        wide[number, upper:, :] = second[: size - upper, :].astype(jnp.float32)
        light[number] = one_row(second[size - upper :, :], size) * factor
        block = ((ids[1] % CORES) ^ flip) * half + ((ids[1] // CORES) ^ away)
        place = pl.ds(pl.multiple_of(block * size, size), size)
        copies.append(
            pltpu.make_async_copy(wide.at[number], units.at[place], sems.at[2 * number])
        )
        copies.append(
            pltpu.make_async_copy(light.at[number], weights.at[block], sems.at[2 * number + 1])
        )
        copies[-2].start()
        copies[-1].start()
    for copy in copies:
        copy.wait()


def assemble(ids, pieces, carried, n_blocks, factor):
    arrays = [array for _, _, halves in pieces for array in halves]
    depth = arrays[0].shape[1]
    size = arrays[0].shape[0] + arrays[1].shape[0] - EXTRA
    spots = [(flip, away) for flip, away, _ in pieces]
    extra = carried or ()
    anywhere = pl.BlockSpec(memory_space=pl.ANY)
    return pl.pallas_call(
        functools.partial(assemble_kernel, factor, spots, n_blocks // CORES),
        in_specs=[pl.BlockSpec(memory_space=pltpu.SMEM)]
        + [pl.BlockSpec(memory_space=pltpu.VMEM)] * len(arrays)
        + [anywhere] * len(extra),
        out_specs=[anywhere, anywhere],
        out_shape=[
            jax.ShapeDtypeStruct((n_blocks * size, depth), jnp.float32),
            jax.ShapeDtypeStruct((n_blocks, 1, size), jnp.float32),
        ],
        scratch_shapes=[
            pltpu.VMEM((len(pieces), size, depth), jnp.float32),
            pltpu.VMEM((len(pieces), 1, size), jnp.float32),
            pltpu.SemaphoreType.DMA((2 * len(pieces),)),
        ],
        input_output_aliases={1 + len(arrays) + n: n for n in range(len(extra))},
        compiler_params=pltpu.CompilerParams(vmem_limit_bytes=VMEM_LIMIT),
        name="assemble",
    )(ids, *arrays, *extra)


def local(embeddings, centroids, log_mix):
    n_places = lax.axis_size("blk")
    n_rows = lax.axis_size("rows")
    n_owners = n_rows // CORES
    place = lax.axis_index("blk")
    me = lax.axis_index("rows")
    core = lax.rem(me, CORES)
    held, depth = embeddings.shape
    local_centroids = centroids.shape[0]
    half = local_centroids // CORES
    ids = jnp.stack([place, me]).astype(jnp.int32)
    orders, moves = arrival_plan(n_places)

    def exchange(array, distance):
        return lax.ppermute(array, "rows", [(i, i ^ distance) for i in range(n_rows)])

    def swap_cores(array, places):
        pairs = [
            (spot * n_rows + i, spot * n_rows + (i ^ 1)) for spot in places for i in range(n_rows)
        ]
        return lax.ppermute(array, ("blk", "rows"), pairs)

    slots = [[(embeddings, list(range(n_places)))]] + [[] for _ in range(n_places - 1)]

    def start_ready(moves):
        groups = {}
        left = []
        for move in moves:
            source, target, source_slot, slot = move
            holds = [n for n, (_, places) in enumerate(slots[source_slot]) if source in places]
            if not holds:
                left.append(move)
                continue
            turn = 0
            while any(source == s for s, _ in groups.get((slot, source_slot, holds[0], turn), [])):
                turn += 1
            groups.setdefault((slot, source_slot, holds[0], turn), []).append((source, target))
        moved = [
            (slot, lax.ppermute(slots[source_slot][hold][0], "blk", pairs), [p[1] for p in pairs])
            for (slot, source_slot, hold, _), pairs in sorted(groups.items())
        ]
        return moved, left

    def merged(candidates):
        if len(candidates) <= 2:
            return candidates
        array, held_at = candidates[0][0], list(candidates[0][1])
        for other, places in candidates[1:]:
            here = functools.reduce(jnp.logical_or, [place == spot for spot in places])
            array = jnp.where(here, other, array)
            held_at += places
        return [(array, held_at)]

    own_centroids = lax.dynamic_slice_in_dim(centroids, core * half, half, 0)
    own_mix = lax.dynamic_slice_in_dim(log_mix, core * half, half, 0)
    units = to_unit(own_centroids)
    offsets = jnp.broadcast_to(((own_mix - concentration) * LOG2E)[:, None], (half, LANES))

    n_columns = n_places * CORES
    carried = None

    def scores_of(slot, carried):
        blocks = [order[slot] for order in orders]
        swapped = [(swap_cores(array, places), places) for array, places in slots[slot]]
        for who, candidates in enumerate((slots[slot], swapped)):
            choice = [
                next(n for n, (_, places) in enumerate(candidates) if spot in places)
                for spot in range(n_places)
            ]
            carried = score_block(
                ids,
                [array for array, _ in candidates],
                choice,
                blocks,
                who,
                units,
                offsets,
                carried,
                slot * CORES + who,
                n_columns,
            )
        return carried

    def totals_of(own):
        both = own + exchange(own, 1)
        return [both] + [
            lax.ppermute(both, "blk", [(i, (i + turn) % n_places) for i in range(n_places)])
            for turn in range(1, n_places)
        ]

    def arrive(moved):
        for slot, array, places in moved:
            slots[slot].append((array, places))

    def arrive_behind(moved, carried):
        if moved:
            arrays, carried = lax.optimization_barrier(([array for _, array, _ in moved], carried))
            arrive([(slot, array, places) for (slot, _, places), array in zip(moved, arrays)])
        return carried

    for turn in range(n_places):
        while sum(len(places) for _, places in slots[turn]) < n_places:
            moved, moves = start_ready(moves)
            arrive(moved)
        slots[turn] = merged(slots[turn])
        moved, moves = start_ready(moves)

        carried = scores_of(turn, carried)
        if turn == 0:
            arrive([m for m in moved if m[0] > turn + 1])
            moved = [m for m in moved if m[0] <= turn + 1]
        carried = arrive_behind(moved, carried)
    scores, rows, totals = carried
    steps = sum_plan(orders)
    *sent, mine, masses = sum_rows(
        ids, steps, totals_of(totals), scores, rows, n_owners, None, True
    )
    size = mine.shape[0]
    one, two = CORES, 2 * CORES
    if n_owners == 4:
        across, along, corner = sent[0:2], sent[2:4], sent[4:6]
        passing = exchange(corner[0], one), exchange(corner[1], two)
        arrived = [exchange(across[0], one), exchange(along[1], two)]
        arrived.append(exchange(pass_on(along[0], passing[0], False, size), two))
        arrived.append(exchange(pass_on(across[1], passing[1], True, size), one))
    else:
        arrived = [
            exchange(array, CORES * (1 + number // 2)) for number, array in enumerate(sent)
        ]
    payload = combine(mine, masses, arrived)

    count = local_centroids * n_places
    factor = count / (held * n_rows * n_places)
    if n_owners == 4:
        first = exchange(payload[0], one), exchange(payload[1], two)
        second = exchange(payload[1], one), exchange(payload[0], two)
        third = exchange(first[0], two), exchange(first[1], one)
        far = [(1, (first[0], second[0])), (2, (second[1], first[1])), (3, third)]
    else:
        far = [
            (away, tuple(exchange(array, CORES * away) for array in payload))
            for away in range(1, n_owners)
        ]
    swap = lambda halves: tuple(exchange(array, 1) for array in halves)
    done = assemble(ids, [(0, 0, payload), (1, 0, swap(payload))], None, n_rows, factor)
    if n_owners == 4:
        last_half, done = lax.optimization_barrier((second[1], done))
        far[1] = (2, (last_half, first[1]))
    swapped = [swap(halves) for _, halves in far[:-1]]
    arrays, swapped, done = lax.optimization_barrier(
        ([halves for _, halves in far], swapped, done)
    )
    swapped.append(swap(arrays[-1]))
    placed = [(0, away, halves) for (away, _), halves in zip(far, arrays)]
    placed += [(1, away, halves) for (away, _), halves in zip(far, swapped)]
    last = [piece for piece in placed if piece[1] == n_owners - 1]
    early = [piece for piece in placed if piece[1] != n_owners - 1]
    done = assemble(ids, early, done, n_rows, factor)
    done = assemble(ids, last, done, n_rows, factor)
    result, weights = done
    return (result, weights.reshape(local_centroids))


def solution(mesh):
    return jax.shard_map(
        local,
        mesh=mesh,
        in_specs=(P(("blk", "rows"), None), P("blk", None), P("blk")),
        out_specs=(P("blk", None), P("blk")),
        check_vma=False,
    )
```

```python
import functools
import math

import jax
import jax.numpy as jnp
from jax import lax
from jax.experimental import pallas as pl
from jax.experimental.pallas import tpu as pltpu
from jax.sharding import PartitionSpec as P

concentration = 32.0
LOG2E = math.log2(math.e)
LANES = 128
CORES = 2
EXTRA = 16
VMEM_LIMIT = 16 * 1024 * 1024


def to_unit(values):
    values = values.astype(jnp.float32)
    return (values * lax.rsqrt(jnp.sum(values * values, axis=-1, keepdims=True) + 1e-06)).astype(
        jnp.bfloat16
    )


def arrival_plan(n):
    orders = []
    for place in range(n):
        first = 1 if place < n // 2 else -1
        if 0 < place < n - 1:
            first = -first
        order = [place]
        for step in range(1, n):
            for way in (first, -first):
                if 0 <= place + way * step < n:
                    order.append(place + way * step)
        orders.append(order)
    moves = []
    for place in range(n):
        for slot in range(1, n):
            block = orders[place][slot]
            source = place + (1 if block > place else -1)
            moves.append((source, place, orders[source].index(block), slot))
    return orders, moves


def pick(index, values):
    result = jnp.int32(values[0])
    for number in range(1, len(values)):
        if values[number] != values[0]:
            result = jnp.where(index == number, jnp.int32(values[number]), result)
    return result


def score_kernel(n_sources, choice, ids, *refs):
    sources = refs[:n_sources]
    units_in, log_mix = refs[n_sources], refs[n_sources + 1]
    scores, rows_out, totals, raw, units, sem = refs[-6:]

    @pl.when(pl.program_id(0) == 0)
    def _():
        chosen = pick(ids[0], choice)
        for number, source in enumerate(sources):

            @pl.when(chosen == number)
            def _():
                pltpu.make_async_copy(source, raw, sem).start()

        pltpu.make_async_copy(sources[0], raw, sem).wait()
        values = raw[...].astype(jnp.float32)
        square = jnp.sum(values * values, axis=-1, keepdims=True)
        unit = (values * lax.rsqrt(square + 1e-06)).astype(jnp.bfloat16)
        units[...] = unit
        rows_out[...] = unit
        totals[...] = jnp.zeros_like(totals)

    cosines = lax.dot_general(
        units_in[...], units[...], (((1,), (1,)), ((), ())), preferred_element_type=jnp.float32
    )
    offset = log_mix[...]
    repeats = cosines.shape[1] // offset.shape[1]
    if repeats > 1:
        offset = jnp.concatenate([offset] * repeats, axis=1)
    value = jnp.exp2(cosines * (concentration * LOG2E) + offset)
    scores[0] = value
    totals[0] += jnp.sum(value, axis=0, keepdims=True)


def score_block(ids, sources, choice, blocks, who, units, offsets, carried, column, n_columns):
    part, depth = sources[0].shape
    count = units.shape[0]
    tile = math.gcd(count, 1024)
    shapes = (
        jax.ShapeDtypeStruct((n_columns, count, part), jnp.float32),
        jax.ShapeDtypeStruct((n_columns * part, depth), jnp.bfloat16),
        jax.ShapeDtypeStruct((n_columns, 1, part), jnp.float32),
    )
    n_sources = len(sources)
    aliases = {}
    extra = ()
    if carried is not None:
        extra = carried
        aliases = {1 + n_sources + 2 + i: i for i in range(3)}
    anywhere = pl.BlockSpec(memory_space=pl.ANY)
    return pl.pallas_call(
        functools.partial(score_kernel, n_sources, choice),
        grid_spec=pltpu.PrefetchScalarGridSpec(
            num_scalar_prefetch=1,
            grid=(count // tile,),
            in_specs=[anywhere] * n_sources
            + [
                pl.BlockSpec((tile, depth), lambda t, s: (t, 0)),
                pl.BlockSpec((tile, offsets.shape[1]), lambda t, s: (t, 0)),
            ]
            + [anywhere] * len(extra),
            out_specs=[
                pl.BlockSpec((1, tile, part), lambda t, s: (column, t, 0)),
                pl.BlockSpec((part, depth), lambda t, s: (column, 0)),
                pl.BlockSpec(
                    (1, 1, part),
                    lambda t, s: (pick(s[0], blocks) * CORES + ((s[1] % CORES) ^ who), 0, 0),
                ),
            ],
            scratch_shapes=[
                pltpu.VMEM((part, depth), jnp.bfloat16),
                pltpu.VMEM((part, depth), jnp.bfloat16),
                pltpu.SemaphoreType.DMA,
            ],
        ),
        out_shape=shapes,
        input_output_aliases=aliases,
        compiler_params=pltpu.CompilerParams(vmem_limit_bytes=VMEM_LIMIT),
        cost_estimate=pl.CostEstimate(
            flops=2 * count * part * depth,
            bytes_accessed=2 * (count * part * 4 + count * depth * 2),
            transcendentals=count * part,
        ),
        name="scores",
    )(ids, *sources, units, offsets, *extra)


def sum_plan(orders):
    n = len(orders)
    last = {order[-1] for order in orders}
    sorted_slots = []
    for order in orders:
        slots = list(range(n))
        sorted_slots.append(sorted(slots, key=lambda slot: (order[slot] in last, slot)))
    steps = []
    for turn in range(n):
        slots = [sorted_slots[place][turn] for place in range(n)]
        blocks = [orders[place][slot] for place, slot in enumerate(slots)]
        for who in range(CORES):
            steps.append(([slot * CORES + who for slot in slots], blocks, who))
    return steps


def three_rows(values, dtype, depth):
    size = values.shape[1]
    line = lax.broadcasted_iota(jnp.int32, (EXTRA, size), 0)
    high = values.astype(dtype).astype(jnp.float32)
    rest = values - high
    middle = rest.astype(dtype).astype(jnp.float32)
    low = rest - middle
    rows = jnp.where(
        line == 0, high, jnp.where(line == 1, middle, jnp.where(line == 2, low, 0.0))
    )
    if size < depth:
        rows = jnp.concatenate([rows, jnp.zeros((EXTRA, depth - size), jnp.float32)], axis=1)
    return rows.astype(dtype)


def one_row(rows, size):
    return jnp.sum(rows[:, :size].astype(jnp.float32), axis=0, keepdims=True)


def sum_kernel(plan, n_totals, n_owners, first, last, ids, *refs):
    totals = refs[:n_totals]
    scores, rows = refs[n_totals], refs[n_totals + 1]
    state = refs[n_totals + 2 : n_totals + 4]
    total, mass, inverse = refs[-3:]
    outs = refs[n_totals + (2 if first else 4) : -3]
    step = pl.program_id(0)

    @pl.when(step == 0)
    def _():
        for number, (_, blocks, who) in enumerate(plan):
            place = pick(ids[0], blocks) * CORES + ((ids[1] % CORES) ^ who)
            value = totals[0][place]
            for more in totals[1:]:
                value = value + more[place]
            inverse[number] = 1.0 / value
        if first:
            total[...] = jnp.zeros_like(total)
            mass[...] = jnp.zeros_like(mass)
        else:
            total[...] = state[0][...]
            mass[...] = state[1][...]

    resp = (scores[0] * inverse[step]).astype(jnp.bfloat16)
    total[...] += lax.dot_general(
        resp, rows[...], (((1,), (0,)), ((), ())), preferred_element_type=jnp.float32
    )
    wide = resp.astype(jnp.float32)
    partial = wide[:, :LANES]
    for start in range(LANES, wide.shape[1], LANES):
        partial = partial + wide[:, start : start + LANES]
    mass[...] += partial

    @pl.when(step == pl.num_programs(0) - 1)
    def _():
        if not last:
            outs[0][...] = total[...]
            outs[1][...] = mass[...]
            return
        sent = outs[:-2]
        mine, masses = outs[-2:]
        size, depth = mine.shape
        upper = size // 2
        quarter = ids[1] // CORES
        sums = jnp.sum(mass[...].T, axis=0, keepdims=True)
        for number in range(n_owners):
            block = total[number * size : (number + 1) * size, :]
            own = sums[:, number * size : (number + 1) * size]

            @pl.when(quarter == number)
            def _():
                mine[...] = block
                masses[...] = own

            for away in range(1, n_owners):

                @pl.when(quarter ^ number == away)
                def _():
                    first_half, second_half = sent[2 * away - 2 : 2 * away]
                    first_half[...] = block[:upper].astype(first_half.dtype)
                    second_half[: size - upper, :] = block[upper:].astype(second_half.dtype)
                    second_half[size - upper :, :] = three_rows(own, second_half.dtype, depth)


def sum_rows(ids, plan, totals, scores, rows, n_owners, carried, last):
    count = scores.shape[1]
    depth = rows.shape[1]
    size = count // n_owners
    part = totals[0].shape[2]
    first = carried is None
    column = lambda t, s: sum(
        jnp.where(t == n, pick(s[0], columns), 0) for n, (columns, _, _) in enumerate(plan)
    )
    fixed = lambda shape: pl.BlockSpec(shape, lambda t, s: (0,) * len(shape))
    in_specs = [fixed(totals[0].shape) for _ in totals] + [
        pl.BlockSpec((1, count, part), lambda t, s: (column(t, s), 0, 0)),
        pl.BlockSpec((part, depth), lambda t, s: (column(t, s), 0)),
    ]
    state = [(count, depth), (count, LANES)]
    if not first:
        in_specs += [fixed(shape) for shape in state]
    if last:
        shapes = []
        for away in range(1, n_owners):
            kept = [n_owners == 4 and keep == away for keep in (2, 1)]
            for keep, height in zip(kept, (size // 2, size - size // 2 + EXTRA)):
                shapes.append(((height, depth), jnp.float32 if keep else jnp.bfloat16))
        shapes += [((size, depth), jnp.float32), ((1, size), jnp.float32)]
    else:
        shapes = [(shape, jnp.float32) for shape in state]
    return pl.pallas_call(
        functools.partial(sum_kernel, plan, len(totals), n_owners, first, last),
        grid_spec=pltpu.PrefetchScalarGridSpec(
            num_scalar_prefetch=1,
            grid=(len(plan),),
            in_specs=in_specs,
            out_specs=[fixed(shape) for shape, _ in shapes],
            scratch_shapes=[
                pltpu.VMEM((count, depth), jnp.float32),
                pltpu.VMEM((count, LANES), jnp.float32),
                pltpu.VMEM((len(plan), 1, part), jnp.float32),
            ],
        ),
        out_shape=[jax.ShapeDtypeStruct(shape, dtype) for shape, dtype in shapes],
        compiler_params=pltpu.CompilerParams(vmem_limit_bytes=VMEM_LIMIT),
        cost_estimate=pl.CostEstimate(
            flops=2 * count * len(plan) * part * depth,
            bytes_accessed=len(plan) * part * (count * 4 + depth * 2) + count * depth * 4,
            transcendentals=0,
        ),
        name="sums",
    )(ids, *totals, scores, rows, *(carried or ()))


def pass_on_kernel(has_masses, size, mine, arrived, out):
    depth = mine.shape[1]
    height = mine.shape[0] - (EXTRA if has_masses else 0)
    total = mine[:height, :] + arrived[:height, :].astype(jnp.float32)
    out[:height, :] = total.astype(out.dtype)
    if has_masses:
        mass = one_row(mine[height:, :], size) + one_row(arrived[height:, :], size)
        out[height:, :] = three_rows(mass, out.dtype, depth)


def pass_on(mine, arrived, has_masses, size):
    return pl.pallas_call(
        functools.partial(pass_on_kernel, has_masses, size),
        out_shape=jax.ShapeDtypeStruct(arrived.shape, arrived.dtype),
        compiler_params=pltpu.CompilerParams(vmem_limit_bytes=VMEM_LIMIT),
        name="pass_on",
    )(mine, arrived)


def combine_kernel(mine, masses, *refs):
    first_out, second_out = refs[-2:]
    size, depth = mine.shape
    upper = size // 2
    first = mine[:upper, :]
    second = mine[upper:, :]
    mass = masses[...]
    for ref in refs[:-2]:
        if ref.shape[0] == upper:
            first = first + ref[...].astype(jnp.float32)
        else:
            second = second + ref[: size - upper, :].astype(jnp.float32)
            mass = mass + one_row(ref[size - upper :, :], size)
    for total, out in ((first, first_out), (second, second_out)):
        square = jnp.sum(total * total, axis=1, keepdims=True)
        out[: total.shape[0], :] = (total * lax.rsqrt(square + 1e-06)).astype(out.dtype)
    second_out[size - upper :, :] = three_rows(mass, second_out.dtype, depth)


def combine(mine, masses, arrived):
    size, depth = mine.shape
    upper = size // 2
    return pl.pallas_call(
        combine_kernel,
        out_shape=[
            jax.ShapeDtypeStruct((upper, depth), jnp.bfloat16),
            jax.ShapeDtypeStruct((size - upper + EXTRA, depth), jnp.bfloat16),
        ],
        compiler_params=pltpu.CompilerParams(vmem_limit_bytes=VMEM_LIMIT),
        name="combine",
    )(mine, masses, *arrived)


def assemble_kernel(factor, spots, half, ids, *refs):
    units, weights, wide, light, sems = refs[-5:]
    size = wide.shape[1]
    upper = size // 2
    copies = []
    for number, (flip, away) in enumerate(spots):
        first, second = refs[2 * number : 2 * number + 2]
        wide[number, :upper, :] = first[...].astype(jnp.float32)
        wide[number, upper:, :] = second[: size - upper, :].astype(jnp.float32)
        light[number] = one_row(second[size - upper :, :], size) * factor
        block = ((ids[1] % CORES) ^ flip) * half + ((ids[1] // CORES) ^ away)
        place = pl.ds(pl.multiple_of(block * size, size), size)
        copies.append(
            pltpu.make_async_copy(wide.at[number], units.at[place], sems.at[2 * number])
        )
        copies.append(
            pltpu.make_async_copy(light.at[number], weights.at[block], sems.at[2 * number + 1])
        )
        copies[-2].start()
        copies[-1].start()
    for copy in copies:
        copy.wait()


def assemble(ids, pieces, carried, n_blocks, factor):
    arrays = [array for _, _, halves in pieces for array in halves]
    depth = arrays[0].shape[1]
    size = arrays[0].shape[0] + arrays[1].shape[0] - EXTRA
    spots = [(flip, away) for flip, away, _ in pieces]
    extra = carried or ()
    anywhere = pl.BlockSpec(memory_space=pl.ANY)
    return pl.pallas_call(
        functools.partial(assemble_kernel, factor, spots, n_blocks // CORES),
        in_specs=[pl.BlockSpec(memory_space=pltpu.SMEM)]
        + [pl.BlockSpec(memory_space=pltpu.VMEM)] * len(arrays)
        + [anywhere] * len(extra),
        out_specs=[anywhere, anywhere],
        out_shape=[
            jax.ShapeDtypeStruct((n_blocks * size, depth), jnp.float32),
            jax.ShapeDtypeStruct((n_blocks, 1, size), jnp.float32),
        ],
        scratch_shapes=[
            pltpu.VMEM((len(pieces), size, depth), jnp.float32),
            pltpu.VMEM((len(pieces), 1, size), jnp.float32),
            pltpu.SemaphoreType.DMA((2 * len(pieces),)),
        ],
        input_output_aliases={1 + len(arrays) + n: n for n in range(len(extra))},
        compiler_params=pltpu.CompilerParams(vmem_limit_bytes=VMEM_LIMIT),
        name="assemble",
    )(ids, *arrays, *extra)


def local(embeddings, centroids, log_mix):
    n_places = lax.axis_size("blk")
    n_rows = lax.axis_size("rows")
    n_owners = n_rows // CORES
    place = lax.axis_index("blk")
    me = lax.axis_index("rows")
    core = lax.rem(me, CORES)
    held, depth = embeddings.shape
    local_centroids = centroids.shape[0]
    half = local_centroids // CORES
    ids = jnp.stack([place, me]).astype(jnp.int32)
    orders, moves = arrival_plan(n_places)

    def exchange(array, distance):
        return lax.ppermute(array, "rows", [(i, i ^ distance) for i in range(n_rows)])

    def swap_cores(array, places):
        pairs = [
            (spot * n_rows + i, spot * n_rows + (i ^ 1)) for spot in places for i in range(n_rows)
        ]
        return lax.ppermute(array, ("blk", "rows"), pairs)

    slots = [[(embeddings, list(range(n_places)))]] + [[] for _ in range(n_places - 1)]

    def start_ready(moves):
        groups = {}
        left = []
        for move in moves:
            source, target, source_slot, slot = move
            holds = [n for n, (_, places) in enumerate(slots[source_slot]) if source in places]
            if not holds:
                left.append(move)
                continue
            turn = 0
            while any(source == s for s, _ in groups.get((slot, source_slot, holds[0], turn), [])):
                turn += 1
            groups.setdefault((slot, source_slot, holds[0], turn), []).append((source, target))
        moved = [
            (slot, lax.ppermute(slots[source_slot][hold][0], "blk", pairs), [p[1] for p in pairs])
            for (slot, source_slot, hold, _), pairs in sorted(groups.items())
        ]
        return moved, left

    def merged(candidates):
        if len(candidates) <= 2:
            return candidates
        array, held_at = candidates[0][0], list(candidates[0][1])
        for other, places in candidates[1:]:
            here = functools.reduce(jnp.logical_or, [place == spot for spot in places])
            array = jnp.where(here, other, array)
            held_at += places
        return [(array, held_at)]

    own_centroids = lax.dynamic_slice_in_dim(centroids, core * half, half, 0)
    own_mix = lax.dynamic_slice_in_dim(log_mix, core * half, half, 0)
    units = to_unit(own_centroids)
    offsets = jnp.broadcast_to(((own_mix - concentration) * LOG2E)[:, None], (half, LANES))

    n_columns = n_places * CORES
    carried = None

    def scores_of(slot, carried):
        blocks = [order[slot] for order in orders]
        swapped = [(swap_cores(array, places), places) for array, places in slots[slot]]
        for who, candidates in enumerate((slots[slot], swapped)):
            choice = [
                next(n for n, (_, places) in enumerate(candidates) if spot in places)
                for spot in range(n_places)
            ]
            carried = score_block(
                ids,
                [array for array, _ in candidates],
                choice,
                blocks,
                who,
                units,
                offsets,
                carried,
                slot * CORES + who,
                n_columns,
            )
        return carried

    def totals_of(own):
        both = own + exchange(own, 1)
        return [both] + [
            lax.ppermute(both, "blk", [(i, (i + turn) % n_places) for i in range(n_places)])
            for turn in range(1, n_places)
        ]

    def arrive(moved):
        for slot, array, places in moved:
            slots[slot].append((array, places))

    def arrive_behind(moved, carried):
        if moved:
            arrays, carried = lax.optimization_barrier(([array for _, array, _ in moved], carried))
            arrive([(slot, array, places) for (slot, _, places), array in zip(moved, arrays)])
        return carried

    for turn in range(n_places):
        while sum(len(places) for _, places in slots[turn]) < n_places:
            moved, moves = start_ready(moves)
            arrive(moved)
        slots[turn] = merged(slots[turn])
        moved, moves = start_ready(moves)

        carried = scores_of(turn, carried)
        if turn == 0:
            arrive([m for m in moved if m[0] > turn + 1])
            moved = [m for m in moved if m[0] <= turn + 1]
        carried = arrive_behind(moved, carried)
    scores, rows, totals = carried
    steps = sum_plan(orders)
    *sent, mine, masses = sum_rows(
        ids, steps, totals_of(totals), scores, rows, n_owners, None, True
    )
    size = mine.shape[0]
    one, two = CORES, 2 * CORES
    if n_owners == 4:
        across, along, corner = sent[0:2], sent[2:4], sent[4:6]
        passing = exchange(corner[0], one), exchange(corner[1], two)
        arrived = [exchange(across[0], one), exchange(along[1], two)]
        arrived.append(exchange(pass_on(along[0], passing[0], False, size), two))
        arrived.append(exchange(pass_on(across[1], passing[1], True, size), one))
    else:
        arrived = [
            exchange(array, CORES * (1 + number // 2)) for number, array in enumerate(sent)
        ]
    payload = combine(mine, masses, arrived)

    count = local_centroids * n_places
    factor = count / (held * n_rows * n_places)
    if n_owners == 4:
        first = exchange(payload[0], one), exchange(payload[1], two)
        second = exchange(payload[1], one), exchange(payload[0], two)
        third = exchange(first[0], two), exchange(first[1], one)
        far = [(1, (first[0], second[0])), (2, (second[1], first[1])), (3, third)]
    else:
        far = [
            (away, tuple(exchange(array, CORES * away) for array in payload))
            for away in range(1, n_owners)
        ]
    swap = lambda halves: tuple(exchange(array, 1) for array in halves)
    done = assemble(ids, [(0, 0, payload), (1, 0, swap(payload))], None, n_rows, factor)
    if n_owners == 4:
        last_half, done = lax.optimization_barrier((second[1], done))
        far[1] = (2, (last_half, first[1]))
    swapped = [swap(halves) for _, halves in far[:-1]]
    *near, (corner_away, corner_halves) = far
    placed = [(0, away, halves) for away, halves in near]
    placed += [(1, away, halves) for (away, _), halves in zip(near, swapped)]
    done = assemble(ids, placed, done, n_rows, factor)
    corner_halves, done = lax.optimization_barrier((corner_halves, done))
    last = [(0, corner_away, corner_halves), (1, corner_away, swap(corner_halves))]
    done = assemble(ids, last, done, n_rows, factor)
    result, weights = done
    return (result, weights.reshape(local_centroids))


def solution(mesh):
    return jax.shard_map(
        local,
        mesh=mesh,
        in_specs=(P(("blk", "rows"), None), P("blk", None), P("blk")),
        out_specs=(P("blk", None), P("blk")),
        check_vma=False,
    )
```
